128 devices in a mesh: stream: 2 (over x_lo), dp: 64 (over y, x_hi, z, core).
Axes of the slice: x: 4 (x_hi: 2, x_lo: 2; x = x_hi * 2 + x_lo), y: 4, z: 4, core: 2. Of those that a mesh axis runs over, the one named last changes fastest.
Arguments:
- inputs: bfloat16 [2, 64, 512, 768], P('stream', 'dp'), may hold values from -6 to 6
- cotangent: bfloat16 [2, 64, 512, 768], P('stream', 'dp'), may hold values from -6 to 6
- lengths: int32 [64], P('dp'), may hold values from 128 to 512, as said below
- block_sizes: int32 [64], P('dp'), may hold values from 4 to 16, as said below
- w_qkv: float32 [768, 2304], P(None, ('stream', 'dp')), may hold values from -0.21875 to 0.21875
- w_out: float32 [768, 768], P(('stream', 'dp')), may hold values from -1.75 to 1.75
- w_up: float32 [768, 3072], P(None, ('stream', 'dp')), may hold values from -0.21875 to 0.21875
- w_down: float32 [3072, 768], P(('stream', 'dp')), may hold values from -0.109375 to 0.109375
- gains: float32 [2, 768], P(None, ('stream', 'dp')), may hold values from 0.5 to 1.5
- first_qkv: float32 [768, 2304], P(None, ('stream', 'dp')), may hold values from -1024 to 1024
- first_out: float32 [768, 768], P(('stream', 'dp')), may hold values from -160 to 160
- first_up: float32 [768, 3072], P(None, ('stream', 'dp')), may hold values from -448 to 448
- first_down: float32 [3072, 768], P(('stream', 'dp')), may hold values from -896 to 896
- first_gains: float32 [2, 768], P(None, ('stream', 'dp')), may hold values from -1536 to 1536
- second_qkv: float32 [768, 2304], P(None, ('stream', 'dp')), may hold values from 32112.64 to 128450.56
- second_out: float32 [768, 768], P(('stream', 'dp')), may hold values from 655.36 to 2621.44
- second_up: float32 [768, 3072], P(None, ('stream', 'dp')), may hold values from 5898.24 to 23592.96
- second_down: float32 [3072, 768], P(('stream', 'dp')), may hold values from 23592.96 to 94371.84
- second_gains: float32 [2, 768], P(None, ('stream', 'dp')), may hold values from 65536 to 262144
Outputs:
- outputs: bfloat16 [2, 64, 512, 768], P('stream', 'dp')
- input_grads: bfloat16 [2, 64, 512, 768], P('stream', 'dp')
- new_qkv: float32 [768, 2304], P(None, ('stream', 'dp'))
- new_out: float32 [768, 768], P(('stream', 'dp'))
- new_up: float32 [768, 3072], P(None, ('stream', 'dp'))
- new_down: float32 [3072, 768], P(('stream', 'dp'))
- new_gains: float32 [2, 768], P(None, ('stream', 'dp'))
- new_first_qkv: float32 [768, 2304], P(None, ('stream', 'dp'))
- new_first_out: float32 [768, 768], P(('stream', 'dp'))
- new_first_up: float32 [768, 3072], P(None, ('stream', 'dp'))
- new_first_down: float32 [3072, 768], P(('stream', 'dp'))
- new_first_gains: float32 [2, 768], P(None, ('stream', 'dp'))
- new_second_qkv: float32 [768, 2304], P(None, ('stream', 'dp'))
- new_second_out: float32 [768, 768], P(('stream', 'dp'))
- new_second_up: float32 [768, 3072], P(None, ('stream', 'dp'))
- new_second_down: float32 [3072, 768], P(('stream', 'dp'))
- new_second_gains: float32 [2, 768], P(None, ('stream', 'dp'))
- low_qkv: bfloat16 [768, 2304], P(None, ('stream', 'dp'))
- low_out: bfloat16 [768, 768], P(('stream', 'dp'))
- low_up: bfloat16 [768, 3072], P(None, ('stream', 'dp'))
- low_down: bfloat16 [3072, 768], P(('stream', 'dp'))
The draws below stay inside these ranges and needn't reach their ends.
Inputs may be any that keep to these rules, and one draw needn't show every extreme that they name: `lengths`: keys of an example at positions of 512 or beyond its length are padding. `block_sizes`: each entry is 4, 8 or 16.
All inputs are finite; a program needn't handle non-finite values.
Results may differ from the reference program's by a relative error of at most 0.017.
Values may be sent and summed in bfloat16 or wider, within the bound.
A program may use at most 192 MiB of HBM per device.

```python
import math
import jax
import jax.numpy as jnp
from jax import lax

D = 768
H = 12
HD = 64
FF = 3072
SEQ = 512
STEP = 7
EXAMPLES = 64
N_DP = 64


def draw_lengths(key, part):
    key = jax.random.fold_in(key, 11)
    key_one, key_two = jax.random.split(key)
    drawn = jax.random.randint(key_one, (EXAMPLES,), SEQ // 4, SEQ + 1)
    placed = jax.random.randint(key_two, (), 0, EXAMPLES)
    position = jnp.arange(EXAMPLES)
    drawn = jnp.where(position == (placed + 1) % EXAMPLES, SEQ // 4, drawn)
    return jnp.where(position == placed, SEQ, drawn).astype(jnp.int32)


def draw_block_sizes(key, part):
    key = jax.random.fold_in(key, 23)
    key_one, key_two = jax.random.split(key)
    chosen = jax.random.randint(key_one, (EXAMPLES,), 0, 3)
    placed = jax.random.randint(key_two, (), 0, EXAMPLES)
    position = jnp.arange(EXAMPLES)
    chosen = jnp.where(position == placed, 0, jnp.where(position == (placed + 1) % EXAMPLES, 2, chosen))
    return jnp.where(chosen == 0, 4, jnp.where(chosen == 1, 8, 16)).astype(jnp.int32)


def level_of(own_key, extent, pieces, least, high):
    level, own = 1.0, jax.random.fold_in(own_key, 6)
    for dim, shards_of in pieces:
        draws = jnp.exp(jax.random.uniform(jax.random.fold_in(own, dim), (shards_of,), jnp.float32, least / len(pieces), high / len(pieces)))
        level = level * jnp.repeat(draws, extent[dim] // shards_of).reshape([-1 if axis == dim else 1 for axis in range(len(extent))])
    return level


def normal_values(key, shape, scale, limit, cuts=(), kind=jnp.bfloat16):
    level = level_of(key, shape, cuts, -0.22, 0.18) if cuts else 1.0
    values = jax.random.normal(key, shape, jnp.float32) * scale * level
    return jnp.minimum(jnp.maximum(values, -limit), limit).astype(kind)


def setup_inputs(seed: int = 0) -> dict:
    keys = jax.random.split(jax.random.key(seed), 20)
    return {
        "inputs": normal_values(keys[0], (2, EXAMPLES, SEQ, D), 1.0, 6.0, ((0, 2), (1, 64))),
        "cotangent": normal_values(keys[1], (2, EXAMPLES, SEQ, D), 1.0, 6.0, ((0, 2), (1, 64))),
        "lengths": draw_lengths(jax.random.fold_in(keys[19], 71), 0),
        "block_sizes": draw_block_sizes(jax.random.fold_in(keys[19], 71), 0),
        "w_qkv": normal_values(keys[4], (D, 3 * D), D ** -0.5, 0.21875, ((1, 128),), jnp.float32),
        "w_out": normal_values(keys[5], (D, D), H ** -0.5, 1.75, ((0, 128),), jnp.float32),
        "w_up": normal_values(keys[6], (D, FF), D ** -0.5, 0.21875, ((1, 128),), jnp.float32),
        "w_down": normal_values(keys[7], (FF, D), FF ** -0.5, 0.109375, ((0, 128),), jnp.float32),
        "gains": jnp.clip(1.0 + 0.1 * jax.random.normal(keys[8], (2, D), jnp.float32), 0.5, 1.5),
        "first_qkv": normal_values(keys[9], (D, 3 * D), (0.7 * (2 * N_DP * SEQ) ** 0.5), 1024.0, ((1, 128),), jnp.float32),
        "first_out": normal_values(keys[10], (D, D), (0.1 * (2 * N_DP * SEQ) ** 0.5), 160.0, ((0, 128),), jnp.float32),
        "first_up": normal_values(keys[11], (D, FF), (0.3 * (2 * N_DP * SEQ) ** 0.5), 448.0, ((1, 128),), jnp.float32),
        "first_down": normal_values(keys[12], (FF, D), (0.6 * (2 * N_DP * SEQ) ** 0.5), 896.0, ((0, 128),), jnp.float32),
        "first_gains": normal_values(keys[13], (2, D), (1.0 * (2 * N_DP * SEQ) ** 0.5), 1536.0, ((1, 128),), jnp.float32),
        "second_qkv": jnp.clip(jnp.exp(math.log(128450.56) - 1.3862944 * jax.random.uniform(keys[14], (D, 3 * D), jnp.float32) ** level_of(keys[14], (D, 3 * D), ((1, 128),), -0.2, 0.2)), 32112.64, 128450.56),
        "second_out": jnp.clip(jnp.exp(math.log(2621.44) - 1.3862944 * jax.random.uniform(keys[15], (D, D), jnp.float32) ** level_of(keys[15], (D, D), ((0, 128),), -0.2, 0.2)), 655.36, 2621.44),
        "second_up": jnp.clip(jnp.exp(math.log(23592.96) - 1.3862944 * jax.random.uniform(keys[16], (D, FF), jnp.float32) ** level_of(keys[16], (D, FF), ((1, 128),), -0.2, 0.2)), 5898.24, 23592.96),
        "second_down": jnp.clip(jnp.exp(math.log(94371.84) - 1.3862944 * jax.random.uniform(keys[17], (FF, D), jnp.float32) ** level_of(keys[17], (FF, D), ((0, 128),), -0.2, 0.2)), 23592.96, 94371.84),
        "second_gains": jnp.clip(jnp.exp(math.log(262144.0) - 1.3862944 * jax.random.uniform(keys[18], (2, D), jnp.float32) ** level_of(keys[18], (2, D), ((1, 128),), -0.2, 0.2)), 65536.0, 262144.0),
    }


PRECISE = lax.Precision.HIGHEST
NORM_EPS = 1e-05
BETA_ONE = 0.5
BETA_TWO = 0.5
ADAM_EPS = 1e-08
WEIGHT_DECAY = 0.01
GAIN_RATE = 0.2

@jax.custom_vjp
def low(v):
    return lax.optimization_barrier(v.astype(jnp.bfloat16)).astype(jnp.float32)

@jax.custom_vjp
def low_back(v):
    return v

def low_keep(v):
    return (low(v), None)

def low_pass(kept, grad):
    return (grad,)

def back_keep(v):
    return (v, None)

def back_low(kept, grad):
    return (low(grad),)
low.defvjp(low_keep, low_pass)
low_back.defvjp(back_keep, back_low)

def normed(values, gain):
    center = values - lax.optimization_barrier(jnp.mean(values, axis=-1, keepdims=True))
    spread = lax.optimization_barrier(jnp.mean(center * center, axis=-1, keepdims=True))
    return center * lax.rsqrt(spread + NORM_EPS) * gain

def rotary_tables(positions_count, head_width):
    half_width = head_width // 2
    frequency = 10000.0 ** (-2.0 * jnp.arange(half_width, dtype=jnp.float32) / head_width)
    angles = jnp.arange(positions_count, dtype=jnp.float32)[:, None] * frequency[None, :]
    return (jnp.cos(angles), jnp.sin(angles))

def rotate(values, cosine_table, sine_table):
    half_width = values.shape[-1] // 2
    leading = values[..., :half_width]
    trailing = values[..., half_width:]
    cosine = cosine_table[:, None, :]
    sine_part = sine_table[:, None, :]
    return jnp.concatenate([leading * cosine - trailing * sine_part, leading * sine_part + trailing * cosine], axis=-1)

def block_masks(length, block_size):
    position = jnp.arange(SEQ, dtype=jnp.int32)
    block_index = position // block_size
    valid_keys = (position < length)[None, :]
    earlier = block_index[:, None] > block_index[None, :]
    same_block = block_index[:, None] == block_index[None, :]
    clean_mask = (earlier | same_block) & valid_keys
    noisy_mask = jnp.concatenate([earlier & valid_keys, same_block & valid_keys], axis=1)
    return (clean_mask, noisy_mask)

def attend(q_rows, keys_all, values_all, allowed, head_scale):
    scores = low_back(jnp.einsum('qhd,khd->hqk', q_rows, keys_all, precision=PRECISE) * head_scale)
    probs = low(jax.nn.softmax(jnp.where(allowed[None], scores, -1e+30), axis=-1))
    return jnp.einsum('hqk,khd->qhd', probs, values_all, precision=PRECISE)

def layer_one(params, inputs_pair, length, block_size):
    w_qkv, w_out, w_up, w_down, gains = params
    head_scale = HD ** (-0.5)
    cosine_table, sine_table = rotary_tables(SEQ, HD)
    clean_mask, noisy_mask = block_masks(length, block_size)
    h_one = low(normed(inputs_pair, gains[0]))
    projected = low_back(jnp.einsum('tsd,de->tse', h_one, w_qkv, precision=PRECISE))
    queries = projected[..., :D].reshape(2, SEQ, H, HD)
    keys_own = projected[..., D:2 * D].reshape(2, SEQ, H, HD)
    values_own = projected[..., 2 * D:].reshape(2, SEQ, H, HD)
    q_low = low(rotate(queries, cosine_table, sine_table))
    k_low = low(rotate(keys_own, cosine_table, sine_table))
    v_low = low(values_own)
    clean_att = attend(q_low[0], k_low[0], v_low[0], clean_mask, head_scale)
    keys_all = jnp.concatenate([k_low[0], k_low[1]], axis=0)
    values_all = jnp.concatenate([v_low[0], v_low[1]], axis=0)
    noisy_att = attend(q_low[1], keys_all, values_all, noisy_mask, head_scale)
    attended = low(low_back(jnp.stack([clean_att, noisy_att]).reshape(2, SEQ, D)))
    mixed_rows = inputs_pair + low_back(jnp.einsum('tsa,ad->tsd', attended, w_out, precision=PRECISE))
    h_two = low(normed(mixed_rows, gains[1]))
    up_proj = low_back(jnp.einsum('tsd,df->tsf', h_two, w_up, precision=PRECISE))
    activated = low(jax.nn.gelu(up_proj))
    return mixed_rows + jnp.einsum('tsf,fd->tsd', activated, w_down, precision=PRECISE)

def adam_update(weight, grad, first, second, rate):
    first_new = BETA_ONE * first + (1.0 - BETA_ONE) * grad
    second_new = BETA_TWO * second + (1.0 - BETA_TWO) * grad * grad
    fix_one = 1.0 - BETA_ONE ** STEP
    fix_two = 1.0 - BETA_TWO ** STEP
    update = first_new / fix_one / (jnp.sqrt(second_new / fix_two) + ADAM_EPS)
    return (weight - rate * (update + WEIGHT_DECAY * weight), first_new, second_new)

def reference(inputs, cotangent, lengths, block_sizes, w_qkv, w_out, w_up, w_down, gains, first_qkv, first_out, first_up, first_down, first_gains, second_qkv, second_out, second_up, second_down, second_gains):
    masters = (w_qkv, w_out, w_up, w_down, gains)

    def forward(params, inputs_all):
        rounded = tuple((low(weight) for weight in params))

        def one_example(bundle):
            return layer_one(rounded, bundle[0], bundle[1], bundle[2])
        return lax.map(jax.checkpoint(one_example), (inputs_all, lengths, block_sizes))
    inputs_all = jnp.swapaxes(inputs.astype(jnp.float32), 0, 1)
    result, pullback = jax.vjp(forward, masters, inputs_all)
    grads, grads_input = pullback(jnp.swapaxes(cotangent.astype(jnp.float32), 0, 1))
    outputs = jnp.swapaxes(result, 0, 1).astype(jnp.bfloat16)
    input_grads = jnp.swapaxes(grads_input, 0, 1).astype(jnp.bfloat16)
    rates = (D ** (-0.5), H ** (-0.5), D ** (-0.5), FF ** (-0.5), GAIN_RATE)
    firsts = (first_qkv, first_out, first_up, first_down, first_gains)
    seconds = (second_qkv, second_out, second_up, second_down, second_gains)
    updated = [adam_update(masters[slot], grads[slot], firsts[slot], seconds[slot], rates[slot]) for slot in range(5)]
    new_weights = tuple((entry[0] for entry in updated))
    new_firsts = tuple((entry[1] for entry in updated))
    new_seconds = tuple((entry[2] for entry in updated))
    return (outputs, input_grads, new_weights[0], new_weights[1], new_weights[2], new_weights[3], new_weights[4], new_firsts[0], new_firsts[1], new_firsts[2], new_firsts[3], new_firsts[4], new_seconds[0], new_seconds[1], new_seconds[2], new_seconds[3], new_seconds[4], new_weights[0].astype(jnp.bfloat16), new_weights[1].astype(jnp.bfloat16), new_weights[2].astype(jnp.bfloat16), new_weights[3].astype(jnp.bfloat16))
```

```python
import functools

import jax
import jax.numpy as jnp
import numpy as np
from jax import lax
from jax.experimental import pallas as pl
from jax.experimental.pallas import tpu as pltpu
from jax.sharding import Mesh
from jax.sharding import PartitionSpec as P

D = 768
H = 12
HD = 64
FF = 3072
SEQ = 512
STEP = 7
TILE = 128
TILES = SEQ // TILE
PAIRS = H // 2
LANES = D // 128
NORM_EPS = 1e-05
BETA_ONE = 0.5
BETA_TWO = 0.5
ADAM_EPS = 1e-08
WEIGHT_DECAY = 0.01
GAIN_RATE = 0.2
RATES = (D ** (-0.5), H ** (-0.5), D ** (-0.5), FF ** (-0.5), GAIN_RATE)
AXES = ("xl", "y", "xh", "z", "core")
ORDER = ((0, 1, 2), (1, 2, 0), (2, 0, 1))
SHARDS = (6, 4, 4, 4, 48, 128)
MASKED = -1e30

f32 = jnp.float32
bf16 = jnp.bfloat16
VMEM = pltpu.VMEM
DMA = pltpu.SemaphoreType.DMA
MESH = pl.DeviceIdType.MESH


def remote(src, dst, send, recv, device):
    return pltpu.make_async_remote_copy(
        src_ref=src,
        dst_ref=dst,
        send_sem=send,
        recv_sem=recv,
        device_id=device,
        device_id_type=MESH,
    )


def dot_nn(a, b):
    return jnp.dot(a, b, preferred_element_type=f32)


def dot_nt(a, b):
    return lax.dot_general(a, b, (((1,), (1,)), ((), ())), preferred_element_type=f32)


def dot_tn(a, b):
    return lax.dot_general(a, b, (((0,), (0,)), ((), ())), preferred_element_type=f32)


def aligned(start, size, step):
    return pl.ds(pl.multiple_of(start, step), size)


class Place:
    def __init__(self):
        self.stream = lax.axis_index("xl")
        self.core = lax.axis_index("core")
        self.chip = (
            lax.axis_index("xh") * 2 + self.stream,
            lax.axis_index("y"),
            lax.axis_index("z"),
        )

    def device(self, chip, core):
        return (lax.rem(chip[0], 2), chip[1], lax.div(chip[0], 2), chip[2], core)

    def along(self, dim, offset):
        chip = list(self.chip)
        chip[dim] = lax.rem(chip[dim] + offset, 4)
        return self.device(chip, self.core)

    def sibling(self):
        return self.device(self.chip, 1 - self.core)

    def partner(self):
        chip = (self.chip[0] + 1 - 2 * self.stream, self.chip[1], self.chip[2])
        return self.device(chip, self.core)

    def region(self, whole, fixed=None):
        out = []
        for dim in range(3):
            if fixed and dim in fixed:
                out.append(fixed[dim])
            elif dim in whole:
                out.append(slice(None))
            else:
                out.append(self.chip[dim])
        return tuple(out)

    def greet(self):
        barrier = pltpu.get_barrier_semaphore()
        others = [self.sibling()]
        others += [self.along(dim, offset) for dim in range(3) for offset in (1, 2, 3)]
        for other in others:
            pl.semaphore_signal(barrier, inc=1, device_id=other, device_id_type=MESH)
        pl.semaphore_wait(barrier, len(others))


class Gather:
    scratch = [
        VMEM((72, 384), f32),
        VMEM((3, 48, 384), f32),
        DMA((3, 3, 3, 3)),
        DMA((3, 3, 3, 3)),
        DMA((3, 3)),
        DMA((3, 3)),
        DMA((2,)),
    ]

    def __init__(self, me, packed, shards, scratch):
        self.me, self.packed, self.shards = me, packed, shards
        self.half, self.block, self.send_sem, self.recv_sem = scratch[:4]
        self.side_send, self.side_recv, self.swap_sem = scratch[4:]

    def swap(self):
        me = self.me
        return remote(
            self.packed.at[:, aligned(384 * (1 - me.core), 384, 128)],
            self.half,
            self.swap_sem.at[0],
            self.swap_sem.at[1],
            me.sibling(),
        )

    def assemble(self):
        core = self.me.core
        own = self.packed[:, aligned(384 * core, 384, 128)]
        for s in range(3):
            self.block[s, aligned(24 * core, 24, 8)] = own[24 * s : 24 * s + 24]
            self.block[s, aligned(24 * (1 - core), 24, 8)] = self.half[24 * s : 24 * s + 24]
        for s in range(3):
            value = self.block[s].astype(bf16)
            for p in range(3):
                self.shards[s][(3 * core + p,) + self.me.chip] = value[:, 128 * p : 128 * p + 128]

    def copies(self, s, p, k):
        me, dim = self.me, ORDER[p][k]
        here = self.shards[s].at[(3 * me.core + p,) + me.region(ORDER[p][:k])]
        return [
            remote(
                here,
                here,
                self.send_sem.at[s, p, k, offset - 1],
                self.recv_sem.at[s, p, k, offset - 1],
                me.along(dim, offset),
            )
            for offset in (1, 3, 2)
        ]

    def across(self, s, p):
        me = self.me
        here = self.shards[s].at[3 * me.core + p]
        return remote(here, here, self.side_send.at[s, p], self.side_recv.at[s, p], me.sibling())

    def start(self, s):
        for p in range(3):
            for copy in self.copies(s, p, 0):
                copy.start()

    def advance(self, s, k):
        for p in range(3):
            for copy in self.copies(s, p, k):
                copy.wait_recv()
            if k < 2:
                for copy in self.copies(s, p, k + 1):
                    copy.start()
            else:
                self.across(s, p).start()

    def finish(self, s):
        for p in range(3):
            self.across(s, p).wait_recv()

    def drain(self, s):
        for p in range(3):
            for k in range(3):
                for copy in self.copies(s, p, k):
                    copy.wait_send()
            self.across(s, p).wait_send()


class Total:
    scratch = [VMEM((5, 8, D), f32), VMEM((4, 3, 8, D), f32), DMA((4, 3)), DMA((4, 3))]

    def __init__(self, me, scratch):
        self.me = me
        self.held, self.slots, self.send_sem, self.recv_sem = scratch

    def copies(self, k):
        me = self.me
        devices = [me.sibling()] if k == 3 else [me.along(k, offset) for offset in (1, 2, 3)]
        return [
            remote(
                self.held.at[k],
                self.slots.at[k, n],
                self.send_sem.at[k, n],
                self.recv_sem.at[k, n],
                device,
            )
            for n, device in enumerate(devices)
        ]

    def send(self, k):
        for copy in self.copies(k):
            copy.start()

    def add(self, k):
        total = self.held[k]
        for n, copy in enumerate(self.copies(k)):
            copy.wait_recv()
            total = total + self.slots[k, n]
        self.held[k + 1] = total

    def drain(self):
        for k in range(4):
            for copy in self.copies(k):
                copy.wait_send()


class Reduce:
    scratch = [
        VMEM((3, 4, 4, 4, 48, 128), bf16),
        VMEM((3, 4, 4, 4, 48, 128), bf16),
        VMEM((3, 4, 4, 4, 48, 128), bf16),
        VMEM((3, 3, 3, 4, 4, 48, 128), bf16),
        VMEM((3, 3, 3, 4, 48, 128), bf16),
        VMEM((3, 3, 3, 48, 128), bf16),
        VMEM((3, 3, 48, 128), f32),
        VMEM((3, 3, 24, 128), f32),
        DMA((3, 2)),
        DMA((3, 3, 3, 3)),
        DMA((3, 3, 3, 3)),
        DMA((3, 2)),
    ]

    def __init__(self, me, shards, scratch):
        self.me, self.shards = me, shards
        self.side, self.slots = scratch[:3], scratch[3:6]
        self.summed, self.crossed = scratch[6:8]
        self.side_sem, self.send_sem, self.recv_sem, self.last_sem = scratch[8:]

    def across(self, s):
        me = self.me
        return remote(
            self.shards[s].at[pl.ds(3 * (1 - me.core), 3)],
            self.side[s],
            self.side_sem.at[s, 0],
            self.side_sem.at[s, 1],
            me.sibling(),
        )

    def copies(self, s, p, k):
        me, dim, whole = self.me, ORDER[p][2 - k], ORDER[p][: 2 - k]
        out = []
        for offset in (2, 1, 3):
            there = {dim: lax.rem(me.chip[dim] + offset, 4)}
            out.append(
                remote(
                    self.shards[s].at[(3 * me.core + p,) + me.region(whole, there)],
                    self.slots[k].at[s, p, offset - 1],
                    self.send_sem.at[s, p, k, offset - 1],
                    self.recv_sem.at[s, p, k, offset - 1],
                    me.along(dim, offset),
                )
            )
        return out

    def send(self, s, p, k):
        for copy in self.copies(s, p, k):
            copy.start()

    def begin(self, s):
        self.across(s).start()

    def enter(self, s):
        self.across(s).wait_recv()
        shards, side = self.shards[s], self.side[s]
        for p in range(3):
            t = 3 * self.me.core + p

            def step(i, carry):
                x, y = lax.div(i, 4), lax.rem(i, 4)
                total = shards[t, x, y].astype(f32) + side[p, x, y].astype(f32)
                shards[t, x, y] = total.astype(bf16)
                return carry

            lax.fori_loop(0, 16, step, 0)
            self.send(s, p, 0)

    def advance(self, s, k):
        me, shards, slots = self.me, self.shards[s], self.slots[k]
        for p in range(3):
            for copy in self.copies(s, p, k):
                copy.wait_recv()
            t, whole = 3 * me.core + p, sorted(ORDER[p][: 2 - k])
            if k == 2:
                total = shards[(t,) + me.chip].astype(f32)
                for n in range(3):
                    total = total + slots[s, p, n].astype(f32)
                self.summed[s, p] = total
                continue

            def step(i, carry):
                inner = (lax.div(i, 4), lax.rem(i, 4)) if k == 0 else (i,)
                chip = me.region((), dict(zip(whole, inner)))
                total = shards[(t,) + chip].astype(f32)
                for n in range(3):
                    total = total + slots[(s, p, n) + inner].astype(f32)
                shards[(t,) + chip] = total.astype(bf16)
                return carry

            lax.fori_loop(0, 16 if k == 0 else 4, step, 0)
            self.send(s, p, k + 1)
        if k == 2:
            self.last(s).start()

    def last(self, s):
        me = self.me
        return remote(
            self.summed.at[s, :, aligned(24 * (1 - me.core), 24, 8)],
            self.crossed.at[s],
            self.last_sem.at[s, 0],
            self.last_sem.at[s, 1],
            me.sibling(),
        )

    def finish(self, s, out):
        core = self.me.core
        self.last(s).wait_recv()
        for p in range(3):
            rows = pl.ds(24 * s, 24)
            own = self.summed[s, p, aligned(24 * core, 24, 8)]
            out[rows, aligned(384 * core + 128 * p, 128, 128)] = own
            out[rows, aligned(384 * (1 - core) + 128 * p, 128, 128)] = self.crossed[s, p]

    def drain(self, s):
        self.across(s).wait_send()
        self.last(s).wait_send()
        for p in range(3):
            for k in range(3):
                for copy in self.copies(s, p, k):
                    copy.wait_send()


def normal_of(x):
    center = x - jnp.mean(x, axis=-1, keepdims=True)
    rstd = lax.rsqrt(jnp.mean(center * center, axis=-1, keepdims=True) + NORM_EPS)
    return center * rstd, rstd


def norm_back(d_h, gain, xhat, rstd):
    e = d_h * gain
    inner = jnp.mean(e, axis=-1, keepdims=True) + xhat * jnp.mean(
        e * xhat, axis=-1, keepdims=True
    )
    return (e - inner) * rstd


def lanes_of(ref, *index):
    return jnp.concatenate([ref[(t,) + index] for t in range(ref.shape[0])], axis=-1)


def swapped(v):
    lane = lax.broadcasted_iota(jnp.int32, v.shape, 1)
    return jnp.where((lane & 63) < 32, pltpu.roll(v, 96, 1), pltpu.roll(v, 32, 1))


def first_head(shape):
    return lax.broadcasted_iota(jnp.int32, shape, 1) < HD


def split_heads(v):
    own, zero = first_head(v.shape), jnp.zeros_like(v)
    return jnp.concatenate([jnp.where(own, v, zero), jnp.where(own, zero, v)], axis=0)


def join_heads(v):
    half = v.shape[0] // 2
    return jnp.where(first_head((half, v.shape[1])), v[:half], v[half:])


class Layer:
    scratch = [
        VMEM((3 * D, D), bf16),
        VMEM((D, D), bf16),
        VMEM((2 * SEQ, D), bf16),
        VMEM((PAIRS, SEQ, 128), bf16),
        VMEM((2 * PAIRS, 2 * SEQ, 128), bf16),
        VMEM((PAIRS, SEQ, 128), bf16),
        VMEM((SEQ, D), f32),
        VMEM((SEQ, D), bf16),
        VMEM((SEQ, D), f32),
        VMEM((SEQ, D), f32),
        VMEM((SEQ, D), bf16),
        VMEM((PAIRS, SEQ, 128), bf16),
        VMEM((4, TILE, 5 * TILE), f32),
    ] + [VMEM((PAIRS, 2 * TILE, (i + 2) * TILE), bf16) for i in range(TILES)]

    def __init__(self, scratch):
        self.qkv, self.out, self.h1, self.q, self.kv, self.att, self.x2, self.h2 = scratch[:8]
        self.sum_a, self.sum_b, self.d_branch, self.d_att, self.mask = scratch[8:13]
        self.probs = scratch[13:17]

    def line(self, i):
        x, y = lax.div(i, 4), lax.rem(i, 4)
        row = (lax.rem(x, 2) * 4 + y) * 2 + lax.div(x, 2)
        return x, y, aligned(144 * row, 144, 16), aligned(48 * row, 48, 16)

    def unpack(self, shards, perm):
        def step(i, carry):
            x, y, rows_qkv, rows_out = self.line(i)
            block = jnp.concatenate([shards[t, x, y].reshape(192, 128) for t in range(6)], axis=1)
            block = dot_nn(perm[...], block).astype(bf16)
            self.qkv[rows_qkv] = block[:144]
            self.out[rows_out] = block[144:]
            return carry

        lax.fori_loop(0, 16, step, 0)

    def pack(self, shards, perm):
        def step(i, carry):
            x, y, rows_qkv, rows_out = self.line(i)
            block = jnp.concatenate([self.qkv[rows_qkv], self.out[rows_out]], axis=0)
            block = dot_tn(perm[...], block).astype(bf16)
            for t in range(6):
                shards[t, x, y] = block[:, 128 * t : 128 * t + 128].reshape(4, 48, 128)
            return carry

        lax.fori_loop(0, 16, step, 0)

    def masks(self, length, size):
        row = lax.broadcasted_iota(jnp.int32, (TILE, TILE), 0)
        col = lax.broadcasted_iota(jnp.int32, (TILE, TILE), 1)
        shift = jnp.where(size == 4, 2, jnp.where(size == 8, 3, 4))
        n_row = lax.shift_right_logical(row, jnp.full_like(row, shift))
        n_col = lax.shift_right_logical(col, jnp.full_like(col, shift))
        for i in range(TILES):
            for j in range(i + 2):
                key = min(j, i) * TILE + col
                seen = key < length
                if j == i:
                    seen = seen & (n_row > n_col)
                if j == i + 1:
                    seen = seen & (n_row == n_col)
                self.mask[i, :, j * TILE : (j + 1) * TILE] = jnp.where(seen, 0.0, MASKED)

    def norm_one(self, x, gains, first_row):
        gain = gains[0:1, :]

        def step(i, carry):
            rows = aligned(i * TILE, TILE, TILE)
            xhat, _ = normal_of(x[rows].astype(f32))
            self.h1[aligned(first_row + i * TILE, TILE, TILE)] = (xhat * gain).astype(bf16)
            return carry

        lax.fori_loop(0, TILES, step, 0)

    def project(self, cos, sin):
        def turned(v, scale):
            c, s = cos[...] * scale, sin[...] * scale
            if v.shape[0] == 2 * SEQ:
                c, s = jnp.concatenate([c, c], axis=0), jnp.concatenate([s, s], axis=0)
            return (v * c + swapped(v) * s).astype(bf16)

        for j in range(3):
            v = dot_nt(self.h1[:SEQ], self.qkv[256 * j : 256 * j + 256])
            for n in range(2):
                self.q[2 * j + n] = turned(v[:, 128 * n : 128 * n + 128], HD ** (-0.5))
        for j in range(6):
            v = dot_nt(self.h1[...], self.qkv[D + 256 * j : D + 256 * j + 256])
            for n in range(2):
                part = v[:, 128 * n : 128 * n + 128]
                self.kv[2 * j + n] = turned(part, 1.0) if j < 3 else part.astype(bf16)

    def keys(self, t, i):
        clean = self.kv[t, SEQ : SEQ + (i + 1) * TILE]
        return jnp.concatenate([clean, self.kv[t, i * TILE : (i + 1) * TILE]], axis=0)

    def attend(self, pair):
        for i in range(TILES):
            rows, width = pl.ds(i * TILE, TILE), (i + 2) * TILE
            queries = split_heads(self.q[pair, rows])
            scores = dot_nt(queries, self.keys(pair, i)).reshape(2, TILE, width)
            scores = (scores + self.mask[i, :, :width][None]).reshape(2 * TILE, width)
            raised = jnp.exp(scores - jnp.max(scores, axis=-1, keepdims=True))
            probs = raised * (1.0 / jnp.sum(raised, axis=-1, keepdims=True))
            probs = probs.astype(bf16)
            self.probs[i][pair] = probs
            mixed = dot_nn(probs, self.keys(PAIRS + pair, i))
            self.att[pair, rows] = join_heads(mixed).astype(bf16)

    def mix(self, x, gains):
        for j in range(3):
            cols = slice(256 * j, 256 * j + 256)
            branch = dot_nn(lanes_of(self.att), self.out[:, cols])
            self.x2[:, cols] = x[:, cols].astype(f32) + branch
        gain = gains[1:2, :]

        def step(i, carry):
            rows = aligned(i * TILE, TILE, TILE)
            xhat, _ = normal_of(self.x2[rows])
            self.h2[rows] = (xhat * gain).astype(bf16)
            self.sum_a[rows] = jnp.zeros((TILE, D), f32)
            self.sum_b[rows] = jnp.zeros((TILE, D), f32)
            return carry

        lax.fori_loop(0, TILES, step, 0)

    def feed(self, up, down, dy, j):
        rows = aligned(256 * j, 256, 256)
        w_up, w_down = lanes_of(up, rows), lanes_of(down, rows)
        u = dot_nt(self.h2[...], w_up)
        d_act = dot_nt(dy[...], w_down)
        c = (2.0 / np.pi) ** 0.5
        squared = u * u
        t = jnp.tanh(c * u * (1.0 + 0.044715 * squared))
        half = 0.5 * (1.0 + t)
        act = (u * half).astype(bf16)
        slope = half + 0.5 * u * (1.0 - t * t) * (c + (3 * 0.044715 * c) * squared)
        d_up = (slope * d_act).astype(bf16)
        self.sum_a[...] += dot_nn(act, w_down)
        self.sum_b[...] += dot_nn(d_up, w_up)
        g_up = dot_tn(d_up, self.h2[...]).astype(bf16)
        g_down = dot_tn(act, dy[...]).astype(bf16)
        for t in range(LANES):
            up[t, rows] = g_up[:, 128 * t : 128 * t + 128]
            down[t, rows] = g_down[:, 128 * t : 128 * t + 128]

    def back_two(self, dy, gains, outputs, d_gains):
        gain = gains[1:2, :]

        def step(i, carry):
            rows = aligned(i * TILE, TILE, TILE)
            x2 = self.x2[rows]
            outputs[rows] = (x2 + self.sum_a[rows]).astype(bf16)
            xhat, rstd = normal_of(x2)
            d_h = self.sum_b[rows]
            d_x2 = dy[rows].astype(f32) + norm_back(d_h, gain, xhat, rstd)
            self.sum_b[rows] = d_x2
            self.d_branch[rows] = d_x2.astype(bf16)
            return carry + jnp.sum(d_h * xhat, axis=0, keepdims=True)

        d_gains[1:2, :] = lax.fori_loop(0, TILES, step, jnp.zeros((1, D), f32))

    def back_mix(self):
        for j in range(3):
            rows = slice(256 * j, 256 * j + 256)
            d_att = dot_nt(self.d_branch[...], self.out[rows]).astype(bf16)
            self.d_att[2 * j] = d_att[:, :128]
            self.d_att[2 * j + 1] = d_att[:, 128:]
        for j in range(3):
            att = jnp.concatenate([self.att[2 * j], self.att[2 * j + 1]], axis=1)
            self.out[256 * j : 256 * j + 256] = dot_tn(att, self.d_branch[...]).astype(bf16)

    def back_attend(self, pair, cos, sin):
        d_keys, d_values, d_query = [None] * 2 * TILES, [None] * 2 * TILES, [None] * TILES
        for i in reversed(range(TILES)):
            rows = pl.ds(i * TILE, TILE)
            queries = split_heads(self.q[pair, rows])
            d_att = split_heads(self.d_att[pair, rows])
            low = self.probs[i][pair]
            probs = low.astype(f32)
            d_probs = dot_nt(d_att, self.keys(PAIRS + pair, i))
            delta = jnp.sum(probs * d_probs, axis=-1, keepdims=True)
            d_scores = (probs * (d_probs - delta)).astype(bf16)
            d_query[i] = join_heads(dot_nn(d_scores, self.keys(pair, i))) * HD ** (-0.5)
            d_k = dot_tn(d_scores, queries)
            d_v = dot_tn(low, d_att)
            for j in range(i + 2):
                to = TILES + i if j == i + 1 else j
                part = slice(j * TILE, (j + 1) * TILE)
                d_keys[to] = d_k[part] if d_keys[to] is None else d_keys[to] + d_k[part]
                d_values[to] = d_v[part] if d_values[to] is None else d_values[to] + d_v[part]

        def back(v, rows):
            return (v * cos[rows] - swapped(v) * sin[rows]).astype(bf16)

        for i in range(TILES):
            rows = slice(i * TILE, (i + 1) * TILE)
            clean = slice(SEQ + i * TILE, SEQ + (i + 1) * TILE)
            self.q[pair, rows] = back(d_query[i], rows)
            self.kv[pair, clean] = back(d_keys[i], rows)
            self.kv[pair, rows] = back(d_keys[TILES + i], rows)
            self.kv[PAIRS + pair, clean] = d_values[i].astype(bf16)
            self.kv[PAIRS + pair, rows] = d_values[TILES + i].astype(bf16)

    def back_project(self, gains, x, x_clean, grads, grads_clean, d_gains):
        gain = gains[0:1, :]

        def step(i, carry):
            clean = aligned(SEQ + i * TILE, TILE, TILE)
            own = aligned(i * TILE, TILE, TILE)
            d_h = dot_nn(lanes_of(self.kv, clean), self.qkv[D:])
            xhat, rstd = normal_of(x_clean[own].astype(f32))
            grads_clean[own] = norm_back(d_h, gain, xhat, rstd).astype(bf16)
            carry = carry + jnp.sum(d_h * xhat, axis=0, keepdims=True)
            d_proj = jnp.concatenate([lanes_of(self.q, own), lanes_of(self.kv, own)], axis=1)
            d_h = dot_nn(d_proj, self.qkv[...])
            xhat, rstd = normal_of(x[own].astype(f32))
            grads[own] = self.sum_b[own] + norm_back(d_h, gain, xhat, rstd)
            return carry + jnp.sum(d_h * xhat, axis=0, keepdims=True)

        d_gains[0:1, :] = lax.fori_loop(0, TILES, step, jnp.zeros((1, D), f32))

    def grad_project(self):
        for j in range(3):
            d_q = jnp.concatenate([self.q[2 * j], self.q[2 * j + 1]], axis=1)
            self.qkv[256 * j : 256 * j + 256] = dot_tn(d_q, self.h1[:SEQ]).astype(bf16)
        for j in range(6):
            d_kv = jnp.concatenate([self.kv[2 * j], self.kv[2 * j + 1]], axis=1)
            rows = slice(D + 256 * j, D + 256 * j + 256)
            self.qkv[rows] = dot_tn(d_kv, self.h1[...]).astype(bf16)


def split(refs, *groups):
    out, at = [], 0
    for group in groups:
        out.append(refs[at : at + len(group.scratch)])
        at += len(group.scratch)
    return out


def gather_kernel(packed, gains, x, s0, s1, s2, gains_all, x_clean, *scratch):
    gather_refs, total_refs = split(scratch, Gather, Total)
    clean_sem = scratch[-1]
    me = Place()
    me.greet()
    gather = Gather(me, packed, (s0, s1, s2), gather_refs)
    total = Total(me, total_refs)
    gather.swap().start()
    total.held[0] = gains[...]
    total.send(0)
    clean = remote(x, x_clean, clean_sem.at[0], clean_sem.at[1], me.partner())

    @pl.when(me.stream == 0)
    def _():
        clean.start()
        x_clean[...] = x[...]

    gather.swap().wait()
    gather.assemble()
    gather.start(0)
    for k in range(4):
        total.add(k)
        if k < 3:
            total.send(k + 1)
    gather.advance(0, 0)
    gather.start(1)
    gather.advance(0, 1)
    gather.advance(1, 0)
    gather.start(2)
    gather.advance(0, 2)
    gather.advance(1, 1)
    gather.advance(2, 0)
    gather.finish(0)
    gather.advance(1, 2)
    gather.advance(2, 1)
    gather.advance(2, 2)
    gather.finish(1)
    gather.finish(2)
    gains_all[...] = total.held[4]

    @pl.when(me.stream == 0)
    def _():
        clean.wait_send()

    @pl.when(me.stream == 1)
    def _():
        clean.wait_recv()

    total.drain()
    for s in range(3):
        gather.drain(s)


def layer_kernel(
    lengths, sizes, x, x_clean, dy, gains, perm, cos, sin, s0, s1, s2,
    outputs, grads, grads_clean, d_gains, g0, g1, g2, *scratch
):
    layer = Layer(scratch)
    g1[...] = s1[...]
    g2[...] = s2[...]
    layer.masks(lengths[0], sizes[0])
    layer.norm_one(x, gains, 0)
    layer.norm_one(x_clean, gains, SEQ)
    layer.unpack(s0, perm)
    layer.project(cos, sin)

    def forward(pair, carry):
        layer.attend(pair)
        return carry

    lax.fori_loop(0, PAIRS, forward, 0)
    layer.mix(x, gains)
    up, down = g1.reshape(6, FF, 128), g2.reshape(6, FF, 128)

    def feed(j, carry):
        layer.feed(up, down, dy, j)
        return carry

    lax.fori_loop(0, FF // 256, feed, 0)
    d_gains[...] = jnp.zeros((8, D), f32)
    layer.back_two(dy, gains, outputs, d_gains)
    layer.back_mix()

    def backward(pair, carry):
        layer.back_attend(pair, cos, sin)
        return carry

    lax.fori_loop(0, PAIRS, backward, 0)
    layer.back_project(gains, x, x_clean, grads, grads_clean, d_gains)
    layer.grad_project()
    layer.pack(g0, perm)


def reduce_kernel(s0, s1, s2, d_gains, own, given, grads, d_gains_all, grads_in, *scratch):
    reduce_refs, total_refs = split(scratch, Reduce, Total)
    back, back_sem = scratch[-2:]
    me = Place()
    me.greet()
    reduce = Reduce(me, (s0, s1, s2), reduce_refs)
    total = Total(me, total_refs)
    clean = remote(given, back, back_sem.at[0], back_sem.at[1], me.partner())
    for s in (2, 1, 0):
        reduce.begin(s)
    total.held[0] = d_gains[...]
    total.send(0)

    @pl.when(me.stream == 1)
    def _():
        clean.start()
        back[...] = jnp.zeros((SEQ, D), bf16)

    reduce.enter(2)
    total.add(0)
    total.send(1)
    reduce.enter(1)
    total.add(1)
    total.send(2)
    reduce.advance(2, 0)
    total.add(2)
    total.send(3)
    reduce.enter(0)
    total.add(3)
    reduce.advance(1, 0)
    reduce.advance(2, 1)
    reduce.advance(0, 0)
    reduce.advance(1, 1)
    reduce.advance(2, 2)
    reduce.advance(0, 1)
    reduce.advance(1, 2)
    reduce.advance(0, 2)
    for s in (2, 1, 0):
        reduce.finish(s, grads)
    d_gains_all[...] = total.held[4]

    @pl.when(me.stream == 0)
    def _():
        clean.wait_recv()
        grads_in[...] = (own[...] + given[...].astype(f32) + back[...].astype(f32)).astype(bf16)

    @pl.when(me.stream == 1)
    def _():
        clean.wait_send()
        grads_in[...] = own[...].astype(bf16)

    total.drain()
    for s in range(3):
        reduce.drain(s)


def adam(weight, grad, first, second, rate):
    first_new = BETA_ONE * first + (1.0 - BETA_ONE) * grad
    second_new = BETA_TWO * second + (1.0 - BETA_TWO) * grad * grad
    fix_one = 1.0 - BETA_ONE**STEP
    fix_two = 1.0 - BETA_TWO**STEP
    update = first_new / fix_one / (jnp.sqrt(second_new / fix_two) + ADAM_EPS)
    return (weight - rate * (update + WEIGHT_DECAY * weight), first_new, second_new)


ROWS = ((0, 18), (18, 24), (24, 48), (48, 72))


def adam_kernel(grads, d_gains, *refs):
    weights, firsts, seconds, outs = refs[:5], refs[5:10], refs[10:15], refs[15:]
    for n in range(5):
        grad = d_gains[...] if n == 4 else grads[ROWS[n][0] : ROWS[n][1]]
        new = adam(weights[n][...], grad, firsts[n][...], seconds[n][...], RATES[n])
        for part in range(3):
            outs[5 * part + n][...] = new[part]
        if n < 4:
            outs[15 + n][...] = new[0].astype(bf16)


def call(kernel, out_shape, operands, scratch=(), collective=None, smem=0):
    spec = pl.BlockSpec(memory_space=VMEM)
    return pl.pallas_call(
        kernel,
        out_shape=out_shape,
        in_specs=[pl.BlockSpec(memory_space=pltpu.SMEM)] * smem + [spec] * (len(operands) - smem),
        out_specs=jax.tree.map(lambda _: spec, out_shape),
        scratch_shapes=list(scratch),
        compiler_params=pltpu.CompilerParams(
            collective_id=collective,
            has_side_effects=collective is not None,
            vmem_limit_bytes=60 << 20,
        ),
    )(*operands)


def permutation():
    perm = np.zeros((192, 192), np.float32)
    for row in range(192):
        if row < 144:
            perm[row, 24 * (row // 18) + row % 18] = 1
        else:
            perm[row, 24 * ((row - 144) // 6) + 18 + (row - 144) % 6] = 1
    return perm


def rotary_tables():
    frequency = 10000.0 ** (-2.0 * np.arange(HD // 2) / HD)
    angles = (np.arange(SEQ)[:, None] * frequency[None, :]).astype(np.float32)
    cos, sin = np.cos(angles), np.sin(angles)
    return np.tile(cos, (1, 4)), np.concatenate([-sin, sin, -sin, sin], axis=1)


def local(
    inputs, cotangent, lengths, block_sizes, w_qkv, w_out, w_up, w_down, gains,
    first_qkv, first_out, first_up, first_down, first_gains,
    second_qkv, second_out, second_up, second_down, second_gains,
):
    shape = jax.ShapeDtypeStruct
    shards = shape(SHARDS, bf16)
    masters = (w_qkv.T, w_out, w_up.T, w_down, gains)
    firsts = (first_qkv.T, first_out, first_up.T, first_down, first_gains)
    seconds = (second_qkv.T, second_out, second_up.T, second_down, second_gains)
    place = 6 * lax.axis_index(AXES)
    packed = jnp.concatenate(masters[:4], axis=0)
    gains_low = gains.astype(bf16).astype(f32)
    placed = lax.dynamic_update_slice(jnp.zeros((8, D), f32), gains_low, (0, place))
    x, dy = inputs[0, 0], cotangent[0, 0]
    rows16, rows32 = shape((SEQ, D), bf16), shape((SEQ, D), f32)
    small = shape((8, D), f32)
    s0, s1, s2, gains_all, x_clean = call(
        gather_kernel,
        (shards, shards, shards, small, rows16),
        (packed, placed, x),
        Gather.scratch + Total.scratch + [DMA((2,))],
        collective=0,
    )
    cos, sin = rotary_tables()
    outputs, own, given, d_gains, g0, g1, g2 = call(
        layer_kernel,
        (rows16, rows32, rows16, small, shards, shards, shards),
        (lengths, block_sizes, x, x_clean, dy, gains_all, jnp.asarray(permutation(), bf16),
         jnp.asarray(cos, f32), jnp.asarray(sin, f32), s0, s1, s2),
        Layer.scratch,
        smem=2,
    )
    grads, d_gains, input_grads = call(
        reduce_kernel,
        (shape((72, D), f32), small, rows16),
        (g0, g1, g2, d_gains, own, given),
        Reduce.scratch + Total.scratch + [VMEM((SEQ, D), bf16), DMA((2,))],
        collective=1,
    )
    d_gains = lax.dynamic_slice(d_gains, (0, place), (2, 6))
    like = [shape(w.shape, f32) for w in masters]
    new = call(
        adam_kernel,
        like * 3 + [shape(w.shape, bf16) for w in masters[:4]],
        (grads, d_gains, *masters, *firsts, *seconds),
    )
    turned = [v.T if n % 5 in (0, 2) else v for n, v in enumerate(new)]
    return (outputs[None, None], input_grads[None, None], *turned)


def solution(mesh):
    mesh = Mesh(mesh.devices.reshape(2, 4, 2, 4, 2), AXES)
    data, one = P("xl", AXES[1:], None, None), P(AXES[1:])
    cols, rows = P(None, AXES), P(AXES, None)
    state = (cols, rows, cols, rows, cols)
    return jax.shard_map(
        local,
        mesh=mesh,
        in_specs=(data, data, one, one) + state * 3,
        out_specs=(data, data) + state * 3 + state[:4],
        check_vma=False,
    )
```

```python
import functools

import jax
import jax.numpy as jnp
import numpy as np
from jax import lax
from jax.experimental import pallas as pl
from jax.experimental.pallas import tpu as pltpu
from jax.sharding import Mesh
from jax.sharding import PartitionSpec as P

D = 768
H = 12
HD = 64
FF = 3072
SEQ = 512
STEP = 7
TILE = 128
TILES = SEQ // TILE
PAIRS = H // 2
LANES = D // 128
NORM_EPS = 1e-05
BETA_ONE = 0.5
BETA_TWO = 0.5
ADAM_EPS = 1e-08
WEIGHT_DECAY = 0.01
GAIN_RATE = 0.2
RATES = (D ** (-0.5), H ** (-0.5), D ** (-0.5), FF ** (-0.5), GAIN_RATE)
AXES = ("xl", "y", "xh", "z", "core")
ORDER = ((0, 1, 2), (1, 2, 0), (2, 0, 1))
SHARDS = (6, 4, 4, 4, 48, 128)
MASKED = -1e30

f32 = jnp.float32
bf16 = jnp.bfloat16
VMEM = pltpu.VMEM
DMA = pltpu.SemaphoreType.DMA
MESH = pl.DeviceIdType.MESH


def remote(src, dst, send, recv, device):
    return pltpu.make_async_remote_copy(
        src_ref=src,
        dst_ref=dst,
        send_sem=send,
        recv_sem=recv,
        device_id=device,
        device_id_type=MESH,
    )


def dot_nn(a, b):
    return jnp.dot(a, b, preferred_element_type=f32)


def dot_nt(a, b):
    return lax.dot_general(a, b, (((1,), (1,)), ((), ())), preferred_element_type=f32)


def dot_tn(a, b):
    return lax.dot_general(a, b, (((0,), (0,)), ((), ())), preferred_element_type=f32)


def aligned(start, size, step):
    return pl.ds(pl.multiple_of(start, step), size)


class Place:
    def __init__(self):
        self.stream = lax.axis_index("xl")
        self.core = lax.axis_index("core")
        self.chip = (
            lax.axis_index("xh") * 2 + self.stream,
            lax.axis_index("y"),
            lax.axis_index("z"),
        )

    def device(self, chip, core):
        return (lax.rem(chip[0], 2), chip[1], lax.div(chip[0], 2), chip[2], core)

    def along(self, dim, offset):
        chip = list(self.chip)
        chip[dim] = lax.rem(chip[dim] + offset, 4)
        return self.device(chip, self.core)

    def sibling(self):
        return self.device(self.chip, 1 - self.core)

    def partner(self):
        chip = (self.chip[0] + 1 - 2 * self.stream, self.chip[1], self.chip[2])
        return self.device(chip, self.core)

    def region(self, whole, fixed=None):
        out = []
        for dim in range(3):
            if fixed and dim in fixed:
                out.append(fixed[dim])
            elif dim in whole:
                out.append(slice(None))
            else:
                out.append(self.chip[dim])
        return tuple(out)

    def greet(self):
        barrier = pltpu.get_barrier_semaphore()
        others = [self.sibling()]
        others += [self.along(dim, offset) for dim in range(3) for offset in (1, 2, 3)]
        for other in others:
            pl.semaphore_signal(barrier, inc=1, device_id=other, device_id_type=MESH)
        pl.semaphore_wait(barrier, len(others))


class Gather:
    scratch = [
        VMEM((72, 384), f32),
        VMEM((3, 48, 384), f32),
        DMA((3, 3, 3, 3)),
        DMA((3, 3, 3, 3)),
        DMA((3, 3)),
        DMA((3, 3)),
        DMA((2,)),
    ]

    def __init__(self, me, packed, shards, scratch):
        self.me, self.packed, self.shards = me, packed, shards
        self.half, self.block, self.send_sem, self.recv_sem = scratch[:4]
        self.side_send, self.side_recv, self.swap_sem = scratch[4:]

    def swap(self):
        me = self.me
        return remote(
            self.packed.at[:, aligned(384 * (1 - me.core), 384, 128)],
            self.half,
            self.swap_sem.at[0],
            self.swap_sem.at[1],
            me.sibling(),
        )

    def assemble(self):
        core = self.me.core
        own = self.packed[:, aligned(384 * core, 384, 128)]
        for s in range(3):
            self.block[s, aligned(24 * core, 24, 8)] = own[24 * s : 24 * s + 24]
            self.block[s, aligned(24 * (1 - core), 24, 8)] = self.half[24 * s : 24 * s + 24]
        for s in range(3):
            value = self.block[s].astype(bf16)
            for p in range(3):
                self.shards[s][(3 * core + p,) + self.me.chip] = value[:, 128 * p : 128 * p + 128]

    def copies(self, s, p, k):
        me, dim = self.me, ORDER[p][k]
        here = self.shards[s].at[(3 * me.core + p,) + me.region(ORDER[p][:k])]
        return [
            remote(
                here,
                here,
                self.send_sem.at[s, p, k, offset - 1],
                self.recv_sem.at[s, p, k, offset - 1],
                me.along(dim, offset),
            )
            for offset in (1, 3, 2)
        ]

    def across(self, s, p):
        me = self.me
        here = self.shards[s].at[3 * me.core + p]
        return remote(here, here, self.side_send.at[s, p], self.side_recv.at[s, p], me.sibling())

    def start(self, s):
        for p in range(3):
            for copy in self.copies(s, p, 0):
                copy.start()

    def advance(self, s, k):
        for p in range(3):
            for copy in self.copies(s, p, k):
                copy.wait_recv()
            if k < 2:
                for copy in self.copies(s, p, k + 1):
                    copy.start()
            else:
                self.across(s, p).start()

    def finish(self, s):
        for p in range(3):
            self.across(s, p).wait_recv()

    def drain(self, s):
        for p in range(3):
            for k in range(3):
                for copy in self.copies(s, p, k):
                    copy.wait_send()
            self.across(s, p).wait_send()


class Total:
    scratch = [VMEM((5, 8, D), f32), VMEM((4, 3, 8, D), f32), DMA((4, 3)), DMA((4, 3))]

    def __init__(self, me, scratch):
        self.me = me
        self.held, self.slots, self.send_sem, self.recv_sem = scratch

    def copies(self, k):
        me = self.me
        devices = [me.sibling()] if k == 3 else [me.along(k, offset) for offset in (1, 2, 3)]
        return [
            remote(
                self.held.at[k],
                self.slots.at[k, n],
                self.send_sem.at[k, n],
                self.recv_sem.at[k, n],
                device,
            )
            for n, device in enumerate(devices)
        ]

    def send(self, k):
        for copy in self.copies(k):
            copy.start()

    def add(self, k):
        total = self.held[k]
        for n, copy in enumerate(self.copies(k)):
            copy.wait_recv()
            total = total + self.slots[k, n]
        self.held[k + 1] = total

    def drain(self):
        for k in range(4):
            for copy in self.copies(k):
                copy.wait_send()


class Reduce:
    scratch = [
        VMEM((3, 4, 4, 4, 48, 128), bf16),
        VMEM((3, 4, 4, 4, 48, 128), bf16),
        VMEM((3, 4, 4, 4, 48, 128), bf16),
        VMEM((3, 3, 3, 4, 4, 48, 128), bf16),
        VMEM((3, 3, 3, 4, 48, 128), bf16),
        VMEM((3, 3, 3, 48, 128), bf16),
        VMEM((3, 3, 48, 128), f32),
        VMEM((3, 3, 24, 128), f32),
        DMA((3, 2)),
        DMA((3, 3, 3, 3)),
        DMA((3, 3, 3, 3)),
        DMA((3, 2)),
    ]

    def __init__(self, me, shards, scratch):
        self.me, self.shards = me, shards
        self.side, self.slots = scratch[:3], scratch[3:6]
        self.summed, self.crossed = scratch[6:8]
        self.side_sem, self.send_sem, self.recv_sem, self.last_sem = scratch[8:]

    def across(self, s):
        me = self.me
        return remote(
            self.shards[s].at[pl.ds(3 * (1 - me.core), 3)],
            self.side[s],
            self.side_sem.at[s, 0],
            self.side_sem.at[s, 1],
            me.sibling(),
        )

    def copies(self, s, p, k):
        me, dim, whole = self.me, ORDER[p][2 - k], ORDER[p][: 2 - k]
        out = []
        for offset in (2, 1, 3):
            there = {dim: lax.rem(me.chip[dim] + offset, 4)}
            out.append(
                remote(
                    self.shards[s].at[(3 * me.core + p,) + me.region(whole, there)],
                    self.slots[k].at[s, p, offset - 1],
                    self.send_sem.at[s, p, k, offset - 1],
                    self.recv_sem.at[s, p, k, offset - 1],
                    me.along(dim, offset),
                )
            )
        return out

    def send(self, s, p, k):
        for copy in self.copies(s, p, k):
            copy.start()

    def begin(self, s):
        self.across(s).start()

    def enter(self, s):
        self.across(s).wait_recv()
        shards, side = self.shards[s], self.side[s]
        for p in range(3):
            t = 3 * self.me.core + p

            def step(i, carry):
                x, y = lax.div(i, 4), lax.rem(i, 4)
                total = shards[t, x, y].astype(f32) + side[p, x, y].astype(f32)
                shards[t, x, y] = total.astype(bf16)
                return carry

            lax.fori_loop(0, 16, step, 0)
            self.send(s, p, 0)

    def advance(self, s, k):
        me, shards, slots = self.me, self.shards[s], self.slots[k]
        for p in range(3):
            for copy in self.copies(s, p, k):
                copy.wait_recv()
            t, whole = 3 * me.core + p, sorted(ORDER[p][: 2 - k])
            if k == 2:
                total = shards[(t,) + me.chip].astype(f32)
                for n in range(3):
                    total = total + slots[s, p, n].astype(f32)
                self.summed[s, p] = total
                continue

            def step(i, carry):
                inner = (lax.div(i, 4), lax.rem(i, 4)) if k == 0 else (i,)
                chip = me.region((), dict(zip(whole, inner)))
                total = shards[(t,) + chip].astype(f32)
                for n in range(3):
                    total = total + slots[(s, p, n) + inner].astype(f32)
                shards[(t,) + chip] = total.astype(bf16)
                return carry

            lax.fori_loop(0, 16 if k == 0 else 4, step, 0)
            self.send(s, p, k + 1)
        if k == 2:
            self.last(s).start()

    def last(self, s):
        me = self.me
        return remote(
            self.summed.at[s, :, aligned(24 * (1 - me.core), 24, 8)],
            self.crossed.at[s],
            self.last_sem.at[s, 0],
            self.last_sem.at[s, 1],
            me.sibling(),
        )

    def finish(self, s, out):
        core = self.me.core
        self.last(s).wait_recv()
        for p in range(3):
            rows = pl.ds(24 * s, 24)
            own = self.summed[s, p, aligned(24 * core, 24, 8)]
            out[rows, aligned(384 * core + 128 * p, 128, 128)] = own
            out[rows, aligned(384 * (1 - core) + 128 * p, 128, 128)] = self.crossed[s, p]

    def drain(self, s):
        self.across(s).wait_send()
        self.last(s).wait_send()
        for p in range(3):
            for k in range(3):
                for copy in self.copies(s, p, k):
                    copy.wait_send()


def normal_of(x):
    center = x - jnp.mean(x, axis=-1, keepdims=True)
    rstd = lax.rsqrt(jnp.mean(center * center, axis=-1, keepdims=True) + NORM_EPS)
    return center * rstd, rstd


def norm_back(d_h, gain, xhat, rstd):
    e = d_h * gain
    inner = jnp.mean(e, axis=-1, keepdims=True) + xhat * jnp.mean(
        e * xhat, axis=-1, keepdims=True
    )
    return (e - inner) * rstd


def lanes_of(ref, *index):
    return jnp.concatenate([ref[(t,) + index] for t in range(ref.shape[0])], axis=-1)


def swapped(v):
    lane = lax.broadcasted_iota(jnp.int32, v.shape, 1)
    return jnp.where((lane & 63) < 32, pltpu.roll(v, 96, 1), pltpu.roll(v, 32, 1))


def first_head(shape):
    return lax.broadcasted_iota(jnp.int32, shape, 1) < HD


def split_heads(v):
    own, zero = first_head(v.shape), jnp.zeros_like(v)
    return jnp.concatenate([jnp.where(own, v, zero), jnp.where(own, zero, v)], axis=0)


def join_heads(v):
    half = v.shape[0] // 2
    return jnp.where(first_head((half, v.shape[1])), v[:half], v[half:])


class Layer:
    scratch = [
        VMEM((3 * D, D), bf16),
        VMEM((D, D), bf16),
        VMEM((2 * SEQ, D), bf16),
        VMEM((PAIRS, SEQ, 128), bf16),
        VMEM((2 * PAIRS, 2 * SEQ, 128), bf16),
        VMEM((PAIRS, SEQ, 128), bf16),
        VMEM((SEQ, D), f32),
        VMEM((SEQ, D), bf16),
        VMEM((SEQ, D), f32),
        VMEM((SEQ, D), f32),
        VMEM((PAIRS, SEQ, 128), bf16),
        VMEM((4, TILE, 5 * TILE), f32),
    ] + [VMEM((PAIRS, 2 * TILE, (i + 2) * TILE), bf16) for i in range(TILES)]

    def __init__(self, scratch):
        self.qkv, self.out, self.h1, self.q, self.kv, self.att, self.x2, self.h2 = scratch[:8]
        self.sum_a, self.sum_b, self.d_att, self.mask = scratch[8:12]
        self.probs = scratch[12:16]
        self.d_branch = self.h2

    def line(self, i):
        x, y = lax.div(i, 4), lax.rem(i, 4)
        row = (lax.rem(x, 2) * 4 + y) * 2 + lax.div(x, 2)
        return x, y, aligned(144 * row, 144, 16), aligned(48 * row, 48, 16)

    def unpack(self, shards, perm):
        def step(i, carry):
            x, y, rows_qkv, rows_out = self.line(i)
            block = jnp.concatenate([shards[t, x, y].reshape(192, 128) for t in range(6)], axis=1)
            block = dot_nn(perm[...], block).astype(bf16)
            self.qkv[rows_qkv] = block[:144]
            self.out[rows_out] = block[144:]
            return carry

        lax.fori_loop(0, 16, step, 0)

    def pack(self, shards, perm):
        def step(i, carry):
            x, y, rows_qkv, rows_out = self.line(i)
            block = jnp.concatenate([self.qkv[rows_qkv], self.out[rows_out]], axis=0)
            block = dot_tn(perm[...], block).astype(bf16)
            for t in range(6):
                shards[t, x, y] = block[:, 128 * t : 128 * t + 128].reshape(4, 48, 128)
            return carry

        lax.fori_loop(0, 16, step, 0)

    def masks(self, length, size):
        row = lax.broadcasted_iota(jnp.int32, (TILE, TILE), 0)
        col = lax.broadcasted_iota(jnp.int32, (TILE, TILE), 1)
        shift = jnp.where(size == 4, 2, jnp.where(size == 8, 3, 4))
        n_row = lax.shift_right_logical(row, jnp.full_like(row, shift))
        n_col = lax.shift_right_logical(col, jnp.full_like(col, shift))
        for i in range(TILES):
            for j in range(i + 2):
                key = min(j, i) * TILE + col
                seen = key < length
                if j == i:
                    seen = seen & (n_row > n_col)
                if j == i + 1:
                    seen = seen & (n_row == n_col)
                self.mask[i, :, j * TILE : (j + 1) * TILE] = jnp.where(seen, 0.0, MASKED)

    def norm_one(self, x, gains, first_row):
        gain = gains[0:1, :]

        def step(i, carry):
            rows = aligned(i * TILE, TILE, TILE)
            xhat, _ = normal_of(x[rows].astype(f32))
            self.h1[aligned(first_row + i * TILE, TILE, TILE)] = (xhat * gain).astype(bf16)
            return carry

        lax.fori_loop(0, TILES, step, 0)

    def project(self, cos, sin):
        def turned(v, scale):
            c, s = cos[...] * scale, sin[...] * scale
            if v.shape[0] == 2 * SEQ:
                c, s = jnp.concatenate([c, c], axis=0), jnp.concatenate([s, s], axis=0)
            return (v * c + swapped(v) * s).astype(bf16)

        for j in range(3):
            v = dot_nt(self.h1[:SEQ], self.qkv[256 * j : 256 * j + 256])
            for n in range(2):
                self.q[2 * j + n] = turned(v[:, 128 * n : 128 * n + 128], HD ** (-0.5))
        for j in range(6):
            v = dot_nt(self.h1[...], self.qkv[D + 256 * j : D + 256 * j + 256])
            for n in range(2):
                part = v[:, 128 * n : 128 * n + 128]
                self.kv[2 * j + n] = turned(part, 1.0) if j < 3 else part.astype(bf16)

    def keys(self, t, i):
        clean = self.kv[t, SEQ : SEQ + (i + 1) * TILE]
        return jnp.concatenate([clean, self.kv[t, i * TILE : (i + 1) * TILE]], axis=0)

    def attend(self, pair):
        for i in range(TILES):
            rows, width = pl.ds(i * TILE, TILE), (i + 2) * TILE
            queries = split_heads(self.q[pair, rows])
            scores = dot_nt(queries, self.keys(pair, i)).reshape(2, TILE, width)
            scores = (scores + self.mask[i, :, :width][None]).reshape(2 * TILE, width)
            raised = jnp.exp(scores - jnp.max(scores, axis=-1, keepdims=True))
            probs = raised * (1.0 / jnp.sum(raised, axis=-1, keepdims=True))
            probs = probs.astype(bf16)
            self.probs[i][pair] = probs
            mixed = dot_nn(probs, self.keys(PAIRS + pair, i))
            self.att[pair, rows] = join_heads(mixed).astype(bf16)

    def mix(self, x, gains):
        for j in range(3):
            cols = slice(256 * j, 256 * j + 256)
            branch = dot_nn(lanes_of(self.att), self.out[:, cols])
            self.x2[:, cols] = x[:, cols].astype(f32) + branch
        gain = gains[1:2, :]

        def step(i, carry):
            rows = aligned(i * TILE, TILE, TILE)
            xhat, _ = normal_of(self.x2[rows])
            self.h2[rows] = (xhat * gain).astype(bf16)
            self.sum_a[rows] = jnp.zeros((TILE, D), f32)
            self.sum_b[rows] = jnp.zeros((TILE, D), f32)
            return carry

        lax.fori_loop(0, TILES, step, 0)

    def feed(self, up, down, dy, j):
        rows = aligned(256 * j, 256, 256)
        w_up, w_down = lanes_of(up, rows), lanes_of(down, rows)
        u = dot_nt(self.h2[...], w_up)
        d_act = dot_nt(dy[...], w_down)
        c = (2.0 / np.pi) ** 0.5
        squared = u * u
        t = jnp.tanh(c * u * (1.0 + 0.044715 * squared))
        half = 0.5 * (1.0 + t)
        act = (u * half).astype(bf16)
        slope = half + 0.5 * u * (1.0 - t * t) * (c + (3 * 0.044715 * c) * squared)
        d_up = (slope * d_act).astype(bf16)
        self.sum_a[...] += dot_nn(act, w_down)
        self.sum_b[...] += dot_nn(d_up, w_up)
        g_up = dot_tn(d_up, self.h2[...]).astype(bf16)
        g_down = dot_tn(act, dy[...]).astype(bf16)
        for t in range(LANES):
            up[t, rows] = g_up[:, 128 * t : 128 * t + 128]
            down[t, rows] = g_down[:, 128 * t : 128 * t + 128]

    def back_two(self, dy, gains, outputs, d_gains):
        gain = gains[1:2, :]

        def step(i, carry):
            rows = aligned(i * TILE, TILE, TILE)
            x2 = self.x2[rows]
            outputs[rows] = (x2 + self.sum_a[rows]).astype(bf16)
            xhat, rstd = normal_of(x2)
            d_h = self.sum_b[rows]
            d_x2 = dy[rows].astype(f32) + norm_back(d_h, gain, xhat, rstd)
            self.sum_b[rows] = d_x2
            self.d_branch[rows] = d_x2.astype(bf16)
            return carry + jnp.sum(d_h * xhat, axis=0, keepdims=True)

        d_gains[1:2, :] = lax.fori_loop(0, TILES, step, jnp.zeros((1, D), f32))

    def back_mix(self):
        for j in range(3):
            rows = slice(256 * j, 256 * j + 256)
            d_att = dot_nt(self.d_branch[...], self.out[rows]).astype(bf16)
            self.d_att[2 * j] = d_att[:, :128]
            self.d_att[2 * j + 1] = d_att[:, 128:]
        for j in range(3):
            att = jnp.concatenate([self.att[2 * j], self.att[2 * j + 1]], axis=1)
            self.out[256 * j : 256 * j + 256] = dot_tn(att, self.d_branch[...]).astype(bf16)

    def back_attend(self, pair, cos, sin):
        d_keys, d_values, d_query = [None] * 2 * TILES, [None] * 2 * TILES, [None] * TILES
        for i in reversed(range(TILES)):
            rows = pl.ds(i * TILE, TILE)
            queries = split_heads(self.q[pair, rows])
            d_att = split_heads(self.d_att[pair, rows])
            low = self.probs[i][pair]
            probs = low.astype(f32)
            d_probs = dot_nt(d_att, self.keys(PAIRS + pair, i))
            delta = jnp.sum(probs * d_probs, axis=-1, keepdims=True)
            d_scores = (probs * (d_probs - delta)).astype(bf16)
            d_query[i] = join_heads(dot_nn(d_scores, self.keys(pair, i))) * HD ** (-0.5)
            d_k = dot_tn(d_scores, queries)
            d_v = dot_tn(low, d_att)
            for j in range(i + 2):
                to = TILES + i if j == i + 1 else j
                part = slice(j * TILE, (j + 1) * TILE)
                d_keys[to] = d_k[part] if d_keys[to] is None else d_keys[to] + d_k[part]
                d_values[to] = d_v[part] if d_values[to] is None else d_values[to] + d_v[part]

        def back(v, rows):
            return (v * cos[rows] - swapped(v) * sin[rows]).astype(bf16)

        for i in range(TILES):
            rows = slice(i * TILE, (i + 1) * TILE)
            clean = slice(SEQ + i * TILE, SEQ + (i + 1) * TILE)
            self.q[pair, rows] = back(d_query[i], rows)
            self.kv[pair, clean] = back(d_keys[i], rows)
            self.kv[pair, rows] = back(d_keys[TILES + i], rows)
            self.kv[PAIRS + pair, clean] = d_values[i].astype(bf16)
            self.kv[PAIRS + pair, rows] = d_values[TILES + i].astype(bf16)

    def back_project(self, gains, x, x_clean, grads, grads_clean, d_gains):
        gain = gains[0:1, :]

        def step(i, carry):
            clean = aligned(SEQ + i * TILE, TILE, TILE)
            own = aligned(i * TILE, TILE, TILE)
            d_h = dot_nn(lanes_of(self.kv, clean), self.qkv[D:])
            xhat, rstd = normal_of(x_clean[own].astype(f32))
            grads_clean[own] = norm_back(d_h, gain, xhat, rstd).astype(bf16)
            carry = carry + jnp.sum(d_h * xhat, axis=0, keepdims=True)
            d_proj = jnp.concatenate([lanes_of(self.q, own), lanes_of(self.kv, own)], axis=1)
            d_h = dot_nn(d_proj, self.qkv[...])
            xhat, rstd = normal_of(x[own].astype(f32))
            grads[own] = self.sum_b[own] + norm_back(d_h, gain, xhat, rstd)
            return carry + jnp.sum(d_h * xhat, axis=0, keepdims=True)

        d_gains[0:1, :] = lax.fori_loop(0, TILES, step, jnp.zeros((1, D), f32))

    def grad_project(self):
        for j in range(3):
            d_q = jnp.concatenate([self.q[2 * j], self.q[2 * j + 1]], axis=1)
            self.qkv[256 * j : 256 * j + 256] = dot_tn(d_q, self.h1[:SEQ]).astype(bf16)
        for j in range(6):
            d_kv = jnp.concatenate([self.kv[2 * j], self.kv[2 * j + 1]], axis=1)
            rows = slice(D + 256 * j, D + 256 * j + 256)
            self.qkv[rows] = dot_tn(d_kv, self.h1[...]).astype(bf16)


class Rest:
    scratch = [
        VMEM(SHARDS, bf16),
        VMEM(SHARDS, bf16),
        VMEM(SHARDS, bf16),
        VMEM((SEQ, D), bf16),
        VMEM((SEQ, D), bf16),
        VMEM((8, D), f32),
        DMA((2,)),
        DMA((2,)),
    ]


def split(refs, *groups):
    out, at = [], 0
    for group in groups:
        out.append(refs[at : at + len(group.scratch)])
        at += len(group.scratch)
    return out


def step_kernel(
    lengths, sizes, packed, gains_in, x, dy, perm, cos, sin,
    outputs, grads_in, grads, d_gains_all, *scratch
):
    gather_refs, total_refs, layer_refs, reduce_refs, back_refs, rest = split(
        scratch, Gather, Total, Layer, Reduce, Total, Rest
    )
    shards = rest[:3]
    x_clean, back, d_gains, clean_sem, back_sem = rest[3:]
    me = Place()
    me.greet()
    gather = Gather(me, packed, shards, gather_refs)
    total = Total(me, total_refs)
    total_back = Total(me, back_refs)
    layer = Layer(layer_refs)
    reduce = Reduce(me, shards, reduce_refs)
    gains, given = total.held.at[4], layer.h2
    to_clean = remote(x, x_clean, clean_sem.at[0], clean_sem.at[1], me.partner())
    from_noisy = remote(given, back, back_sem.at[0], back_sem.at[1], me.partner())
    gather.swap().start()
    total.held[0] = gains_in[...]
    total.send(0)

    @pl.when(me.stream == 0)
    def _():
        to_clean.start()
        x_clean[...] = x[...]

    gather.swap().wait()
    gather.assemble()
    gather.start(0)
    layer.masks(lengths[0], sizes[0])
    total.add(0)
    total.send(1)
    gather.advance(0, 0)
    gather.start(1)
    total.add(1)
    total.send(2)
    gather.advance(0, 1)
    gather.advance(1, 0)
    gather.start(2)
    total.add(2)
    total.send(3)
    total.add(3)
    layer.norm_one(x, gains, 0)
    gather.advance(0, 2)
    gather.advance(1, 1)
    gather.advance(2, 0)
    gather.finish(0)
    layer.unpack(shards[0], perm)
    gather.advance(2, 1)

    @pl.when(me.stream == 1)
    def _():
        to_clean.wait_recv()

    layer.norm_one(x_clean, gains, SEQ)
    layer.project(cos, sin)
    gather.advance(1, 2)

    def forward(pair, carry):
        layer.attend(pair)

        @pl.when(pair == 3)
        def _():
            gather.advance(2, 2)

        return carry

    lax.fori_loop(0, PAIRS, forward, 0)
    layer.mix(x, gains)
    for s in range(3):
        if s > 0:
            gather.finish(s)
        gather.drain(s)
    total.drain()
    up, down = shards[1].reshape(6, FF, 128), shards[2].reshape(6, FF, 128)

    def feed(j, carry):
        layer.feed(up, down, dy, j)
        return carry

    lax.fori_loop(0, FF // 256, feed, 0)
    reduce.begin(2)
    reduce.begin(1)
    d_gains[...] = jnp.zeros((8, D), f32)
    layer.back_two(dy, gains, outputs, d_gains)
    layer.back_mix()
    reduce.enter(2)
    reduce.enter(1)

    def backward(pair, carry):
        layer.back_attend(pair, cos, sin)
        for at, s, k in ((1, 2, 0), (2, 1, 0), (3, 2, 1), (4, 1, 1), (4, 2, 2), (5, 1, 2)):

            @pl.when(pair == at)
            def _():
                reduce.advance(s, k)

        return carry

    lax.fori_loop(0, PAIRS, backward, 0)
    layer.back_project(gains, x, x_clean, layer.x2, given, d_gains)

    @pl.when(me.stream == 1)
    def _():
        from_noisy.start()

    total_back.held[0] = d_gains[...]
    total_back.send(0)
    layer.grad_project()
    layer.pack(shards[0], perm)
    reduce.begin(0)
    total_back.add(0)
    total_back.send(1)
    reduce.enter(0)
    total_back.add(1)
    total_back.send(2)
    reduce.finish(2, grads)
    reduce.finish(1, grads)
    reduce.advance(0, 0)
    total_back.add(2)
    total_back.send(3)
    reduce.advance(0, 1)
    total_back.add(3)
    d_gains_all[...] = total_back.held[4]

    @pl.when(me.stream == 0)
    def _():
        from_noisy.wait_recv()
        both = given[...].astype(f32) + back[...].astype(f32)
        grads_in[...] = (layer.x2[...] + both).astype(bf16)

    @pl.when(me.stream == 1)
    def _():
        grads_in[...] = layer.x2[...].astype(bf16)

    reduce.advance(0, 2)
    reduce.finish(0, grads)

    @pl.when(me.stream == 0)
    def _():
        to_clean.wait_send()

    @pl.when(me.stream == 1)
    def _():
        from_noisy.wait_send()

    total_back.drain()
    for s in range(3):
        reduce.drain(s)


def adam(weight, grad, first, second, rate):
    first_new = BETA_ONE * first + (1.0 - BETA_ONE) * grad
    second_new = BETA_TWO * second + (1.0 - BETA_TWO) * grad * grad
    fix_one = 1.0 - BETA_ONE**STEP
    fix_two = 1.0 - BETA_TWO**STEP
    update = first_new / fix_one / (jnp.sqrt(second_new / fix_two) + ADAM_EPS)
    return (weight - rate * (update + WEIGHT_DECAY * weight), first_new, second_new)


ROWS = ((0, 18), (18, 24), (24, 48), (48, 72))


def adam_kernel(grads, d_gains, *refs):
    weights, firsts, seconds, outs = refs[:5], refs[5:10], refs[10:15], refs[15:]
    for n in range(5):
        grad = d_gains[...] if n == 4 else grads[ROWS[n][0] : ROWS[n][1]]
        new = adam(weights[n][...], grad, firsts[n][...], seconds[n][...], RATES[n])
        for part in range(3):
            outs[5 * part + n][...] = new[part]
        if n < 4:
            outs[15 + n][...] = new[0].astype(bf16)


def call(kernel, out_shape, operands, scratch=(), collective=None, smem=0):
    spec = pl.BlockSpec(memory_space=VMEM)
    return pl.pallas_call(
        kernel,
        out_shape=out_shape,
        in_specs=[pl.BlockSpec(memory_space=pltpu.SMEM)] * smem + [spec] * (len(operands) - smem),
        out_specs=jax.tree.map(lambda _: spec, out_shape),
        scratch_shapes=list(scratch),
        compiler_params=pltpu.CompilerParams(
            collective_id=collective,
            has_side_effects=collective is not None,
            vmem_limit_bytes=60 << 20,
        ),
    )(*operands)


def permutation():
    perm = np.zeros((192, 192), np.float32)
    for row in range(192):
        if row < 144:
            perm[row, 24 * (row // 18) + row % 18] = 1
        else:
            perm[row, 24 * ((row - 144) // 6) + 18 + (row - 144) % 6] = 1
    return perm


def rotary_tables():
    frequency = 10000.0 ** (-2.0 * np.arange(HD // 2) / HD)
    angles = (np.arange(SEQ)[:, None] * frequency[None, :]).astype(np.float32)
    cos, sin = np.cos(angles), np.sin(angles)
    return np.tile(cos, (1, 4)), np.concatenate([-sin, sin, -sin, sin], axis=1)


def local(
    inputs, cotangent, lengths, block_sizes, w_qkv, w_out, w_up, w_down, gains,
    first_qkv, first_out, first_up, first_down, first_gains,
    second_qkv, second_out, second_up, second_down, second_gains,
):
    shape = jax.ShapeDtypeStruct
    masters = (w_qkv.T, w_out, w_up.T, w_down, gains)
    firsts = (first_qkv.T, first_out, first_up.T, first_down, first_gains)
    seconds = (second_qkv.T, second_out, second_up.T, second_down, second_gains)
    place = 6 * lax.axis_index(AXES)
    packed = jnp.concatenate(masters[:4], axis=0)
    gains_low = gains.astype(bf16).astype(f32)
    placed = lax.dynamic_update_slice(jnp.zeros((8, D), f32), gains_low, (0, place))
    x, dy = inputs[0, 0], cotangent[0, 0]
    rows16, small = shape((SEQ, D), bf16), shape((8, D), f32)
    cos, sin = rotary_tables()
    groups = (Gather, Total, Layer, Reduce, Total, Rest)
    outputs, input_grads, grads, d_gains = call(
        step_kernel,
        (rows16, rows16, shape((72, D), f32), small),
        (lengths, block_sizes, packed, placed, x, dy, jnp.asarray(permutation(), bf16),
         jnp.asarray(cos, f32), jnp.asarray(sin, f32)),
        [item for group in groups for item in group.scratch],
        collective=0,
        smem=2,
    )
    d_gains = lax.dynamic_slice(d_gains, (0, place), (2, 6))
    like = [shape(w.shape, f32) for w in masters]
    new = call(
        adam_kernel,
        like * 3 + [shape(w.shape, bf16) for w in masters[:4]],
        (grads, d_gains, *masters, *firsts, *seconds),
    )
    turned = [v.T if n % 5 in (0, 2) else v for n, v in enumerate(new)]
    return (outputs[None, None], input_grads[None, None], *turned)


def solution(mesh):
    mesh = Mesh(mesh.devices.reshape(2, 4, 2, 4, 2), AXES)
    data, one = P("xl", AXES[1:], None, None), P(AXES[1:])
    cols, rows = P(None, AXES), P(AXES, None)
    state = (cols, rows, cols, rows, cols)
    return jax.shard_map(
        local,
        mesh=mesh,
        in_specs=(data, data, one, one) + state * 3,
        out_specs=(data, data) + state * 3 + state[:4],
        check_vma=False,
    )
```

```python
import functools

import jax
import jax.numpy as jnp
import numpy as np
from jax import lax
from jax.experimental import pallas as pl
from jax.experimental.pallas import tpu as pltpu
from jax.sharding import Mesh
from jax.sharding import PartitionSpec as P

D = 768
H = 12
HD = 64
FF = 3072
SEQ = 512
STEP = 7
TILE = 128
TILES = SEQ // TILE
PAIRS = H // 2
LANES = D // 128
NORM_EPS = 1e-05
BETA_ONE = 0.5
BETA_TWO = 0.5
ADAM_EPS = 1e-08
WEIGHT_DECAY = 0.01
GAIN_RATE = 0.2
RATES = (D ** (-0.5), H ** (-0.5), D ** (-0.5), FF ** (-0.5), GAIN_RATE)
AXES = ("xl", "y", "xh", "z", "core")
EVEN = ((0, 1, 2), (1, 2, 0), (2, 0, 1))
GATHERED = (EVEN, ((0, 2, 1), (0, 1, 2), (0, 2, 1)), ((0, 2, 1), (0, 1, 2), (0, 1, 2)))
SHARDS = (6, 4, 4, 4, 48, 128)
MASKED = -1e30

f32 = jnp.float32
bf16 = jnp.bfloat16
VMEM = pltpu.VMEM
DMA = pltpu.SemaphoreType.DMA
MESH = pl.DeviceIdType.MESH


def remote(src, dst, send, recv, device):
    return pltpu.make_async_remote_copy(
        src_ref=src,
        dst_ref=dst,
        send_sem=send,
        recv_sem=recv,
        device_id=device,
        device_id_type=MESH,
    )


def wait_sent(ref, sem, device):
    remote(ref, ref, sem, sem, device).wait_send()


def wait_came(ref, sem, device):
    remote(ref, ref, sem, sem, device).wait_recv()


def dot_nn(a, b):
    return jnp.dot(a, b, preferred_element_type=f32)


def dot_nt(a, b):
    return lax.dot_general(a, b, (((1,), (1,)), ((), ())), preferred_element_type=f32)


def dot_tn(a, b):
    return lax.dot_general(a, b, (((0,), (0,)), ((), ())), preferred_element_type=f32)


def aligned(start, size, step):
    return pl.ds(pl.multiple_of(start, step), size)


class Place:
    def __init__(self):
        self.stream = lax.axis_index("xl")
        self.core = lax.axis_index("core")
        self.chip = (
            lax.axis_index("xh") * 2 + self.stream,
            lax.axis_index("y"),
            lax.axis_index("z"),
        )

    def device(self, chip, core):
        return (lax.rem(chip[0], 2), chip[1], lax.div(chip[0], 2), chip[2], core)

    def along(self, dim, offset):
        chip = list(self.chip)
        chip[dim] = lax.rem(chip[dim] + offset, 4)
        return self.device(chip, self.core)

    def sibling(self):
        return self.device(self.chip, 1 - self.core)

    def partner(self):
        chip = (self.chip[0] + 1 - 2 * self.stream, self.chip[1], self.chip[2])
        return self.device(chip, self.core)

    def region(self, whole, fixed=None):
        out = []
        for dim in range(3):
            if fixed and dim in fixed:
                out.append(fixed[dim])
            elif dim in whole:
                out.append(slice(None))
            else:
                out.append(self.chip[dim])
        return tuple(out)

    def greet(self):
        barrier = pltpu.get_barrier_semaphore()
        others = [self.sibling()]
        others += [self.along(dim, offset) for dim in range(3) for offset in (1, 2, 3)]
        for other in others:
            pl.semaphore_signal(barrier, inc=1, device_id=other, device_id_type=MESH)
        pl.semaphore_wait(barrier, len(others))


class Gather:
    scratch = [
        VMEM((72, D), f32),
        VMEM((72, 384), f32),
        VMEM((3, 48, 384), f32),
        DMA((3, 3)),
        DMA((3, 3, 3)),
        DMA((3, 3)),
        DMA((3,)),
        DMA((3, 3)),
        DMA((3,)),
        DMA((3,)),
        DMA((2,)),
    ]

    def __init__(self, me, shards, scratch):
        self.me, self.shards = me, shards
        self.packed, self.half, self.block, self.send_sem, self.recv_sem = scratch[:5]
        self.last_recv, self.relay_send, self.relay_recv = scratch[5:8]
        self.side_send, self.side_recv, self.swap_sem = scratch[8:]

    def swap(self):
        me = self.me
        return remote(
            self.packed.at[:, aligned(384 * (1 - me.core), 384, 128)],
            self.half,
            self.swap_sem.at[0],
            self.swap_sem.at[1],
            me.sibling(),
        )

    def assemble(self):
        core = self.me.core
        own = self.packed[:, aligned(384 * core, 384, 128)]
        for s in range(3):
            self.block[s, aligned(24 * core, 24, 8)] = own[24 * s : 24 * s + 24]
            self.block[s, aligned(24 * (1 - core), 24, 8)] = self.half[24 * s : 24 * s + 24]
        for s in range(3):
            value = self.block[s].astype(bf16)
            for p in range(3):
                self.shards[s][(3 * core + p,) + self.me.chip] = value[:, 128 * p : 128 * p + 128]

    def here(self, s, p, whole, fixed=None):
        return self.shards[s].at[(3 * self.me.core + p,) + self.me.region(whole, fixed)]

    def copies(self, s, p, k):
        dim, whole = GATHERED[s][p][k], GATHERED[s][p][:k]
        block = self.here(s, p, whole)
        return [
            remote(
                block,
                block,
                self.send_sem.at[s, k],
                self.last_recv.at[p, offset - 1] if s == 0 and k == 2 else self.recv_sem.at[s, p, k],
                self.me.along(dim, offset),
            )
            for offset in ((1, 3) if s > 0 and k == 2 else (1, 3, 2))
        ]

    def came(self, s, p, k):
        dim, whole = GATHERED[s][p][k], GATHERED[s][p][:k]
        count = 2 if s > 0 and k == 2 else 3
        blocks = self.here(s, p, whole, {dim: pl.ds(0, count)})
        wait_came(blocks, self.recv_sem.at[s, p, k], self.me.sibling())

    def relays(self, s, p):
        me, (dim, whole) = self.me, (GATHERED[s][p][2], GATHERED[s][p][:2])
        out = []
        for n, (source, target) in enumerate(((3, 1), (1, 3))):
            fixed = {dim: lax.rem(me.chip[dim] + source, 4), 0: pl.ds(2 * n, 2)}
            block = self.here(s, p, whole, fixed)
            sems = self.relay_send.at[s], self.relay_recv.at[s, p]
            out.append(remote(block, block, *sems, me.along(dim, target)))
        return out

    def across(self, s, p, part=0):
        me, (dim, whole) = self.me, (GATHERED[s][p][2], GATHERED[s][p][:2])
        if s > 0:
            block = self.here(s, p, (0, 1, 2))
        else:
            block = self.here(s, p, whole, {dim: lax.rem(me.chip[dim] + 4 - part, 4)})
        return remote(block, block, self.side_send.at[s], self.side_recv.at[s], me.sibling())

    def start(self, s):
        for p in range(3):
            for copy in self.copies(s, p, 0):
                copy.start()

    def advance(self, s, k):
        for p in range(3):
            self.came(s, p, k)
            for copy in self.copies(s, p, k + 1):
                copy.start()
            if s == 0 and k == 1:
                self.across(s, p, 0).start()

    def hand_over(self):
        copies = [self.copies(0, p, 2) for p in range(3)]
        for n, part in enumerate((1, 3, 2)):
            for p in range(3):
                copies[p][n].wait_recv()
                self.across(0, p, part).start()

    def relay(self, s):
        for p in range(3):
            self.came(s, p, 2)
            for onward in self.relays(s, p):
                onward.start()

    def close(self, s):
        for p in range(3):
            block = self.here(s, p, GATHERED[s][p][:2])
            wait_came(block, self.relay_recv.at[s, p], self.me.sibling())
            self.across(s, p).start()

    def finish(self, s):
        wait_came(self.shards[s].at[pl.ds(0, 3)], self.side_recv.at[s], self.me.sibling())

    def drain(self, s):
        shards, other, three = self.shards[s], self.me.sibling(), pl.ds(0, 3)
        wait_sent(shards.at[three, 0, 0, three], self.send_sem.at[s, 0], other)
        wait_sent(shards.at[three, 0, three], self.send_sem.at[s, 1], other)
        count = pl.ds(0, 2) if s > 0 else three
        wait_sent(shards.at[three, count], self.send_sem.at[s, 2], other)
        if s > 0:
            wait_sent(shards.at[three, 0], self.relay_send.at[s], other)
        wait_sent(shards.at[three], self.side_send.at[s], other)


class Total:
    scratch = [VMEM((5, 8, D), f32), VMEM((4, 3, 8, D), f32), DMA((4,)), DMA((4,))]

    def __init__(self, me, scratch):
        self.me = me
        self.held, self.slots, self.send_sem, self.recv_sem = scratch

    def copies(self, k):
        me = self.me
        devices = [me.sibling()] if k == 3 else [me.along(k, offset) for offset in (1, 2, 3)]
        return [
            remote(
                self.held.at[k],
                self.slots.at[k, n],
                self.send_sem.at[k],
                self.recv_sem.at[k],
                device,
            )
            for n, device in enumerate(devices)
        ]

    def send(self, k):
        for copy in self.copies(k):
            copy.start()

    def came(self, k):
        return self.slots.at[3, pl.ds(0, 1)] if k == 3 else self.slots.at[k]

    def add(self, k):
        wait_came(self.came(k), self.recv_sem.at[k], self.me.sibling())
        total = self.held[k]
        for n in range(1 if k == 3 else 3):
            total = total + self.slots[k, n]
        self.held[k + 1] = total

    def drain(self):
        for k in range(4):
            wait_sent(self.came(k), self.send_sem.at[k], self.me.sibling())


class Reduce:
    scratch = [
        VMEM((3, 4, 4, 4, 48, 128), bf16),
        VMEM((3, 4, 4, 4, 48, 128), bf16),
        VMEM((3, 4, 4, 4, 48, 128), bf16),
        VMEM((3, 3, 3, 4, 4, 48, 128), bf16),
        VMEM((3, 3, 3, 4, 48, 128), bf16),
        VMEM((3, 3, 3, 48, 128), bf16),
        VMEM((3, 3, 48, 128), f32),
        VMEM((3, 3, 24, 128), f32),
        DMA((3,)),
        DMA((3, 4)),
        DMA((3, 3)),
        DMA((3, 3, 3)),
        DMA((3, 2)),
    ]

    def __init__(self, me, shards, scratch):
        self.me, self.shards = me, shards
        self.side, self.slots = scratch[:3], scratch[3:6]
        self.summed, self.crossed = scratch[6:8]
        self.side_send, self.side_recv, self.send_sem, self.recv_sem = scratch[8:12]
        self.last_sem = scratch[12]

    def slab(self, turn):
        return lax.rem(self.me.chip[0] + 1 + turn, 4)

    def across(self, s, turn):
        me, x = self.me, self.slab(turn)
        return remote(
            self.shards[s].at[pl.ds(3 * (1 - me.core), 3), x],
            self.side[s].at[:, x],
            self.side_send.at[s],
            self.side_recv.at[s, turn],
            me.sibling(),
        )

    def send_first(self, s, p, turn):
        me, x, dim = self.me, self.slab(turn), EVEN[p][2]
        own, slots = self.shards[s].at[3 * me.core + p, x], self.slots[0].at[s, p]
        sems = self.send_sem.at[s, 0], self.recv_sem.at[s, p, 0]
        if dim == 0:

            @pl.when(turn < 3)
            def _():
                remote(own, slots.at[turn], *sems, me.along(0, turn + 1)).start()

            return
        for offset in (2, 1, 3):
            there = lax.rem(me.chip[dim] + offset, 4)
            part = own.at[there] if dim == 1 else own.at[:, there]
            remote(part, slots.at[offset - 1, x], *sems, me.along(dim, offset)).start()

    def send(self, s, p, k):
        me, dim, whole = self.me, EVEN[p][2 - k], EVEN[p][: 2 - k]
        for offset in (2, 1, 3):
            there = {dim: lax.rem(me.chip[dim] + offset, 4)}
            remote(
                self.shards[s].at[(3 * me.core + p,) + me.region(whole, there)],
                self.slots[k].at[s, p, offset - 1],
                self.send_sem.at[s, k],
                self.recv_sem.at[s, p, k],
                me.along(dim, offset),
            ).start()

    def begin(self, s, turn):
        self.across(s, turn).start()

    def enter(self, s, turn):
        self.across(s, turn).wait_recv()
        shards, side, x = self.shards[s], self.side[s], self.slab(turn)
        for p in range(3):
            t = 3 * self.me.core + p

            def step(y, carry):
                total = shards[t, x, y].astype(f32) + side[p, x, y].astype(f32)
                shards[t, x, y] = total.astype(bf16)
                return carry

            lax.fori_loop(0, 4, step, 0)
            self.send_first(s, p, turn)

    def advance(self, s, k):
        me, shards, slots = self.me, self.shards[s], self.slots[k]
        for p in range(3):
            wait_came(slots.at[s, p], self.recv_sem.at[s, p, k], me.sibling())
            t, whole = 3 * me.core + p, sorted(EVEN[p][: 2 - k])
            if k == 2:
                total = shards[(t,) + me.chip].astype(f32)
                for n in range(3):
                    total = total + slots[s, p, n].astype(f32)
                self.summed[s, p] = total
                continue

            def step(i, carry):
                inner = (lax.div(i, 4), lax.rem(i, 4)) if k == 0 else (i,)
                chip = me.region((), dict(zip(whole, inner)))
                total = shards[(t,) + chip].astype(f32)
                for n in range(3):
                    total = total + slots[(s, p, n) + inner].astype(f32)
                shards[(t,) + chip] = total.astype(bf16)
                return carry

            lax.fori_loop(0, 16 if k == 0 else 4, step, 0)
            self.send(s, p, k + 1)
        if k == 2:
            self.last(s).start()

    def last(self, s):
        me = self.me
        return remote(
            self.summed.at[s, :, aligned(24 * (1 - me.core), 24, 8)],
            self.crossed.at[s],
            self.last_sem.at[s, 0],
            self.last_sem.at[s, 1],
            me.sibling(),
        )

    def finish(self, s, out):
        core = self.me.core
        self.last(s).wait_recv()
        for p in range(3):
            rows = pl.ds(24 * s, 24)
            own = self.summed[s, p, aligned(24 * core, 24, 8)]
            out[rows, aligned(384 * core + 128 * p, 128, 128)] = own
            out[rows, aligned(384 * (1 - core) + 128 * p, 128, 128)] = self.crossed[s, p]

    def drain(self, s):
        self.last(s).wait_send()
        wait_sent(self.side[s], self.side_send.at[s], self.me.sibling())
        for k in range(3):
            wait_sent(self.slots[k].at[s], self.send_sem.at[s, k], self.me.sibling())


def normal_of(x):
    center = x - jnp.mean(x, axis=-1, keepdims=True)
    rstd = lax.rsqrt(jnp.mean(center * center, axis=-1, keepdims=True) + NORM_EPS)
    return center * rstd, rstd


def norm_back(d_h, gain, xhat, rstd):
    e = d_h * gain
    inner = jnp.mean(e, axis=-1, keepdims=True) + xhat * jnp.mean(
        e * xhat, axis=-1, keepdims=True
    )
    return (e - inner) * rstd


def lanes_of(ref, *index):
    return jnp.concatenate([ref[(t,) + index] for t in range(ref.shape[0])], axis=-1)


def swapped(v):
    lane = lax.broadcasted_iota(jnp.int32, v.shape, 1)
    return jnp.where((lane & 63) < 32, pltpu.roll(v, 96, 1), pltpu.roll(v, 32, 1))


def first_head(shape):
    return lax.broadcasted_iota(jnp.int32, shape, 1) < HD


def split_heads(v):
    own, zero = first_head(v.shape), jnp.zeros_like(v)
    return jnp.concatenate([jnp.where(own, v, zero), jnp.where(own, zero, v)], axis=0)


def join_heads(v):
    half = v.shape[0] // 2
    return jnp.where(first_head((half, v.shape[1])), v[:half], v[half:])


class Layer:
    scratch = [
        VMEM((3 * D, D), bf16),
        VMEM((D, D), bf16),
        VMEM((2 * SEQ, D), bf16),
        VMEM((PAIRS, SEQ, 128), bf16),
        VMEM((2 * PAIRS, 2 * SEQ, 128), bf16),
        VMEM((PAIRS, SEQ, 128), bf16),
        VMEM((SEQ, D), f32),
        VMEM((SEQ, D), bf16),
        VMEM((SEQ, D), f32),
        VMEM((SEQ, D), f32),
        VMEM((PAIRS, SEQ, 128), bf16),
        VMEM((4, TILE, 5 * TILE), f32),
    ] + [VMEM((PAIRS, 2 * TILE, (i + 2) * TILE), bf16) for i in range(TILES)]

    def __init__(self, scratch):
        self.qkv, self.out, self.h1, self.q, self.kv, self.att, self.x2, self.h2 = scratch[:8]
        self.sum_a, self.sum_b, self.d_att, self.mask = scratch[8:12]
        self.probs = scratch[12:16]
        self.d_branch = self.h2

    def line(self, x, y):
        row = (lax.rem(x, 2) * 4 + y) * 2 + lax.div(x, 2)
        return aligned(144 * row, 144, 16), aligned(48 * row, 48, 16)

    def unpack(self, shards, perm):
        def step(x, carry):
            for y in range(4):
                tiles = [shards[t, x, y].reshape(192, 128) for t in range(6)]
                block = dot_nn(perm[...], jnp.concatenate(tiles, axis=1)).astype(bf16)
                rows_qkv, rows_out = self.line(x, y)
                self.qkv[rows_qkv] = block[:144]
                self.out[rows_out] = block[144:]
            return carry

        lax.fori_loop(0, 4, step, 0)

    def pack(self, grads, shards, perm, x):
        for y in range(4):
            rows_qkv, rows_out = self.line(x, y)
            tiles = [grads[t // 3][t % 3, rows_qkv] for t in range(6)]
            block = jnp.concatenate(tiles, axis=1)
            block = jnp.concatenate([block, self.out[rows_out]], axis=0)
            block = dot_tn(perm[...], block).astype(bf16)
            for t in range(6):
                shards[t, x, y] = block[:, 128 * t : 128 * t + 128].reshape(4, 48, 128)

    def masks(self, length, size):
        row = lax.broadcasted_iota(jnp.int32, (TILE, TILE), 0)
        col = lax.broadcasted_iota(jnp.int32, (TILE, TILE), 1)
        shift = jnp.where(size == 4, 2, jnp.where(size == 8, 3, 4))
        n_row = lax.shift_right_logical(row, jnp.full_like(row, shift))
        n_col = lax.shift_right_logical(col, jnp.full_like(col, shift))
        for i in range(TILES):
            for j in range(i + 2):
                key = min(j, i) * TILE + col
                seen = key < length
                if j == i:
                    seen = seen & (n_row > n_col)
                if j == i + 1:
                    seen = seen & (n_row == n_col)
                self.mask[i, :, j * TILE : (j + 1) * TILE] = jnp.where(seen, 0.0, MASKED)

    def norm_one(self, x, gains, first_row):
        gain = gains[0:1, :]

        def step(i, carry):
            rows = aligned(i * TILE, TILE, TILE)
            xhat, _ = normal_of(x[rows].astype(f32))
            self.h1[aligned(first_row + i * TILE, TILE, TILE)] = (xhat * gain).astype(bf16)
            return carry

        lax.fori_loop(0, TILES, step, 0)

    def project(self, cos, sin, clean):
        def turned(v, scale):
            return (v * (cos[...] * scale) + swapped(v) * (sin[...] * scale)).astype(bf16)

        rows = slice(SEQ, 2 * SEQ) if clean else slice(0, SEQ)
        for j in range(3 if clean else 0, 9):
            v = dot_nt(self.h1[rows], self.qkv[256 * j : 256 * j + 256])
            for n in range(2):
                part = v[:, 128 * n : 128 * n + 128]
                if j < 3:
                    self.q[2 * j + n] = turned(part, HD ** (-0.5))
                elif j < 6:
                    self.kv[2 * j - 6 + n, rows] = turned(part, 1.0)
                else:
                    self.kv[2 * j - 6 + n, rows] = part.astype(bf16)

    def keys(self, t, i):
        clean = self.kv[t, SEQ : SEQ + (i + 1) * TILE]
        return jnp.concatenate([clean, self.kv[t, i * TILE : (i + 1) * TILE]], axis=0)

    def attend(self, pair):
        for i in range(TILES):
            rows, width = pl.ds(i * TILE, TILE), (i + 2) * TILE
            queries = split_heads(self.q[pair, rows])
            scores = dot_nt(queries, self.keys(pair, i)).reshape(2, TILE, width)
            scores = (scores + self.mask[i, :, :width][None]).reshape(2 * TILE, width)
            raised = jnp.exp(scores - jnp.max(scores, axis=-1, keepdims=True))
            probs = raised * (1.0 / jnp.sum(raised, axis=-1, keepdims=True))
            probs = probs.astype(bf16)
            self.probs[i][pair] = probs
            mixed = dot_nn(probs, self.keys(PAIRS + pair, i))
            self.att[pair, rows] = join_heads(mixed).astype(bf16)

    def mix(self, x, gains):
        for j in range(3):
            cols = slice(256 * j, 256 * j + 256)
            branch = dot_nn(lanes_of(self.att), self.out[:, cols])
            self.x2[:, cols] = x[:, cols].astype(f32) + branch
        gain = gains[1:2, :]

        def step(i, carry):
            rows = aligned(i * TILE, TILE, TILE)
            xhat, _ = normal_of(self.x2[rows])
            self.h2[rows] = (xhat * gain).astype(bf16)
            self.sum_a[rows] = jnp.zeros((TILE, D), f32)
            self.sum_b[rows] = jnp.zeros((TILE, D), f32)
            return carry

        lax.fori_loop(0, TILES, step, 0)

    def feed(self, up, down, dy, j):
        rows = aligned(256 * j, 256, 256)
        w_up, w_down = lanes_of(up, rows), lanes_of(down, rows)
        u = dot_nt(self.h2[...], w_up)
        d_act = dot_nt(dy[...], w_down)
        c = (2.0 / np.pi) ** 0.5
        squared = u * u
        t = jnp.tanh(c * u * (1.0 + 0.044715 * squared))
        half = 0.5 * (1.0 + t)
        act = (u * half).astype(bf16)
        slope = half + 0.5 * u * (1.0 - t * t) * (c + (3 * 0.044715 * c) * squared)
        d_up = (slope * d_act).astype(bf16)
        self.sum_a[...] += dot_nn(act, w_down)
        self.sum_b[...] += dot_nn(d_up, w_up)
        g_up = dot_tn(d_up, self.h2[...]).astype(bf16)
        g_down = dot_tn(act, dy[...]).astype(bf16)
        for t in range(LANES):
            up[t, rows] = g_up[:, 128 * t : 128 * t + 128]
            down[t, rows] = g_down[:, 128 * t : 128 * t + 128]

    def back_two(self, dy, gains, outputs, d_gains):
        gain = gains[1:2, :]

        def step(i, carry):
            rows = aligned(i * TILE, TILE, TILE)
            x2 = self.x2[rows]
            outputs[rows] = (x2 + self.sum_a[rows]).astype(bf16)
            xhat, rstd = normal_of(x2)
            d_h = self.sum_b[rows]
            d_x2 = dy[rows].astype(f32) + norm_back(d_h, gain, xhat, rstd)
            self.sum_b[rows] = d_x2
            self.d_branch[rows] = d_x2.astype(bf16)
            return carry + jnp.sum(d_h * xhat, axis=0, keepdims=True)

        d_gains[1:2, :] = lax.fori_loop(0, TILES, step, jnp.zeros((1, D), f32))

    def back_mix(self):
        for j in range(3):
            rows = slice(256 * j, 256 * j + 256)
            d_att = dot_nt(self.d_branch[...], self.out[rows]).astype(bf16)
            self.d_att[2 * j] = d_att[:, :128]
            self.d_att[2 * j + 1] = d_att[:, 128:]
        for j in range(3):
            att = jnp.concatenate([self.att[2 * j], self.att[2 * j + 1]], axis=1)
            self.out[256 * j : 256 * j + 256] = dot_tn(att, self.d_branch[...]).astype(bf16)

    def back_attend(self, pair, cos, sin):
        d_keys, d_values, d_query = [None] * 2 * TILES, [None] * 2 * TILES, [None] * TILES
        for i in reversed(range(TILES)):
            rows = pl.ds(i * TILE, TILE)
            queries = split_heads(self.q[pair, rows])
            d_att = split_heads(self.d_att[pair, rows])
            low = self.probs[i][pair]
            probs = low.astype(f32)
            d_probs = dot_nt(d_att, self.keys(PAIRS + pair, i))
            delta = jnp.sum(probs * d_probs, axis=-1, keepdims=True)
            d_scores = (probs * (d_probs - delta)).astype(bf16)
            d_query[i] = join_heads(dot_nn(d_scores, self.keys(pair, i))) * HD ** (-0.5)
            d_k = dot_tn(d_scores, queries)
            d_v = dot_tn(low, d_att)
            for j in range(i + 2):
                to = TILES + i if j == i + 1 else j
                part = slice(j * TILE, (j + 1) * TILE)
                d_keys[to] = d_k[part] if d_keys[to] is None else d_keys[to] + d_k[part]
                d_values[to] = d_v[part] if d_values[to] is None else d_values[to] + d_v[part]

        def back(v, rows):
            return (v * cos[rows] - swapped(v) * sin[rows]).astype(bf16)

        for i in range(TILES):
            rows = slice(i * TILE, (i + 1) * TILE)
            clean = slice(SEQ + i * TILE, SEQ + (i + 1) * TILE)
            self.q[pair, rows] = back(d_query[i], rows)
            self.kv[pair, clean] = back(d_keys[i], rows)
            self.kv[pair, rows] = back(d_keys[TILES + i], rows)
            self.kv[PAIRS + pair, clean] = d_values[i].astype(bf16)
            self.kv[PAIRS + pair, rows] = d_values[TILES + i].astype(bf16)

    def back_clean(self, gains, x_clean, grads_clean, d_gains):
        gain = gains[0:1, :]

        def step(i, carry):
            clean = aligned(SEQ + i * TILE, TILE, TILE)
            own = aligned(i * TILE, TILE, TILE)
            d_h = dot_nn(lanes_of(self.kv, clean), self.qkv[D:])
            xhat, rstd = normal_of(x_clean[own].astype(f32))
            grads_clean[own] = norm_back(d_h, gain, xhat, rstd).astype(bf16)
            return carry + jnp.sum(d_h * xhat, axis=0, keepdims=True)

        d_gains[0:1, :] = lax.fori_loop(0, TILES, step, jnp.zeros((1, D), f32))

    def back_own(self, weights, gains, x, grads, d_gains):
        gain = gains[0:1, :]

        def step(i, carry):
            own = aligned(i * TILE, TILE, TILE)
            d_proj = jnp.concatenate([lanes_of(self.q, own), lanes_of(self.kv, own)], axis=1)
            d_h = dot_nn(d_proj, weights[...])
            xhat, rstd = normal_of(x[own].astype(f32))
            grads[own] = self.sum_b[own] + norm_back(d_h, gain, xhat, rstd)
            return carry + jnp.sum(d_h * xhat, axis=0, keepdims=True)

        d_gains[0:1, :] += lax.fori_loop(0, TILES, step, jnp.zeros((1, D), f32))

    def grad_project(self, grads):
        def put(rows, value):
            for t in range(6):
                grads[t // 3][t % 3, rows] = value[:, 128 * t : 128 * t + 128]

        for j in range(3):
            d_q = jnp.concatenate([self.q[2 * j], self.q[2 * j + 1]], axis=1)
            put(pl.ds(256 * j, 256), dot_tn(d_q, self.h1[:SEQ]).astype(bf16))
        for j in range(6):
            d_kv = jnp.concatenate([self.kv[2 * j], self.kv[2 * j + 1]], axis=1)
            put(pl.ds(D + 256 * j, 256), dot_tn(d_kv, self.h1[...]).astype(bf16))


class Rest:
    scratch = [
        VMEM(SHARDS, bf16),
        VMEM(SHARDS, bf16),
        VMEM(SHARDS, bf16),
        VMEM((SEQ, D), bf16),
        VMEM((SEQ, D), bf16),
        VMEM((8, D), f32),
        DMA((2,)),
        DMA((2,)),
    ]


def split(refs, *groups):
    out, at = [], 0
    for group in groups:
        out.append(refs[at : at + len(group.scratch)])
        at += len(group.scratch)
    return out


CLEAN = ((0, 128), (128, 128), (256, 256))
NOISY = ((0, 192), (192, 128), (320, 96), (416, 96))


def pieces(src, dst, sems, device, cuts):
    out = []
    for n, (row, count) in enumerate(cuts):
        rows = pl.ds(row, count)
        out.append(remote(src.at[rows], dst.at[rows], sems.at[0], sems.at[1], device))
    return out


def step_kernel(
    lengths, sizes, w_qkv, w_out, w_up, w_down, gains_own, x, dy, perm, cos, sin,
    outputs, grads_in, grads, d_gains_all, *scratch
):
    gather_refs, total_refs, layer_refs, reduce_refs, back_refs, rest = split(
        scratch, Gather, Total, Layer, Reduce, Total, Rest
    )
    shards = rest[:3]
    x_clean, back, d_gains, clean_sem, back_sem = rest[3:]
    me = Place()
    gather = Gather(me, shards, gather_refs)
    total = Total(me, total_refs)
    total_back = Total(me, back_refs)
    layer = Layer(layer_refs)
    reduce = Reduce(me, shards, reduce_refs)
    gains, given = total.held.at[4], layer.h2
    to_clean = pieces(x, x_clean, clean_sem, me.partner(), CLEAN)
    from_noisy = pieces(given, back, back_sem, me.partner(), NOISY)

    def clean_sends(n):
        @pl.when(me.stream == 0)
        def _():
            to_clean[n].start()

    def noisy_sends(n):
        @pl.when(me.stream == 1)
        def _():
            from_noisy[n].start()

    packed = gather.packed
    packed[0:18] = w_qkv[...]
    packed[18:24] = w_out[...]
    packed[24:48] = w_up[...]
    packed[48:72] = w_down[...]
    total.held[0] = jnp.zeros((8, D), f32)
    total.held[0, 0:2, 0:6] = gains_own[...].astype(bf16).astype(f32)
    total.held[0] = pltpu.roll(total.held[0], 6 * lax.axis_index(AXES), 1)
    me.greet()
    gather.swap().start()
    total.send(0)
    layer.masks(lengths[0], sizes[0])

    @pl.when(me.stream == 0)
    def _():
        x_clean[...] = x[...]

    gather.swap().wait()
    gather.assemble()
    gather.start(0)
    clean_sends(0)
    total.add(0)
    total.send(1)
    gather.advance(0, 0)
    gather.start(1)
    gather.start(2)
    clean_sends(1)
    total.add(1)
    total.send(2)
    gather.advance(0, 1)
    clean_sends(2)
    total.add(2)
    total.send(3)
    gather.advance(1, 0)
    gather.advance(2, 0)
    total.add(3)
    layer.norm_one(x, gains, 0)
    gather.hand_over()
    gather.advance(1, 1)
    gather.advance(2, 1)
    gather.finish(0)
    layer.unpack(shards[0], perm)
    layer.project(cos, sin, False)
    gather.relay(1)

    @pl.when(me.stream == 1)
    def _():
        wait_came(x_clean, clean_sem.at[1], me.partner())

    layer.norm_one(x_clean, gains, SEQ)
    layer.project(cos, sin, True)
    gather.relay(2)

    def forward(pair, carry):
        layer.attend(pair)
        for at, s in ((2, 1), (4, 2)):

            @pl.when(pair == at)
            def _():
                gather.close(s)

        return carry

    lax.fori_loop(0, PAIRS, forward, 0)
    layer.mix(x, gains)
    for s in range(3):
        if s > 0:
            gather.finish(s)
        gather.drain(s)
    total.drain()
    up, down = shards[1].reshape(6, FF, 128), shards[2].reshape(6, FF, 128)

    def feed(turn, carry):
        def chunk(j, carry):
            layer.feed(up, down, dy, 3 * reduce.slab(turn) + j)
            return carry

        lax.fori_loop(0, 3, chunk, 0)
        reduce.begin(1, turn)
        reduce.begin(2, turn)

        @pl.when(turn > 0)
        def _():
            reduce.enter(1, turn - 1)
            reduce.enter(2, turn - 1)

        return carry

    lax.fori_loop(0, 4, feed, 0)
    d_gains[...] = jnp.zeros((8, D), f32)
    layer.back_two(dy, gains, outputs, d_gains)
    reduce.enter(1, 3)
    reduce.enter(2, 3)
    layer.back_mix()

    def backward(pair, carry):
        layer.back_attend(pair, cos, sin)
        for at, s, k in ((1, 1, 0), (2, 2, 0), (3, 1, 1), (4, 2, 1), (5, 1, 2)):

            @pl.when(pair == at)
            def _():
                reduce.advance(s, k)

        return carry

    lax.fori_loop(0, PAIRS, backward, 0)
    layer.back_clean(gains, x_clean, given, d_gains)
    noisy_sends(0)
    grads_qkv = [side.reshape(3, FF, 128) for side in reduce.side[1:]]
    layer.grad_project(grads_qkv)
    reduce.advance(2, 2)
    for turn in range(4):
        layer.pack(grads_qkv, shards[0], perm, reduce.slab(turn))
        reduce.begin(0, turn)
        if turn > 0:
            reduce.enter(0, turn - 1)
    reduce.enter(0, 3)
    noisy_sends(1)
    layer.back_own(layer.qkv, gains, x, layer.x2, d_gains)
    total_back.held[0] = d_gains[...]
    total_back.send(0)
    reduce.finish(1, grads)
    reduce.finish(2, grads)
    reduce.advance(0, 0)
    noisy_sends(2)
    total_back.add(0)
    total_back.send(1)
    reduce.advance(0, 1)
    noisy_sends(3)
    total_back.add(1)
    total_back.send(2)
    reduce.advance(0, 2)
    total_back.add(2)
    total_back.send(3)

    @pl.when(me.stream == 0)
    def _():
        wait_came(back, back_sem.at[1], me.partner())
        both = given[...].astype(f32) + back[...].astype(f32)
        grads_in[...] = (layer.x2[...] + both).astype(bf16)

    @pl.when(me.stream == 1)
    def _():
        grads_in[...] = layer.x2[...].astype(bf16)

    reduce.finish(0, grads)
    total_back.add(3)
    d_gains_all[...] = total_back.held[4]

    @pl.when(me.stream == 0)
    def _():
        wait_sent(x_clean, clean_sem.at[0], me.partner())

    @pl.when(me.stream == 1)
    def _():
        wait_sent(back, back_sem.at[0], me.partner())

    total_back.drain()
    for s in range(3):
        reduce.drain(s)


def adam(weight, grad, first, second, rate):
    first_new = BETA_ONE * first + (1.0 - BETA_ONE) * grad
    second_new = BETA_TWO * second + (1.0 - BETA_TWO) * grad * grad
    fix_one = 1.0 - BETA_ONE**STEP
    fix_two = 1.0 - BETA_TWO**STEP
    update = first_new / fix_one / (jnp.sqrt(second_new / fix_two) + ADAM_EPS)
    return (weight - rate * (update + WEIGHT_DECAY * weight), first_new, second_new)


ROWS = ((0, 18), (18, 24), (24, 48), (48, 72))


def adam_kernel(grads, d_gains, outputs, grads_in, *refs):
    weights, firsts, seconds, outs = refs[:5], refs[5:10], refs[10:15], refs[15:]
    outs[19][...] = outputs[...]
    outs[20][...] = grads_in[...]
    turn = lax.rem(D - 6 * lax.axis_index(AXES), D)
    d_gains_own = pltpu.roll(d_gains[...], turn, 1)[0:2, 0:6]
    for n in range(5):
        grad = d_gains_own if n == 4 else grads[ROWS[n][0] : ROWS[n][1]]
        new = adam(weights[n][...], grad, firsts[n][...], seconds[n][...], RATES[n])
        for part in range(3):
            outs[5 * part + n][...] = new[part]
        if n < 4:
            outs[15 + n][...] = new[0].astype(bf16)


def call(kernel, out_shape, operands, scratch=(), collective=None, smem=0):
    spec, place = pl.BlockSpec(memory_space=VMEM), pl.BlockSpec(memory_space=pltpu.SMEM)
    return pl.pallas_call(
        kernel,
        out_shape=out_shape,
        in_specs=[place] * smem + [spec] * (len(operands) - smem),
        out_specs=[spec] * len(out_shape),
        scratch_shapes=list(scratch),
        compiler_params=pltpu.CompilerParams(
            collective_id=collective,
            has_side_effects=collective is not None,
            vmem_limit_bytes=61 << 20,
        ),
    )(*operands)


def permutation():
    perm = np.zeros((192, 192), np.float32)
    for row in range(192):
        if row < 144:
            perm[row, 24 * (row // 18) + row % 18] = 1
        else:
            perm[row, 24 * ((row - 144) // 6) + 18 + (row - 144) % 6] = 1
    return perm


def rotary_tables():
    frequency = 10000.0 ** (-2.0 * np.arange(HD // 2) / HD)
    angles = (np.arange(SEQ)[:, None] * frequency[None, :]).astype(np.float32)
    cos, sin = np.cos(angles), np.sin(angles)
    return np.tile(cos, (1, 4)), np.concatenate([-sin, sin, -sin, sin], axis=1)


def local(
    inputs, cotangent, lengths, block_sizes, w_qkv, w_out, w_up, w_down, gains,
    first_qkv, first_out, first_up, first_down, first_gains,
    second_qkv, second_out, second_up, second_down, second_gains,
):
    shape = jax.ShapeDtypeStruct
    masters = (w_qkv.T, w_out, w_up.T, w_down, gains)
    firsts = (first_qkv.T, first_out, first_up.T, first_down, first_gains)
    seconds = (second_qkv.T, second_out, second_up.T, second_down, second_gains)
    x, dy = inputs[0, 0], cotangent[0, 0]
    rows16, small = shape((SEQ, D), bf16), shape((8, D), f32)
    cos, sin = rotary_tables()
    groups = (Gather, Total, Layer, Reduce, Total, Rest)
    outputs, input_grads, grads, d_gains = call(
        step_kernel,
        [rows16, rows16, shape((72, D), f32), small],
        (lengths, block_sizes, *masters, x, dy, jnp.asarray(permutation(), bf16),
         jnp.asarray(cos, f32), jnp.asarray(sin, f32)),
        [item for group in groups for item in group.scratch],
        collective=0,
        smem=2,
    )
    like = [shape(w.shape, f32) for w in masters]
    *new, outputs, input_grads = call(
        adam_kernel,
        like * 3 + [shape(w.shape, bf16) for w in masters[:4]] + [rows16] * 2,
        (grads, d_gains, outputs, input_grads, *masters, *firsts, *seconds),
    )
    turned = [v.T if n % 5 in (0, 2) else v for n, v in enumerate(new)]
    return (outputs[None, None], input_grads[None, None], *turned)


def solution(mesh):
    mesh = Mesh(mesh.devices.reshape(2, 4, 2, 4, 2), AXES)
    data, one = P("xl", AXES[1:], None, None), P(AXES[1:])
    cols, rows = P(None, AXES), P(AXES, None)
    state = (cols, rows, cols, rows, cols)
    return jax.shard_map(
        local,
        mesh=mesh,
        in_specs=(data, data, one, one) + state * 3,
        out_specs=(data, data) + state * 3 + state[:4],
        check_vma=False,
    )
```

```python
import functools

import jax
import jax.numpy as jnp
import numpy as np
from jax import lax
from jax.experimental import pallas as pl
from jax.experimental.pallas import tpu as pltpu
from jax.sharding import Mesh
from jax.sharding import PartitionSpec as P

D = 768
H = 12
HD = 64
FF = 3072
SEQ = 512
STEP = 7
TILE = 128
TILES = SEQ // TILE
PAIRS = H // 2
LANES = D // 128
NORM_EPS = 1e-05
BETA_ONE = 0.5
BETA_TWO = 0.5
ADAM_EPS = 1e-08
WEIGHT_DECAY = 0.01
GAIN_RATE = 0.2
RATES = (D ** (-0.5), H ** (-0.5), D ** (-0.5), FF ** (-0.5), GAIN_RATE)
AXES = ("xl", "y", "xh", "z", "core")
EVEN = ((0, 1, 2), (1, 2, 0), (2, 0, 1))
GATHERED = (EVEN, ((0, 2, 1), (0, 1, 2), (0, 2, 1)), EVEN)
SHARDS = (6, 4, 4, 4, 48, 128)
MASKED = -1e30
VALUES_OWN, VALUES_CLEAN = 0, 1536

f32 = jnp.float32
bf16 = jnp.bfloat16
VMEM = pltpu.VMEM
DMA = pltpu.SemaphoreType.DMA
MESH = pl.DeviceIdType.MESH


def remote(src, dst, send, recv, device):
    return pltpu.make_async_remote_copy(
        src_ref=src,
        dst_ref=dst,
        send_sem=send,
        recv_sem=recv,
        device_id=device,
        device_id_type=MESH,
    )


def wait_sent(ref, sem, device):
    remote(ref, ref, sem, sem, device).wait_send()


def wait_came(ref, sem, device):
    remote(ref, ref, sem, sem, device).wait_recv()


def dot_nn(a, b):
    return jnp.dot(a, b, preferred_element_type=f32)


def dot_nt(a, b):
    return lax.dot_general(a, b, (((1,), (1,)), ((), ())), preferred_element_type=f32)


def dot_tn(a, b):
    return lax.dot_general(a, b, (((0,), (0,)), ((), ())), preferred_element_type=f32)


def aligned(start, size, step):
    return pl.ds(pl.multiple_of(start, step), size)


class Place:
    def __init__(self):
        self.stream = lax.axis_index("xl")
        self.core = lax.axis_index("core")
        self.chip = (
            lax.axis_index("xh") * 2 + self.stream,
            lax.axis_index("y"),
            lax.axis_index("z"),
        )

    def device(self, chip, core):
        return (lax.rem(chip[0], 2), chip[1], lax.div(chip[0], 2), chip[2], core)

    def along(self, dim, offset):
        chip = list(self.chip)
        chip[dim] = lax.rem(chip[dim] + offset, 4)
        return self.device(chip, self.core)

    def sibling(self):
        return self.device(self.chip, 1 - self.core)

    def partner(self):
        chip = (self.chip[0] + 1 - 2 * self.stream, self.chip[1], self.chip[2])
        return self.device(chip, self.core)

    def region(self, whole, fixed=None):
        out = []
        for dim in range(3):
            if fixed and dim in fixed:
                out.append(fixed[dim])
            elif dim in whole:
                out.append(slice(None))
            else:
                out.append(self.chip[dim])
        return tuple(out)

    def greet(self):
        barrier = pltpu.get_barrier_semaphore()
        others = [self.sibling()]
        others += [self.along(dim, offset) for dim in range(3) for offset in (1, 2, 3)]
        for other in others:
            pl.semaphore_signal(barrier, inc=1, device_id=other, device_id_type=MESH)
        pl.semaphore_wait(barrier, len(others))


class Gather:
    scratch = [
        VMEM((72, D), f32),
        VMEM((72, 384), f32),
        VMEM((3, 48, 384), f32),
        DMA((3, 3)),
        DMA((3, 3, 3)),
        DMA((3, 3)),
        DMA((3,)),
        DMA((3, 3)),
        DMA((3,)),
        DMA((3,)),
        DMA((2,)),
    ]

    def __init__(self, me, shards, scratch):
        self.me, self.shards = me, shards
        self.packed, self.half, self.block, self.send_sem, self.recv_sem = scratch[:5]
        self.last_recv, self.relay_send, self.relay_recv = scratch[5:8]
        self.side_send, self.side_recv, self.swap_sem = scratch[8:]

    def swap(self):
        me = self.me
        return remote(
            self.packed.at[:, aligned(384 * (1 - me.core), 384, 128)],
            self.half,
            self.swap_sem.at[0],
            self.swap_sem.at[1],
            me.sibling(),
        )

    def assemble(self):
        core = self.me.core
        own = self.packed[:, aligned(384 * core, 384, 128)]
        for s in range(3):
            self.block[s, aligned(24 * core, 24, 8)] = own[24 * s : 24 * s + 24]
            self.block[s, aligned(24 * (1 - core), 24, 8)] = self.half[24 * s : 24 * s + 24]
        for s in range(3):
            value = self.block[s].astype(bf16)
            for p in range(3):
                self.shards[s][(3 * core + p,) + self.me.chip] = value[:, 128 * p : 128 * p + 128]

    def here(self, s, p, whole, fixed=None):
        return self.shards[s].at[(3 * self.me.core + p,) + self.me.region(whole, fixed)]

    def copies(self, s, p, k):
        dim, whole = GATHERED[s][p][k], GATHERED[s][p][:k]
        block = self.here(s, p, whole)
        return [
            remote(
                block,
                block,
                self.send_sem.at[s, k],
                self.last_recv.at[p, offset - 1] if s == 0 and k == 2 else self.recv_sem.at[s, p, k],
                self.me.along(dim, offset),
            )
            for offset in ((1, 3) if s > 0 and k == 2 else (1, 3, 2))
        ]

    def came(self, s, p, k):
        dim, whole = GATHERED[s][p][k], GATHERED[s][p][:k]
        count = 2 if s > 0 and k == 2 else 3
        blocks = self.here(s, p, whole, {dim: pl.ds(0, count)})
        wait_came(blocks, self.recv_sem.at[s, p, k], self.me.sibling())

    def relays(self, s, p):
        me, (dim, whole) = self.me, (GATHERED[s][p][2], GATHERED[s][p][:2])
        out = []
        for n, (source, target) in enumerate(((3, 1), (1, 3))):
            fixed = {dim: lax.rem(me.chip[dim] + source, 4), whole[0]: pl.ds(2 * n, 2)}
            block = self.here(s, p, whole, fixed)
            sems = self.relay_send.at[s], self.relay_recv.at[s, p]
            out.append(remote(block, block, *sems, me.along(dim, target)))
        return out

    def across(self, s, p, part):
        me, (dim, whole) = self.me, (GATHERED[s][p][2], GATHERED[s][p][:2])
        block = self.here(s, p, whole, {dim: lax.rem(me.chip[dim] + 4 - part, 4)})
        return remote(block, block, self.side_send.at[s], self.side_recv.at[s], me.sibling())

    def start(self, s):
        for p in range(3):
            for copy in self.copies(s, p, 0):
                copy.start()

    def advance(self, s, k):
        for p in range(3):
            self.came(s, p, k)
            for copy in self.copies(s, p, k + 1):
                copy.start()
            if k == 1:
                self.across(s, p, 0).start()

    def hand_over(self):
        copies = [self.copies(0, p, 2) for p in range(3)]
        for n, part in enumerate((1, 3, 2)):
            for p in range(3):
                copies[p][n].wait_recv()
                self.across(0, p, part).start()

    def relay(self, s):
        for p in range(3):
            self.came(s, p, 2)
            for onward in self.relays(s, p):
                onward.start()
        for p in range(3):
            self.across(s, p, 1).start()
            self.across(s, p, 3).start()

    def close(self, s):
        for p in range(3):
            block = self.here(s, p, GATHERED[s][p][:2])
            wait_came(block, self.relay_recv.at[s, p], self.me.sibling())
            self.across(s, p, 2).start()

    def finish(self, s):
        wait_came(self.shards[s].at[pl.ds(0, 3)], self.side_recv.at[s], self.me.sibling())

    def drain(self, s):
        shards, other, three = self.shards[s], self.me.sibling(), pl.ds(0, 3)
        wait_sent(shards.at[three, 0, 0, three], self.send_sem.at[s, 0], other)
        wait_sent(shards.at[three, 0, three], self.send_sem.at[s, 1], other)
        count = pl.ds(0, 2) if s > 0 else three
        wait_sent(shards.at[three, count], self.send_sem.at[s, 2], other)
        if s > 0:
            wait_sent(shards.at[three, 0], self.relay_send.at[s], other)
        wait_sent(shards.at[three], self.side_send.at[s], other)


class Total:
    scratch = [VMEM((5, 8, D), f32), VMEM((4, 3, 8, D), f32), DMA((4,)), DMA((4,))]

    def __init__(self, me, scratch):
        self.me = me
        self.held, self.slots, self.send_sem, self.recv_sem = scratch

    def copies(self, k):
        me = self.me
        devices = [me.sibling()] if k == 3 else [me.along(k, offset) for offset in (1, 2, 3)]
        return [
            remote(
                self.held.at[k],
                self.slots.at[k, n],
                self.send_sem.at[k],
                self.recv_sem.at[k],
                device,
            )
            for n, device in enumerate(devices)
        ]

    def send(self, k):
        for copy in self.copies(k):
            copy.start()

    def came(self, k):
        return self.slots.at[3, pl.ds(0, 1)] if k == 3 else self.slots.at[k]

    def add(self, k):
        wait_came(self.came(k), self.recv_sem.at[k], self.me.sibling())
        total = self.held[k]
        for n in range(1 if k == 3 else 3):
            total = total + self.slots[k, n]
        self.held[k + 1] = total

    def drain(self):
        for k in range(4):
            wait_sent(self.came(k), self.send_sem.at[k], self.me.sibling())


class Reduce:
    scratch = [
        VMEM((3, 4, 4, 4, 48, 128), bf16),
        VMEM((3, 4, 4, 4, 48, 128), bf16),
        VMEM((3, 4, 4, 4, 48, 128), bf16),
        VMEM((3, 3, 3, 4, 4, 48, 128), bf16),
        VMEM((3, 3, 3, 4, 48, 128), bf16),
        VMEM((3, 3, 3, 48, 128), bf16),
        VMEM((3, 3, 48, 128), f32),
        VMEM((3, 3, 24, 128), f32),
        DMA((3,)),
        DMA((3, 4)),
        DMA((3, 3)),
        DMA((3, 3, 3)),
        DMA((3, 2)),
    ]

    def __init__(self, me, shards, scratch):
        self.me, self.shards = me, shards
        self.side, self.slots = scratch[:3], scratch[3:6]
        self.summed, self.crossed = scratch[6:8]
        self.side_send, self.side_recv, self.send_sem, self.recv_sem = scratch[8:12]
        self.last_sem = scratch[12]

    def slab(self, turn):
        return lax.rem(self.me.chip[0] + 1 + turn, 4)

    def across(self, s, turn):
        me, x = self.me, self.slab(turn)
        return remote(
            self.shards[s].at[pl.ds(3 * (1 - me.core), 3), x],
            self.side[s].at[:, x],
            self.side_send.at[s],
            self.side_recv.at[s, turn],
            me.sibling(),
        )

    def send_first(self, s, p, turn):
        me, x, dim = self.me, self.slab(turn), EVEN[p][2]
        own, slots = self.shards[s].at[3 * me.core + p, x], self.slots[0].at[s, p]
        sems = self.send_sem.at[s, 0], self.recv_sem.at[s, p, 0]
        if dim == 0:

            @pl.when(turn < 3)
            def _():
                remote(own, slots.at[turn], *sems, me.along(0, turn + 1)).start()

            return
        for offset in (2, 1, 3):
            there = lax.rem(me.chip[dim] + offset, 4)
            part = own.at[there] if dim == 1 else own.at[:, there]
            remote(part, slots.at[offset - 1, x], *sems, me.along(dim, offset)).start()

    def send(self, s, p, k):
        me, dim, whole = self.me, EVEN[p][2 - k], EVEN[p][: 2 - k]
        for offset in (2, 1, 3):
            there = {dim: lax.rem(me.chip[dim] + offset, 4)}
            remote(
                self.shards[s].at[(3 * me.core + p,) + me.region(whole, there)],
                self.slots[k].at[s, p, offset - 1],
                self.send_sem.at[s, k],
                self.recv_sem.at[s, p, k],
                me.along(dim, offset),
            ).start()

    def begin(self, s, turn):
        self.across(s, turn).start()

    def enter(self, s, turn):
        self.across(s, turn).wait_recv()
        shards, side, x = self.shards[s], self.side[s], self.slab(turn)
        for p in range(3):
            t = 3 * self.me.core + p

            def step(y, carry):
                total = shards[t, x, y].astype(f32) + side[p, x, y].astype(f32)
                shards[t, x, y] = total.astype(bf16)
                return carry

            lax.fori_loop(0, 4, step, 0)
            self.send_first(s, p, turn)

    def advance(self, s, k):
        me, shards, slots = self.me, self.shards[s], self.slots[k]
        for p in range(3):
            wait_came(slots.at[s, p], self.recv_sem.at[s, p, k], me.sibling())
            t, whole = 3 * me.core + p, sorted(EVEN[p][: 2 - k])
            if k == 2:
                total = shards[(t,) + me.chip].astype(f32)
                for n in range(3):
                    total = total + slots[s, p, n].astype(f32)
                self.summed[s, p] = total
                continue

            def step(i, carry):
                inner = (lax.div(i, 4), lax.rem(i, 4)) if k == 0 else (i,)
                chip = me.region((), dict(zip(whole, inner)))
                total = shards[(t,) + chip].astype(f32)
                for n in range(3):
                    total = total + slots[(s, p, n) + inner].astype(f32)
                shards[(t,) + chip] = total.astype(bf16)
                return carry

            lax.fori_loop(0, 16 if k == 0 else 4, step, 0)
            self.send(s, p, k + 1)
        if k == 2:
            self.last(s).start()

    def last(self, s):
        me = self.me
        return remote(
            self.summed.at[s, :, aligned(24 * (1 - me.core), 24, 8)],
            self.crossed.at[s],
            self.last_sem.at[s, 0],
            self.last_sem.at[s, 1],
            me.sibling(),
        )

    def finish(self, s, out):
        core = self.me.core
        self.last(s).wait_recv()
        for p in range(3):
            rows = pl.ds(24 * s, 24)
            own = self.summed[s, p, aligned(24 * core, 24, 8)]
            out[rows, aligned(384 * core + 128 * p, 128, 128)] = own
            out[rows, aligned(384 * (1 - core) + 128 * p, 128, 128)] = self.crossed[s, p]

    def drain(self, s):
        self.last(s).wait_send()
        wait_sent(self.side[s], self.side_send.at[s], self.me.sibling())
        for k in range(3):
            wait_sent(self.slots[k].at[s], self.send_sem.at[s, k], self.me.sibling())


def normal_of(x):
    center = x - jnp.mean(x, axis=-1, keepdims=True)
    rstd = lax.rsqrt(jnp.mean(center * center, axis=-1, keepdims=True) + NORM_EPS)
    return center * rstd, rstd


def norm_back(d_h, gain, xhat, rstd):
    e = d_h * gain
    inner = jnp.mean(e, axis=-1, keepdims=True) + xhat * jnp.mean(
        e * xhat, axis=-1, keepdims=True
    )
    return (e - inner) * rstd


def lanes_of(ref, *index):
    return jnp.concatenate([ref[(t,) + index] for t in range(ref.shape[0])], axis=-1)


def swapped(v):
    lane = lax.broadcasted_iota(jnp.int32, v.shape, 1)
    return jnp.where((lane & 63) < 32, pltpu.roll(v, 96, 1), pltpu.roll(v, 32, 1))


def first_head(shape):
    return lax.broadcasted_iota(jnp.int32, shape, 1) < HD


def split_heads(v):
    own, zero = first_head(v.shape), jnp.zeros_like(v)
    return jnp.concatenate([jnp.where(own, v, zero), jnp.where(own, zero, v)], axis=0)


def join_heads(v):
    half = v.shape[0] // 2
    return jnp.where(first_head((half, v.shape[1])), v[:half], v[half:])


class Layer:
    scratch = [
        VMEM((3 * D, D), bf16),
        VMEM((D, D), bf16),
        VMEM((2 * SEQ, D), bf16),
        VMEM((PAIRS, SEQ, 128), bf16),
        VMEM((2 * PAIRS, 2 * SEQ, 128), bf16),
        VMEM((PAIRS, SEQ, 128), bf16),
        VMEM((SEQ, D), f32),
        VMEM((SEQ, D), bf16),
        VMEM((SEQ, D), f32),
        VMEM((SEQ, D), f32),
        VMEM((4, TILE, 5 * TILE), bf16),
    ] + [VMEM((PAIRS, 2 * TILE, (i + 2) * TILE), bf16) for i in range(TILES)]

    def __init__(self, scratch):
        self.qkv, self.out, self.h1, self.q, self.kv, self.att, self.x2, self.h2 = scratch[:8]
        self.sum_a, self.sum_b, self.mask = scratch[8:11]
        self.probs = scratch[11:15]
        self.d_branch, self.d_att = self.h2, self.att

    def line(self, x, y):
        row = (lax.rem(x, 2) * 4 + y) * 2 + lax.div(x, 2)
        return aligned(144 * row, 144, 16), aligned(48 * row, 48, 16)

    def unpack(self, shards, perm):
        def step(x, carry):
            for y in range(4):
                tiles = [shards[t, x, y].reshape(192, 128) for t in range(6)]
                block = dot_nn(perm[...], jnp.concatenate(tiles, axis=1)).astype(bf16)
                rows_qkv, rows_out = self.line(x, y)
                self.qkv[rows_qkv] = block[:144]
                self.out[rows_out] = block[144:]
            return carry

        lax.fori_loop(0, 4, step, 0)

    def pack(self, grads, shards, perm, x):
        for y in range(4):
            rows_qkv, rows_out = self.line(x, y)
            tiles = [grads[t // 3][t % 3, rows_qkv] for t in range(6)]
            block = jnp.concatenate(tiles, axis=1)
            block = jnp.concatenate([block, self.out[rows_out]], axis=0)
            block = dot_tn(perm[...], block).astype(bf16)
            for t in range(6):
                shards[t, x, y] = block[:, 128 * t : 128 * t + 128].reshape(4, 48, 128)

    def masks(self, length, size):
        row = lax.broadcasted_iota(jnp.int32, (TILE, TILE), 0)
        col = lax.broadcasted_iota(jnp.int32, (TILE, TILE), 1)
        shift = jnp.where(size == 4, 2, jnp.where(size == 8, 3, 4))
        n_row = lax.shift_right_logical(row, jnp.full_like(row, shift))
        n_col = lax.shift_right_logical(col, jnp.full_like(col, shift))
        for i in range(TILES):
            for j in range(i + 2):
                key = min(j, i) * TILE + col
                seen = key < length
                if j == i:
                    seen = seen & (n_row > n_col)
                if j == i + 1:
                    seen = seen & (n_row == n_col)
                self.mask[i, :, j * TILE : (j + 1) * TILE] = jnp.where(seen, 0.0, MASKED).astype(bf16)

    def norm_one(self, x, gains, first_row):
        gain = gains[0:1, :]

        def step(i, carry):
            rows = aligned(i * TILE, TILE, TILE)
            xhat, _ = normal_of(x[rows].astype(f32))
            self.h1[aligned(first_row + i * TILE, TILE, TILE)] = (xhat * gain).astype(bf16)
            return carry

        lax.fori_loop(0, TILES, step, 0)

    def project(self, cos, sin, clean):
        def turned(v, scale):
            return (v * (cos[...] * scale) + swapped(v) * (sin[...] * scale)).astype(bf16)

        rows = slice(SEQ, 2 * SEQ) if clean else slice(0, SEQ)
        for j in range(3 if clean else 0, 9):
            v = dot_nt(self.h1[rows], self.qkv[256 * j : 256 * j + 256])
            for n in range(2):
                part = v[:, 128 * n : 128 * n + 128]
                if j < 3:
                    self.q[2 * j + n] = turned(part, HD ** (-0.5))
                elif j < 6:
                    self.kv[2 * j - 6 + n, rows] = turned(part, 1.0)
                else:
                    self.kv[2 * j - 6 + n, rows] = part.astype(bf16)

    def keys(self, t, i):
        clean = self.kv[t, SEQ : SEQ + (i + 1) * TILE]
        return jnp.concatenate([clean, self.kv[t, i * TILE : (i + 1) * TILE]], axis=0)

    def scores(self, pair, i):
        width = (i + 2) * TILE
        queries = split_heads(self.q[pair, pl.ds(i * TILE, TILE)])
        scores = dot_nt(queries, self.keys(pair, i)).reshape(2, TILE, width)
        return (scores + self.mask[i, :, :width].astype(f32)[None]).reshape(2 * TILE, width)

    def attend(self, pairs):
        places = [(pair, i) for pair in pairs for i in range(TILES)]
        scores = [self.scores(pair, i) for pair, i in places]
        raised = [jnp.exp(s - jnp.max(s, axis=-1, keepdims=True)) for s in scores]
        mixed = [
            dot_nn(e.astype(bf16), self.keys(PAIRS + pair, i))
            for e, (pair, i) in zip(raised, places)
        ]
        for e, o, (pair, i) in zip(raised, mixed, places):
            share = 1.0 / jnp.sum(e, axis=-1, keepdims=True)
            self.probs[i][pair] = (e * share).astype(bf16)
            self.att[pair, pl.ds(i * TILE, TILE)] = join_heads(o * share).astype(bf16)

    def mix(self, x, gains):
        for j in range(3):
            cols = slice(256 * j, 256 * j + 256)
            branch = dot_nn(lanes_of(self.att), self.out[:, cols])
            self.x2[:, cols] = x[:, cols].astype(f32) + branch
        gain = gains[1:2, :]

        def step(i, carry):
            rows = aligned(i * TILE, TILE, TILE)
            xhat, _ = normal_of(self.x2[rows])
            self.h2[rows] = (xhat * gain).astype(bf16)
            self.sum_a[rows] = jnp.zeros((TILE, D), f32)
            self.sum_b[rows] = jnp.zeros((TILE, D), f32)
            return carry

        lax.fori_loop(0, TILES, step, 0)

    def feed(self, up, down, dy, x, act_ref, d_up_ref):
        c = (2.0 / np.pi) ** 0.5
        rows = [aligned(768 * x + 256 * j, 256, 256) for j in range(3)]
        cols = [slice(256 * j, 256 * j + 256) for j in range(3)]
        ups = [dot_nt(self.h2[...], lanes_of(up, r)) for r in rows]
        d_acts = [dot_nt(dy[...], lanes_of(down, r)) for r in rows]
        for u, d_act, part in zip(ups, d_acts, cols):
            squared = u * u
            t = jnp.tanh(u * (c + (0.044715 * c) * squared))
            half = 0.5 + 0.5 * t
            act_ref[:, part] = (u * half).astype(bf16)
            slope = half + (0.5 * u) * (1.0 - t * t) * (c + (3 * 0.044715 * c) * squared)
            d_up_ref[:, part] = (slope * d_act).astype(bf16)
        slab = aligned(768 * x, 768, 256)
        for n, part in enumerate(cols):
            tiles = (2 * n, 2 * n + 1)
            w_up = jnp.concatenate([up[t, slab] for t in tiles], axis=1)
            w_down = jnp.concatenate([down[t, slab] for t in tiles], axis=1)
            self.sum_a[:, part] += dot_nn(act_ref[...], w_down)
            self.sum_b[:, part] += dot_nn(d_up_ref[...], w_up)
        g_up = [dot_tn(d_up_ref[:, part], self.h2[...]).astype(bf16) for part in cols]
        g_down = [dot_tn(act_ref[:, part], dy[...]).astype(bf16) for part in cols]
        for j in range(3):
            for t in range(LANES):
                up[t, rows[j]] = g_up[j][:, 128 * t : 128 * t + 128]
                down[t, rows[j]] = g_down[j][:, 128 * t : 128 * t + 128]

    def back_two(self, dy, gains, outputs, d_gains):
        gain = gains[1:2, :]

        def step(i, carry):
            rows = aligned(i * TILE, TILE, TILE)
            x2 = self.x2[rows]
            outputs[rows] = (x2 + self.sum_a[rows]).astype(bf16)
            xhat, rstd = normal_of(x2)
            d_h = self.sum_b[rows]
            d_x2 = dy[rows].astype(f32) + norm_back(d_h, gain, xhat, rstd)
            self.sum_b[rows] = d_x2
            self.d_branch[rows] = d_x2.astype(bf16)
            return carry + jnp.sum(d_h * xhat, axis=0, keepdims=True)

        d_gains[1:2, :] = lax.fori_loop(0, TILES, step, jnp.zeros((1, D), f32))

    def back_mix(self):
        for j in range(3):
            rows = slice(256 * j, 256 * j + 256)
            att = jnp.concatenate([self.att[2 * j], self.att[2 * j + 1]], axis=1)
            d_att = dot_nt(self.d_branch[...], self.out[rows]).astype(bf16)
            self.out[rows] = dot_tn(att, self.d_branch[...]).astype(bf16)
            self.d_att[2 * j] = d_att[:, :128]
            self.d_att[2 * j + 1] = d_att[:, 128:]

    def back_values(self, pair, d_values):
        parts = []
        for i in range(TILES):
            d_att = split_heads(self.d_att[pair, pl.ds(i * TILE, TILE)])
            parts.append(dot_tn(self.probs[i][pair], d_att))
        for i in range(TILES):
            rows = slice(i * TILE, (i + 1) * TILE)
            own = slice(VALUES_OWN + i * TILE, VALUES_OWN + (i + 1) * TILE)
            clean = slice(VALUES_CLEAN + i * TILE, VALUES_CLEAN + (i + 1) * TILE)
            d_values[pair, own] = parts[i][(i + 1) * TILE :].astype(bf16)
            d_values[pair, clean] = sum(part[rows] for part in parts[i:]).astype(bf16)

    def back_attend(self, pair, cos, sin, d_values):
        tiles = [pl.ds(i * TILE, TILE) for i in range(TILES)]
        queries = [split_heads(self.q[pair, rows]) for rows in tiles]
        d_atts = [split_heads(self.d_att[pair, rows]) for rows in tiles]
        d_probs = [dot_nt(d_atts[i], self.keys(PAIRS + pair, i)) for i in range(TILES)]
        d_scores = []
        for i in range(TILES):
            probs = self.probs[i][pair].astype(f32)
            delta = jnp.sum(probs * d_probs[i], axis=-1, keepdims=True)
            d_scores.append((probs * (d_probs[i] - delta)).astype(bf16))
        d_query = [join_heads(dot_nn(d_scores[i], self.keys(pair, i))) for i in range(TILES)]
        parts = [dot_tn(d_scores[i], queries[i]) for i in range(TILES)]

        def back(v, rows):
            return (v * cos[rows] - swapped(v) * sin[rows]).astype(bf16)

        for i, rows in enumerate(tiles):
            clean, part = pl.ds(SEQ + i * TILE, TILE), slice(i * TILE, (i + 1) * TILE)
            self.q[pair, rows] = back(d_query[i] * HD ** (-0.5), rows)
            self.kv[pair, clean] = back(sum(d_k[part] for d_k in parts[i:]), rows)
            self.kv[pair, rows] = back(parts[i][(i + 1) * TILE :], rows)
        self.kv[PAIRS + pair, :SEQ] = d_values[pair, VALUES_OWN : VALUES_OWN + SEQ]
        self.kv[PAIRS + pair, SEQ:] = d_values[pair, VALUES_CLEAN : VALUES_CLEAN + SEQ]

    def back_clean(self, gains, x_clean, grads_clean, d_gains):
        gain = gains[0:1, :]

        def step(i, carry):
            clean = aligned(SEQ + i * TILE, TILE, TILE)
            own = aligned(i * TILE, TILE, TILE)
            d_h = dot_nn(lanes_of(self.kv, clean), self.qkv[D:])
            xhat, rstd = normal_of(x_clean[own].astype(f32))
            grads_clean[own] = norm_back(d_h, gain, xhat, rstd).astype(bf16)
            return carry + jnp.sum(d_h * xhat, axis=0, keepdims=True)

        d_gains[0:1, :] = lax.fori_loop(0, TILES, step, jnp.zeros((1, D), f32))

    def back_own(self, weights, gains, x, grads, d_gains):
        gain = gains[0:1, :]

        def step(i, carry):
            own = aligned(i * TILE, TILE, TILE)
            d_proj = jnp.concatenate([lanes_of(self.q, own), lanes_of(self.kv, own)], axis=1)
            d_h = dot_nn(d_proj, weights[...])
            xhat, rstd = normal_of(x[own].astype(f32))
            grads[own] = self.sum_b[own] + norm_back(d_h, gain, xhat, rstd)
            return carry + jnp.sum(d_h * xhat, axis=0, keepdims=True)

        d_gains[0:1, :] += lax.fori_loop(0, TILES, step, jnp.zeros((1, D), f32))

    def grad_project(self, grads, d_values, second):
        def put(row, tiles, tokens):
            value = dot_tn(jnp.concatenate(tiles, axis=1), self.h1[:tokens]).astype(bf16)
            for t in range(6):
                grads[t // 3][t % 3, row : row + 384] = value[:, 128 * t : 128 * t + 128]

        def values_of(pair):
            own = d_values[pair, VALUES_OWN : VALUES_OWN + SEQ]
            return jnp.concatenate([own, d_values[pair, VALUES_CLEAN : VALUES_CLEAN + SEQ]], axis=0)

        if second:
            put(1152, [self.kv[t] for t in (3, 4, 5)], 2 * SEQ)
            put(1536, [values_of(t) for t in (0, 1, 2)], 2 * SEQ)
            put(1920, [values_of(t) for t in (3, 4, 5)], 2 * SEQ)
        else:
            put(0, [self.q[t] for t in (0, 1, 2)], SEQ)
            put(384, [self.q[t] for t in (3, 4, 5)], SEQ)
            put(768, [self.kv[t] for t in (0, 1, 2)], 2 * SEQ)


class Rest:
    scratch = [
        VMEM(SHARDS, bf16),
        VMEM(SHARDS, bf16),
        VMEM(SHARDS, bf16),
        VMEM((SEQ, D), bf16),
        VMEM((SEQ, D), bf16),
        VMEM((8, D), f32),
        DMA((2,)),
        DMA((2,)),
    ]


def split(refs, *groups):
    out, at = [], 0
    for group in groups:
        out.append(refs[at : at + len(group.scratch)])
        at += len(group.scratch)
    return out


CLEAN = ((0, 128), (128, 128), (256, 256))
NOISY = ((0, 128), (128, 128), (256, 128), (384, 128))


def pieces(src, dst, sems, device, cuts):
    out = []
    for n, (row, count) in enumerate(cuts):
        rows = pl.ds(row, count)
        out.append(remote(src.at[rows], dst.at[rows], sems.at[0], sems.at[1], device))
    return out


def step_kernel(
    lengths, sizes, w_qkv, w_out, w_up, w_down, gains_own, x, dy, perm, cos, sin,
    outputs, grads_in, grads, d_gains_all, *scratch
):
    gather_refs, total_refs, layer_refs, reduce_refs, back_refs, rest = split(
        scratch, Gather, Total, Layer, Reduce, Total, Rest
    )
    shards = rest[:3]
    x_clean, back, d_gains, clean_sem, back_sem = rest[3:]
    me = Place()
    gather = Gather(me, shards, gather_refs)
    total = Total(me, total_refs)
    total_back = Total(me, back_refs)
    layer = Layer(layer_refs)
    reduce = Reduce(me, shards, reduce_refs)
    gains, given = total.held.at[4], layer.h2
    to_clean = pieces(x, x_clean, clean_sem, me.partner(), CLEAN)
    from_noisy = pieces(given, back, back_sem, me.partner(), NOISY)

    def clean_sends(n):
        @pl.when(me.stream == 0)
        def _():
            to_clean[n].start()

    def noisy_sends(n):
        @pl.when(me.stream == 1)
        def _():
            from_noisy[n].start()

    packed = gather.packed
    packed[0:18] = w_qkv[...]
    packed[18:24] = w_out[...]
    packed[24:48] = w_up[...]
    packed[48:72] = w_down[...]
    total.held[0] = jnp.zeros((8, D), f32)
    total.held[0, 0:2, 0:6] = gains_own[...].astype(bf16).astype(f32)
    total.held[0] = pltpu.roll(total.held[0], 6 * lax.axis_index(AXES), 1)
    me.greet()
    gather.swap().start()
    total.send(0)
    layer.masks(lengths[0], sizes[0])

    @pl.when(me.stream == 0)
    def _():
        x_clean[...] = x[...]

    gather.swap().wait()
    gather.assemble()
    gather.start(0)
    gather.start(1)
    gather.start(2)
    clean_sends(0)
    total.add(0)
    total.send(1)
    gather.advance(0, 0)
    clean_sends(1)
    total.add(1)
    total.send(2)
    gather.advance(1, 0)
    gather.advance(2, 0)
    gather.advance(0, 1)
    clean_sends(2)
    total.add(2)
    total.send(3)
    total.add(3)
    layer.norm_one(x, gains, 0)
    gather.advance(1, 1)
    gather.advance(2, 1)
    gather.hand_over()
    gather.finish(0)
    layer.unpack(shards[0], perm)
    layer.project(cos, sin, False)
    gather.relay(1)

    @pl.when(me.stream == 1)
    def _():
        wait_came(x_clean, clean_sem.at[1], me.partner())

    layer.norm_one(x_clean, gains, SEQ)
    layer.project(cos, sin, True)
    gather.relay(2)

    def forward(n, carry):
        layer.attend((2 * n, 2 * n + 1))
        for at, s in ((0, 1), (1, 2)):

            @pl.when(n == at)
            def _():
                gather.close(s)

        return carry

    lax.fori_loop(0, PAIRS // 2, forward, 0)
    layer.mix(x, gains)
    for s in range(3):
        if s > 0:
            gather.finish(s)
        gather.drain(s)
    total.drain()
    up, down = shards[1].reshape(6, FF, 128), shards[2].reshape(6, FF, 128)

    def feed(turn, carry):
        layer.feed(up, down, dy, reduce.slab(turn), outputs, grads_in)
        reduce.begin(1, turn)
        reduce.begin(2, turn)

        @pl.when(turn > 0)
        def _():
            reduce.enter(1, turn - 1)
            reduce.enter(2, turn - 1)

        return carry

    lax.fori_loop(0, 4, feed, 0)
    d_gains[...] = jnp.zeros((8, D), f32)
    layer.back_two(dy, gains, outputs, d_gains)
    reduce.enter(1, 3)
    reduce.enter(2, 3)
    layer.back_mix()

    d_values = shards[0].reshape(6, FF, 128)
    grads_qkv = [side.reshape(3, FF, 128) for side in reduce.side[1:]]

    def values(pair, carry):
        layer.back_values(pair, d_values)
        return carry

    lax.fori_loop(0, PAIRS, values, 0)
    odd = lax.rem(me.chip[0], 2)

    def half(second):
        layer.grad_project(grads_qkv, d_values, second)
        for n in (0, 2):
            turn = (odd if second else 1 - odd) + n
            layer.pack(grads_qkv, shards[0], perm, reduce.slab(turn))
            reduce.begin(0, turn)

    def enter(second):
        for n in (0, 2):
            reduce.enter(0, (odd if second else 1 - odd) + n)

    def backward(n, carry):
        layer.back_attend(lax.rem(n + 3, PAIRS), cos, sin, d_values)

        @pl.when(n == 1)
        def _():
            reduce.advance(1, 0)

        @pl.when(n == 2)
        def _():
            reduce.advance(2, 0)
            half(True)

        @pl.when(n == 3)
        def _():
            enter(True)
            reduce.advance(1, 1)

        @pl.when(n == 4)
        def _():
            reduce.advance(2, 1)

        return carry

    lax.fori_loop(0, PAIRS, backward, 0)
    layer.back_clean(gains, x_clean, given, d_gains)
    noisy_sends(0)
    half(False)
    reduce.advance(1, 2)
    enter(False)
    noisy_sends(1)
    layer.back_own(layer.qkv, gains, x, layer.x2, d_gains)
    total_back.held[0] = d_gains[...]
    total_back.send(0)
    reduce.advance(2, 2)
    reduce.finish(1, grads)
    reduce.advance(0, 0)
    reduce.finish(2, grads)
    noisy_sends(2)
    total_back.add(0)
    total_back.send(1)
    reduce.advance(0, 1)
    noisy_sends(3)
    total_back.add(1)
    total_back.send(2)
    reduce.advance(0, 2)
    total_back.add(2)
    total_back.send(3)

    @pl.when(me.stream == 0)
    def _():
        wait_came(back, back_sem.at[1], me.partner())
        both = given[...].astype(f32) + back[...].astype(f32)
        grads_in[...] = (layer.x2[...] + both).astype(bf16)

    @pl.when(me.stream == 1)
    def _():
        grads_in[...] = layer.x2[...].astype(bf16)

    reduce.finish(0, grads)
    total_back.add(3)
    d_gains_all[...] = total_back.held[4]

    @pl.when(me.stream == 0)
    def _():
        wait_sent(x_clean, clean_sem.at[0], me.partner())

    @pl.when(me.stream == 1)
    def _():
        wait_sent(back, back_sem.at[0], me.partner())

    total_back.drain()
    for s in range(3):
        reduce.drain(s)


def adam(weight, grad, first, second, rate):
    first_new = BETA_ONE * first + (1.0 - BETA_ONE) * grad
    second_new = BETA_TWO * second + (1.0 - BETA_TWO) * grad * grad
    fix_one = 1.0 - BETA_ONE**STEP
    fix_two = 1.0 - BETA_TWO**STEP
    update = first_new / fix_one / (jnp.sqrt(second_new / fix_two) + ADAM_EPS)
    return (weight - rate * (update + WEIGHT_DECAY * weight), first_new, second_new)


ROWS = ((0, 18), (18, 24), (24, 48), (48, 72))


def adam_kernel(grads, d_gains, outputs, grads_in, *refs):
    weights, firsts, seconds, outs = refs[:5], refs[5:10], refs[10:15], refs[15:]
    outs[19][...] = outputs[...]
    outs[20][...] = grads_in[...]
    turn = lax.rem(D - 6 * lax.axis_index(AXES), D)
    d_gains_own = pltpu.roll(d_gains[...], turn, 1)[0:2, 0:6]
    for n in range(5):
        grad = d_gains_own if n == 4 else grads[ROWS[n][0] : ROWS[n][1]]
        new = adam(weights[n][...], grad, firsts[n][...], seconds[n][...], RATES[n])
        for part in range(3):
            outs[5 * part + n][...] = new[part]
        if n < 4:
            outs[15 + n][...] = new[0].astype(bf16)


def call(kernel, out_shape, operands, scratch=(), collective=None, smem=0):
    spec, place = pl.BlockSpec(memory_space=VMEM), pl.BlockSpec(memory_space=pltpu.SMEM)
    return pl.pallas_call(
        kernel,
        out_shape=out_shape,
        in_specs=[place] * smem + [spec] * (len(operands) - smem),
        out_specs=[spec] * len(out_shape),
        scratch_shapes=list(scratch),
        compiler_params=pltpu.CompilerParams(
            collective_id=collective,
            has_side_effects=collective is not None,
            vmem_limit_bytes=63 << 20,
        ),
    )(*operands)


def permutation():
    perm = np.zeros((192, 192), np.float32)
    for row in range(192):
        if row < 144:
            perm[row, 24 * (row // 18) + row % 18] = 1
        else:
            perm[row, 24 * ((row - 144) // 6) + 18 + (row - 144) % 6] = 1
    return perm


def rotary_tables():
    frequency = 10000.0 ** (-2.0 * np.arange(HD // 2) / HD)
    angles = (np.arange(SEQ)[:, None] * frequency[None, :]).astype(np.float32)
    cos, sin = np.cos(angles), np.sin(angles)
    return np.tile(cos, (1, 4)), np.concatenate([-sin, sin, -sin, sin], axis=1)


def local(
    inputs, cotangent, lengths, block_sizes, w_qkv, w_out, w_up, w_down, gains,
    first_qkv, first_out, first_up, first_down, first_gains,
    second_qkv, second_out, second_up, second_down, second_gains,
):
    shape = jax.ShapeDtypeStruct
    masters = (w_qkv.T, w_out, w_up.T, w_down, gains)
    firsts = (first_qkv.T, first_out, first_up.T, first_down, first_gains)
    seconds = (second_qkv.T, second_out, second_up.T, second_down, second_gains)
    x, dy = inputs[0, 0], cotangent[0, 0]
    rows16, small = shape((SEQ, D), bf16), shape((8, D), f32)
    cos, sin = rotary_tables()
    groups = (Gather, Total, Layer, Reduce, Total, Rest)
    outputs, input_grads, grads, d_gains = call(
        step_kernel,
        [rows16, rows16, shape((72, D), f32), small],
        (lengths, block_sizes, *masters, x, dy, jnp.asarray(permutation(), bf16),
         jnp.asarray(cos, f32), jnp.asarray(sin, f32)),
        [item for group in groups for item in group.scratch],
        collective=0,
        smem=2,
    )
    like = [shape(w.shape, f32) for w in masters]
    *new, outputs, input_grads = call(
        adam_kernel,
        like * 3 + [shape(w.shape, bf16) for w in masters[:4]] + [rows16] * 2,
        (grads, d_gains, outputs, input_grads, *masters, *firsts, *seconds),
    )
    turned = [v.T if n % 5 in (0, 2) else v for n, v in enumerate(new)]
    return (outputs[None, None], input_grads[None, None], *turned)


def solution(mesh):
    mesh = Mesh(mesh.devices.reshape(2, 4, 2, 4, 2), AXES)
    data, one = P("xl", AXES[1:], None, None), P(AXES[1:])
    cols, rows = P(None, AXES), P(AXES, None)
    state = (cols, rows, cols, rows, cols)
    return jax.shard_map(
        local,
        mesh=mesh,
        in_specs=(data, data, one, one) + state * 3,
        out_specs=(data, data) + state * 3 + state[:4],
        check_vma=False,
    )
```

```python
import functools

import jax
import jax.numpy as jnp
import numpy as np
from jax import lax
from jax.experimental import pallas as pl
from jax.experimental.pallas import tpu as pltpu
from jax.sharding import Mesh
from jax.sharding import PartitionSpec as P

D = 768
H = 12
HD = 64
FF = 3072
SEQ = 512
STEP = 7
TILE = 128
TILES = SEQ // TILE
PAIRS = H // 2
LANES = D // 128
NORM_EPS = 1e-05
BETA_ONE = 0.5
BETA_TWO = 0.5
ADAM_EPS = 1e-08
WEIGHT_DECAY = 0.01
GAIN_RATE = 0.2
RATES = (D ** (-0.5), H ** (-0.5), D ** (-0.5), FF ** (-0.5), GAIN_RATE)
AXES = ("xl", "y", "xh", "z", "core")
EVEN = ((0, 1, 2), (1, 2, 0), (2, 0, 1))
GATHERED = (EVEN, ((0, 2, 1), (0, 1, 2), (0, 2, 1)), EVEN)
SHARDS = (6, 4, 4, 4, 48, 128)
MASKED = -1e30
VALUES_OWN, VALUES_CLEAN = 0, 1536

f32 = jnp.float32
bf16 = jnp.bfloat16
VMEM = pltpu.VMEM
DMA = pltpu.SemaphoreType.DMA
MESH = pl.DeviceIdType.MESH


def remote(src, dst, send, recv, device):
    return pltpu.make_async_remote_copy(
        src_ref=src,
        dst_ref=dst,
        send_sem=send,
        recv_sem=recv,
        device_id=device,
        device_id_type=MESH,
    )


def wait_sent(ref, sem, device):
    remote(ref, ref, sem, sem, device).wait_send()


def wait_came(ref, sem, device):
    remote(ref, ref, sem, sem, device).wait_recv()


def dot_nn(a, b):
    return jnp.dot(a, b, preferred_element_type=f32)


def dot_nt(a, b):
    return lax.dot_general(a, b, (((1,), (1,)), ((), ())), preferred_element_type=f32)


def dot_tn(a, b):
    return lax.dot_general(a, b, (((0,), (0,)), ((), ())), preferred_element_type=f32)


def aligned(start, size, step):
    return pl.ds(pl.multiple_of(start, step), size)


class Place:
    def __init__(self):
        self.stream = lax.axis_index("xl")
        self.core = lax.axis_index("core")
        self.chip = (
            lax.axis_index("xh") * 2 + self.stream,
            lax.axis_index("y"),
            lax.axis_index("z"),
        )

    def device(self, chip, core):
        return (lax.rem(chip[0], 2), chip[1], lax.div(chip[0], 2), chip[2], core)

    def along(self, dim, offset):
        chip = list(self.chip)
        chip[dim] = lax.rem(chip[dim] + offset, 4)
        return self.device(chip, self.core)

    def sibling(self):
        return self.device(self.chip, 1 - self.core)

    def partner(self):
        chip = (self.chip[0] + 1 - 2 * self.stream, self.chip[1], self.chip[2])
        return self.device(chip, self.core)

    def region(self, whole, fixed=None):
        out = []
        for dim in range(3):
            if fixed and dim in fixed:
                out.append(fixed[dim])
            elif dim in whole:
                out.append(slice(None))
            else:
                out.append(self.chip[dim])
        return tuple(out)

    def greet(self):
        barrier = pltpu.get_barrier_semaphore()
        others = [self.sibling()]
        others += [self.along(dim, offset) for dim in range(3) for offset in (1, 2, 3)]
        for other in others:
            pl.semaphore_signal(barrier, inc=1, device_id=other, device_id_type=MESH)
        pl.semaphore_wait(barrier, len(others))


class Gather:
    scratch = [
        VMEM((72, D), f32),
        VMEM((72, 384), f32),
        VMEM((3, 48, 384), f32),
        DMA((3, 3)),
        DMA((3, 3, 3)),
        DMA((3, 3)),
        DMA((3,)),
        DMA((3, 3)),
        DMA((3,)),
        DMA((3,)),
        DMA((2,)),
    ]

    def __init__(self, me, shards, scratch):
        self.me, self.shards = me, shards
        self.packed, self.half, self.block, self.send_sem, self.recv_sem = scratch[:5]
        self.last_recv, self.relay_send, self.relay_recv = scratch[5:8]
        self.side_send, self.side_recv, self.swap_sem = scratch[8:]

    def swap(self):
        me = self.me
        return remote(
            self.packed.at[:, aligned(384 * (1 - me.core), 384, 128)],
            self.half,
            self.swap_sem.at[0],
            self.swap_sem.at[1],
            me.sibling(),
        )

    def assemble(self):
        core = self.me.core
        own = self.packed[:, aligned(384 * core, 384, 128)]
        for s in range(3):
            self.block[s, aligned(24 * core, 24, 8)] = own[24 * s : 24 * s + 24]
            self.block[s, aligned(24 * (1 - core), 24, 8)] = self.half[24 * s : 24 * s + 24]
        for s in range(3):
            value = self.block[s].astype(bf16)
            for p in range(3):
                self.shards[s][(3 * core + p,) + self.me.chip] = value[:, 128 * p : 128 * p + 128]

    def here(self, s, p, whole, fixed=None):
        return self.shards[s].at[(3 * self.me.core + p,) + self.me.region(whole, fixed)]

    def copies(self, s, p, k):
        dim, whole = GATHERED[s][p][k], GATHERED[s][p][:k]
        block = self.here(s, p, whole)
        return [
            remote(
                block,
                block,
                self.send_sem.at[s, k],
                self.last_recv.at[p, offset - 1] if s == 0 and k == 2 else self.recv_sem.at[s, p, k],
                self.me.along(dim, offset),
            )
            for offset in ((1, 3) if s > 0 and k == 2 else (1, 3, 2))
        ]

    def came(self, s, p, k):
        dim, whole = GATHERED[s][p][k], GATHERED[s][p][:k]
        count = 2 if s > 0 and k == 2 else 3
        blocks = self.here(s, p, whole, {dim: pl.ds(0, count)})
        wait_came(blocks, self.recv_sem.at[s, p, k], self.me.sibling())

    def relays(self, s, p):
        me, (dim, whole) = self.me, (GATHERED[s][p][2], GATHERED[s][p][:2])
        out = []
        for n, (source, target) in enumerate(((3, 1), (1, 3))):
            fixed = {dim: lax.rem(me.chip[dim] + source, 4), whole[0]: pl.ds(2 * n, 2)}
            block = self.here(s, p, whole, fixed)
            sems = self.relay_send.at[s], self.relay_recv.at[s, p]
            out.append(remote(block, block, *sems, me.along(dim, target)))
        return out

    def across(self, s, p, part):
        me, (dim, whole) = self.me, (GATHERED[s][p][2], GATHERED[s][p][:2])
        block = self.here(s, p, whole, {dim: lax.rem(me.chip[dim] + 4 - part, 4)})
        return remote(block, block, self.side_send.at[s], self.side_recv.at[s], me.sibling())

    def start(self, s):
        for p in range(3):
            for copy in self.copies(s, p, 0):
                copy.start()

    def advance(self, s, k):
        for p in range(3):
            self.came(s, p, k)
            for copy in self.copies(s, p, k + 1):
                copy.start()
            if k == 1:
                self.across(s, p, 0).start()

    def hand_over(self):
        copies = [self.copies(0, p, 2) for p in range(3)]
        for n, part in enumerate((1, 3, 2)):
            for p in range(3):
                copies[p][n].wait_recv()
                self.across(0, p, part).start()

    def relay(self, s):
        for p in range(3):
            self.came(s, p, 2)
            for onward in self.relays(s, p):
                onward.start()
        for p in range(3):
            self.across(s, p, 1).start()
            self.across(s, p, 3).start()

    def close(self, s):
        for p in range(3):
            block = self.here(s, p, GATHERED[s][p][:2])
            wait_came(block, self.relay_recv.at[s, p], self.me.sibling())
            self.across(s, p, 2).start()

    def finish(self, s):
        wait_came(self.shards[s].at[pl.ds(0, 3)], self.side_recv.at[s], self.me.sibling())

    def drain(self, s):
        shards, other, three = self.shards[s], self.me.sibling(), pl.ds(0, 3)
        wait_sent(shards.at[three, 0, 0, three], self.send_sem.at[s, 0], other)
        wait_sent(shards.at[three, 0, three], self.send_sem.at[s, 1], other)
        count = pl.ds(0, 2) if s > 0 else three
        wait_sent(shards.at[three, count], self.send_sem.at[s, 2], other)
        if s > 0:
            wait_sent(shards.at[three, 0], self.relay_send.at[s], other)
        wait_sent(shards.at[three], self.side_send.at[s], other)


class Total:
    scratch = [VMEM((5, 8, D), f32), VMEM((4, 3, 8, D), f32), DMA((4,)), DMA((4,))]

    def __init__(self, me, scratch):
        self.me = me
        self.held, self.slots, self.send_sem, self.recv_sem = scratch

    def copies(self, k):
        me = self.me
        devices = [me.sibling()] if k == 3 else [me.along(k, offset) for offset in (1, 2, 3)]
        return [
            remote(
                self.held.at[k],
                self.slots.at[k, n],
                self.send_sem.at[k],
                self.recv_sem.at[k],
                device,
            )
            for n, device in enumerate(devices)
        ]

    def send(self, k):
        for copy in self.copies(k):
            copy.start()

    def came(self, k):
        return self.slots.at[3, pl.ds(0, 1)] if k == 3 else self.slots.at[k]

    def add(self, k):
        wait_came(self.came(k), self.recv_sem.at[k], self.me.sibling())
        total = self.held[k]
        for n in range(1 if k == 3 else 3):
            total = total + self.slots[k, n]
        self.held[k + 1] = total

    def drain(self):
        for k in range(4):
            wait_sent(self.came(k), self.send_sem.at[k], self.me.sibling())


class Reduce:
    scratch = [
        VMEM((3, 4, 4, 4, 48, 128), bf16),
        VMEM((3, 4, 4, 4, 48, 128), bf16),
        VMEM((3, 4, 4, 4, 48, 128), bf16),
        VMEM((3, 3, 3, 4, 4, 48, 128), bf16),
        VMEM((3, 3, 3, 4, 48, 128), bf16),
        VMEM((3, 3, 3, 48, 128), bf16),
        VMEM((3, 3, 48, 128), f32),
        VMEM((3, 3, 24, 128), f32),
        DMA((3,)),
        DMA((3, 4)),
        DMA((3, 3)),
        DMA((3, 3, 3)),
        DMA((3, 2)),
    ]

    def __init__(self, me, shards, scratch):
        self.me, self.shards = me, shards
        self.side, self.slots = scratch[:3], scratch[3:6]
        self.summed, self.crossed = scratch[6:8]
        self.side_send, self.side_recv, self.send_sem, self.recv_sem = scratch[8:12]
        self.last_sem = scratch[12]

    def slab(self, turn):
        return lax.rem(self.me.chip[0] + 1 + turn, 4)

    def across(self, s, turn):
        me, x = self.me, self.slab(turn)
        return remote(
            self.shards[s].at[pl.ds(3 * (1 - me.core), 3), x],
            self.side[s].at[:, x],
            self.side_send.at[s],
            self.side_recv.at[s, turn],
            me.sibling(),
        )

    def send_first(self, s, p, turn):
        me, x, dim = self.me, self.slab(turn), EVEN[p][2]
        own, slots = self.shards[s].at[3 * me.core + p, x], self.slots[0].at[s, p]
        sems = self.send_sem.at[s, 0], self.recv_sem.at[s, p, 0]
        if dim == 0:

            @pl.when(turn < 3)
            def _():
                remote(own, slots.at[turn], *sems, me.along(0, turn + 1)).start()

            return
        for offset in (2, 1, 3):
            there = lax.rem(me.chip[dim] + offset, 4)
            part = own.at[there] if dim == 1 else own.at[:, there]
            remote(part, slots.at[offset - 1, x], *sems, me.along(dim, offset)).start()

    def send(self, s, p, k):
        me, dim, whole = self.me, EVEN[p][2 - k], EVEN[p][: 2 - k]
        for offset in (2, 1, 3):
            there = {dim: lax.rem(me.chip[dim] + offset, 4)}
            remote(
                self.shards[s].at[(3 * me.core + p,) + me.region(whole, there)],
                self.slots[k].at[s, p, offset - 1],
                self.send_sem.at[s, k],
                self.recv_sem.at[s, p, k],
                me.along(dim, offset),
            ).start()

    def begin(self, s, turn):
        self.across(s, turn).start()

    def enter(self, s, turn):
        self.across(s, turn).wait_recv()
        shards, side, x = self.shards[s], self.side[s], self.slab(turn)
        for p in range(3):
            t = 3 * self.me.core + p

            def step(y, carry):
                total = shards[t, x, y].astype(f32) + side[p, x, y].astype(f32)
                shards[t, x, y] = total.astype(bf16)
                return carry

            lax.fori_loop(0, 4, step, 0)
            self.send_first(s, p, turn)

    def advance(self, s, k):
        me, shards, slots = self.me, self.shards[s], self.slots[k]
        for p in range(3):
            wait_came(slots.at[s, p], self.recv_sem.at[s, p, k], me.sibling())
            t, whole = 3 * me.core + p, sorted(EVEN[p][: 2 - k])
            if k == 2:
                total = shards[(t,) + me.chip].astype(f32)
                for n in range(3):
                    total = total + slots[s, p, n].astype(f32)
                self.summed[s, p] = total
                continue

            def step(i, carry):
                inner = (lax.div(i, 4), lax.rem(i, 4)) if k == 0 else (i,)
                chip = me.region((), dict(zip(whole, inner)))
                total = shards[(t,) + chip].astype(f32)
                for n in range(3):
                    total = total + slots[(s, p, n) + inner].astype(f32)
                shards[(t,) + chip] = total.astype(bf16)
                return carry

            lax.fori_loop(0, 16 if k == 0 else 4, step, 0)
            self.send(s, p, k + 1)
        if k == 2:
            self.last(s).start()

    def last(self, s):
        me = self.me
        return remote(
            self.summed.at[s, :, aligned(24 * (1 - me.core), 24, 8)],
            self.crossed.at[s],
            self.last_sem.at[s, 0],
            self.last_sem.at[s, 1],
            me.sibling(),
        )

    def finish(self, s, out):
        core = self.me.core
        self.last(s).wait_recv()
        for p in range(3):
            rows = pl.ds(24 * s, 24)
            own = self.summed[s, p, aligned(24 * core, 24, 8)]
            out[rows, aligned(384 * core + 128 * p, 128, 128)] = own
            out[rows, aligned(384 * (1 - core) + 128 * p, 128, 128)] = self.crossed[s, p]

    def drain(self, s):
        self.last(s).wait_send()
        wait_sent(self.side[s], self.side_send.at[s], self.me.sibling())
        for k in range(3):
            wait_sent(self.slots[k].at[s], self.send_sem.at[s, k], self.me.sibling())


def normal_of(x):
    center = x - jnp.mean(x, axis=-1, keepdims=True)
    rstd = lax.rsqrt(jnp.mean(center * center, axis=-1, keepdims=True) + NORM_EPS)
    return center * rstd, rstd


def norm_back(d_h, gain, xhat, rstd):
    e = d_h * gain
    inner = jnp.mean(e, axis=-1, keepdims=True) + xhat * jnp.mean(
        e * xhat, axis=-1, keepdims=True
    )
    return (e - inner) * rstd


def lanes_of(ref, *index):
    return jnp.concatenate([ref[(t,) + index] for t in range(ref.shape[0])], axis=-1)


def swapped(v):
    lane = lax.broadcasted_iota(jnp.int32, v.shape, 1)
    return jnp.where((lane & 63) < 32, pltpu.roll(v, 96, 1), pltpu.roll(v, 32, 1))


def first_head(shape):
    return lax.broadcasted_iota(jnp.int32, shape, 1) < HD


def split_heads(v):
    own, zero = first_head(v.shape), jnp.zeros_like(v)
    return jnp.concatenate([jnp.where(own, v, zero), jnp.where(own, zero, v)], axis=0)


def join_heads(v):
    half = v.shape[0] // 2
    return jnp.where(first_head((half, v.shape[1])), v[:half], v[half:])


class Layer:
    scratch = [
        VMEM((3 * D, D), bf16),
        VMEM((D, D), bf16),
        VMEM((2 * SEQ, D), bf16),
        VMEM((PAIRS, SEQ, 128), bf16),
        VMEM((2 * PAIRS, 2 * SEQ, 128), bf16),
        VMEM((PAIRS, SEQ, 128), bf16),
        VMEM((SEQ, D), f32),
        VMEM((SEQ, D), bf16),
        VMEM((SEQ, D), f32),
        VMEM((SEQ, D), f32),
        VMEM((4, TILE, 5 * TILE), bf16),
    ] + [VMEM((PAIRS, 2 * TILE, (i + 2) * TILE), bf16) for i in range(TILES)]

    def __init__(self, scratch):
        self.qkv, self.out, self.h1, self.q, self.kv, self.att, self.x2, self.h2 = scratch[:8]
        self.sum_a, self.sum_b, self.mask = scratch[8:11]
        self.probs = scratch[11:15]
        self.d_branch, self.d_att = self.h2, self.att

    def line(self, x, y):
        row = (lax.rem(x, 2) * 4 + y) * 2 + lax.div(x, 2)
        return aligned(144 * row, 144, 16), aligned(48 * row, 48, 16)

    def unpack(self, shards, perm):
        def step(x, carry):
            for y in range(4):
                tiles = [shards[t, x, y].reshape(192, 128) for t in range(6)]
                block = dot_nn(perm[...], jnp.concatenate(tiles, axis=1)).astype(bf16)
                rows_qkv, rows_out = self.line(x, y)
                self.qkv[rows_qkv] = block[:144]
                self.out[rows_out] = block[144:]
            return carry

        lax.fori_loop(0, 4, step, 0)

    def pack(self, grads, shards, perm, x):
        for y in range(4):
            rows_qkv, rows_out = self.line(x, y)
            tiles = [grads[t // 3][t % 3, rows_qkv] for t in range(6)]
            block = jnp.concatenate(tiles, axis=1)
            block = jnp.concatenate([block, self.out[rows_out]], axis=0)
            block = dot_tn(perm[...], block).astype(bf16)
            for t in range(6):
                shards[t, x, y] = block[:, 128 * t : 128 * t + 128].reshape(4, 48, 128)

    def masks(self, length, size):
        row = lax.broadcasted_iota(jnp.int32, (TILE, TILE), 0)
        col = lax.broadcasted_iota(jnp.int32, (TILE, TILE), 1)
        shift = jnp.where(size == 4, 2, jnp.where(size == 8, 3, 4))
        n_row = lax.shift_right_logical(row, jnp.full_like(row, shift))
        n_col = lax.shift_right_logical(col, jnp.full_like(col, shift))
        for i in range(TILES):
            for j in range(i + 2):
                key = min(j, i) * TILE + col
                seen = key < length
                if j == i:
                    seen = seen & (n_row > n_col)
                if j == i + 1:
                    seen = seen & (n_row == n_col)
                self.mask[i, :, j * TILE : (j + 1) * TILE] = jnp.where(seen, 0.0, MASKED).astype(bf16)

    def norm_one(self, x, gains, first_row):
        gain = gains[0:1, :]

        def step(i, carry):
            rows = aligned(i * TILE, TILE, TILE)
            xhat, _ = normal_of(x[rows].astype(f32))
            self.h1[aligned(first_row + i * TILE, TILE, TILE)] = (xhat * gain).astype(bf16)
            return carry

        lax.fori_loop(0, TILES, step, 0)

    def project(self, cos, sin, clean):
        def turned(v, scale):
            return (v * (cos[...] * scale) + swapped(v) * (sin[...] * scale)).astype(bf16)

        rows = slice(SEQ, 2 * SEQ) if clean else slice(0, SEQ)
        for j in range(3 if clean else 0, 9):
            v = dot_nt(self.h1[rows], self.qkv[256 * j : 256 * j + 256])
            for n in range(2):
                part = v[:, 128 * n : 128 * n + 128]
                if j < 3:
                    self.q[2 * j + n] = turned(part, HD ** (-0.5))
                elif j < 6:
                    self.kv[2 * j - 6 + n, rows] = turned(part, 1.0)
                else:
                    self.kv[2 * j - 6 + n, rows] = part.astype(bf16)

    def keys(self, t, i):
        clean = self.kv[t, SEQ : SEQ + (i + 1) * TILE]
        return jnp.concatenate([clean, self.kv[t, i * TILE : (i + 1) * TILE]], axis=0)

    def scores(self, pair, i):
        width = (i + 2) * TILE
        queries = split_heads(self.q[pair, pl.ds(i * TILE, TILE)])
        scores = dot_nt(queries, self.keys(pair, i)).reshape(2, TILE, width)
        return (scores + self.mask[i, :, :width].astype(f32)[None]).reshape(2 * TILE, width)

    def attend(self, pairs):
        places = [(pair, i) for pair in pairs for i in range(TILES)]
        scores = [self.scores(pair, i) for pair, i in places]
        raised = [jnp.exp(s - jnp.max(s, axis=-1, keepdims=True)) for s in scores]
        mixed = [
            dot_nn(e.astype(bf16), self.keys(PAIRS + pair, i))
            for e, (pair, i) in zip(raised, places)
        ]
        for e, o, (pair, i) in zip(raised, mixed, places):
            share = 1.0 / jnp.sum(e, axis=-1, keepdims=True)
            self.probs[i][pair] = (e * share).astype(bf16)
            self.att[pair, pl.ds(i * TILE, TILE)] = join_heads(o * share).astype(bf16)

    def mix(self, x, gains):
        for j in range(3):
            cols = slice(256 * j, 256 * j + 256)
            branch = dot_nn(lanes_of(self.att), self.out[:, cols])
            self.x2[:, cols] = x[:, cols].astype(f32) + branch
        gain = gains[1:2, :]

        def step(i, carry):
            rows = aligned(i * TILE, TILE, TILE)
            xhat, _ = normal_of(self.x2[rows])
            self.h2[rows] = (xhat * gain).astype(bf16)
            self.sum_a[rows] = jnp.zeros((TILE, D), f32)
            self.sum_b[rows] = jnp.zeros((TILE, D), f32)
            return carry

        lax.fori_loop(0, TILES, step, 0)

    def feed(self, up, down, dy, x, act_ref, d_up_ref):
        c = (2.0 / np.pi) ** 0.5
        rows = [aligned(768 * x + 256 * j, 256, 256) for j in range(3)]
        cols = [slice(256 * j, 256 * j + 256) for j in range(3)]
        ups = [dot_nt(self.h2[...], lanes_of(up, r)) for r in rows]
        d_acts = [dot_nt(dy[...], lanes_of(down, r)) for r in rows]
        for u, d_act, part in zip(ups, d_acts, cols):
            squared = u * u
            t = jnp.tanh(u * (c + (0.044715 * c) * squared))
            half = 0.5 + 0.5 * t
            act_ref[:, part] = (u * half).astype(bf16)
            slope = half + (0.5 * u) * (1.0 - t * t) * (c + (3 * 0.044715 * c) * squared)
            d_up_ref[:, part] = (slope * d_act).astype(bf16)
        slab = aligned(768 * x, 768, 256)
        for n, part in enumerate(cols):
            tiles = (2 * n, 2 * n + 1)
            w_up = jnp.concatenate([up[t, slab] for t in tiles], axis=1)
            w_down = jnp.concatenate([down[t, slab] for t in tiles], axis=1)
            self.sum_a[:, part] += dot_nn(act_ref[...], w_down)
            self.sum_b[:, part] += dot_nn(d_up_ref[...], w_up)
        g_up = [dot_tn(d_up_ref[:, part], self.h2[...]).astype(bf16) for part in cols]
        g_down = [dot_tn(act_ref[:, part], dy[...]).astype(bf16) for part in cols]
        for j in range(3):
            for t in range(LANES):
                up[t, rows[j]] = g_up[j][:, 128 * t : 128 * t + 128]
                down[t, rows[j]] = g_down[j][:, 128 * t : 128 * t + 128]

    def back_two(self, dy, gains, outputs, d_gains):
        gain = gains[1:2, :]

        def step(i, carry):
            rows = aligned(i * TILE, TILE, TILE)
            x2 = self.x2[rows]
            outputs[rows] = (x2 + self.sum_a[rows]).astype(bf16)
            xhat, rstd = normal_of(x2)
            d_h = self.sum_b[rows]
            d_x2 = dy[rows].astype(f32) + norm_back(d_h, gain, xhat, rstd)
            self.sum_b[rows] = d_x2
            self.d_branch[rows] = d_x2.astype(bf16)
            return carry + jnp.sum(d_h * xhat, axis=0, keepdims=True)

        d_gains[1:2, :] = lax.fori_loop(0, TILES, step, jnp.zeros((1, D), f32))

    def back_mix(self):
        for j in range(3):
            rows = slice(256 * j, 256 * j + 256)
            att = jnp.concatenate([self.att[2 * j], self.att[2 * j + 1]], axis=1)
            d_att = dot_nt(self.d_branch[...], self.out[rows]).astype(bf16)
            self.out[rows] = dot_tn(att, self.d_branch[...]).astype(bf16)
            self.d_att[2 * j] = d_att[:, :128]
            self.d_att[2 * j + 1] = d_att[:, 128:]

    def back_values(self, pair, d_values):
        parts = []
        for i in range(TILES):
            d_att = split_heads(self.d_att[pair, pl.ds(i * TILE, TILE)])
            parts.append(dot_tn(self.probs[i][pair], d_att))
        for i in range(TILES):
            rows = slice(i * TILE, (i + 1) * TILE)
            own = slice(VALUES_OWN + i * TILE, VALUES_OWN + (i + 1) * TILE)
            clean = slice(VALUES_CLEAN + i * TILE, VALUES_CLEAN + (i + 1) * TILE)
            d_values[pair, own] = parts[i][(i + 1) * TILE :].astype(bf16)
            d_values[pair, clean] = sum(part[rows] for part in parts[i:]).astype(bf16)

    def back_attend(self, pair, cos, sin, d_values):
        tiles = [pl.ds(i * TILE, TILE) for i in range(TILES)]
        queries = [split_heads(self.q[pair, rows]) for rows in tiles]
        d_atts = [split_heads(self.d_att[pair, rows]) for rows in tiles]
        d_probs = [dot_nt(d_atts[i], self.keys(PAIRS + pair, i)) for i in range(TILES)]
        d_scores = []
        for i in range(TILES):
            probs = self.probs[i][pair].astype(f32)
            delta = jnp.sum(probs * d_probs[i], axis=-1, keepdims=True)
            d_scores.append((probs * (d_probs[i] - delta)).astype(bf16))
        d_query = [join_heads(dot_nn(d_scores[i], self.keys(pair, i))) for i in range(TILES)]
        parts = [dot_tn(d_scores[i], queries[i]) for i in range(TILES)]

        def back(v, rows):
            return (v * cos[rows] - swapped(v) * sin[rows]).astype(bf16)

        for i, rows in enumerate(tiles):
            clean, part = pl.ds(SEQ + i * TILE, TILE), slice(i * TILE, (i + 1) * TILE)
            self.q[pair, rows] = back(d_query[i] * HD ** (-0.5), rows)
            self.kv[pair, clean] = back(sum(d_k[part] for d_k in parts[i:]), rows)
            self.kv[pair, rows] = back(parts[i][(i + 1) * TILE :], rows)
        self.kv[PAIRS + pair, :SEQ] = d_values[pair, VALUES_OWN : VALUES_OWN + SEQ]
        self.kv[PAIRS + pair, SEQ:] = d_values[pair, VALUES_CLEAN : VALUES_CLEAN + SEQ]

    def back_clean(self, gains, x_clean, grads_clean, d_gains):
        for i in range(TILES):
            clean, own = pl.ds(SEQ + i * TILE, TILE), pl.ds(i * TILE, TILE)
            d_h = dot_nn(lanes_of(self.kv, clean), self.qkv[D:])
            xhat, rstd = normal_of(x_clean[own].astype(f32))
            grads_clean[own] = norm_back(d_h, gains[0:1, :], xhat, rstd).astype(bf16)
            d_gains[0:1, :] += jnp.sum(d_h * xhat, axis=0, keepdims=True)

    def back_own(self, gains, x, grads, d_gains):
        for i in range(2):
            own = pl.ds(2 * TILE * i, 2 * TILE)
            d_proj = jnp.concatenate([lanes_of(self.q, own), lanes_of(self.kv, own)], axis=1)
            d_h = dot_nn(d_proj, self.qkv[...])
            xhat, rstd = normal_of(x[own].astype(f32))
            grads[own] = self.sum_b[own] + norm_back(d_h, gains[0:1, :], xhat, rstd)
            d_gains[0:1, :] += jnp.sum(d_h * xhat, axis=0, keepdims=True)

    def grad_project(self, grads, d_values, second):
        def put(row, tiles, tokens):
            value = dot_tn(jnp.concatenate(tiles, axis=1), self.h1[:tokens]).astype(bf16)
            for t in range(6):
                grads[t // 3][t % 3, row : row + 384] = value[:, 128 * t : 128 * t + 128]

        def values_of(pair):
            own = d_values[pair, VALUES_OWN : VALUES_OWN + SEQ]
            return jnp.concatenate([own, d_values[pair, VALUES_CLEAN : VALUES_CLEAN + SEQ]], axis=0)

        if second:
            put(1152, [self.kv[t] for t in (3, 4, 5)], 2 * SEQ)
            put(1536, [values_of(t) for t in (0, 1, 2)], 2 * SEQ)
            put(1920, [values_of(t) for t in (3, 4, 5)], 2 * SEQ)
        else:
            put(0, [self.q[t] for t in (0, 1, 2)], SEQ)
            put(384, [self.q[t] for t in (3, 4, 5)], SEQ)
            put(768, [self.kv[t] for t in (0, 1, 2)], 2 * SEQ)


class Rest:
    scratch = [
        VMEM(SHARDS, bf16),
        VMEM(SHARDS, bf16),
        VMEM(SHARDS, bf16),
        VMEM((SEQ, D), bf16),
        VMEM((SEQ, D), bf16),
        VMEM((8, D), f32),
        DMA((2,)),
        DMA((2,)),
    ]


def split(refs, *groups):
    out, at = [], 0
    for group in groups:
        out.append(refs[at : at + len(group.scratch)])
        at += len(group.scratch)
    return out


CLEAN = ((0, 128), (128, 128), (256, 256))
NOISY = ((0, 128), (128, 128), (256, 128), (384, 128))


def pieces(src, dst, sems, device, cuts):
    out = []
    for n, (row, count) in enumerate(cuts):
        rows = pl.ds(row, count)
        out.append(remote(src.at[rows], dst.at[rows], sems.at[0], sems.at[1], device))
    return out


def step_kernel(
    lengths, sizes, w_qkv, w_out, w_up, w_down, gains_own, x, dy, perm, cos, sin,
    outputs, grads_in, grads, d_gains_all, *scratch
):
    gather_refs, total_refs, layer_refs, reduce_refs, back_refs, rest = split(
        scratch, Gather, Total, Layer, Reduce, Total, Rest
    )
    shards = rest[:3]
    x_clean, back, d_gains, clean_sem, back_sem = rest[3:]
    me = Place()
    gather = Gather(me, shards, gather_refs)
    total = Total(me, total_refs)
    total_back = Total(me, back_refs)
    layer = Layer(layer_refs)
    reduce = Reduce(me, shards, reduce_refs)
    gains, given = total.held.at[4], layer.h2
    to_clean = pieces(x, x_clean, clean_sem, me.partner(), CLEAN)
    from_noisy = pieces(given, back, back_sem, me.partner(), NOISY)

    def clean_sends(n):
        @pl.when(me.stream == 0)
        def _():
            to_clean[n].start()

    def noisy_sends(n):
        @pl.when(me.stream == 1)
        def _():
            from_noisy[n].start()

    packed = gather.packed
    packed[0:18] = w_qkv[...]
    packed[18:24] = w_out[...]
    packed[24:48] = w_up[...]
    packed[48:72] = w_down[...]
    total.held[0] = jnp.zeros((8, D), f32)
    total.held[0, 0:2, 0:6] = gains_own[...].astype(bf16).astype(f32)
    total.held[0] = pltpu.roll(total.held[0], 6 * lax.axis_index(AXES), 1)
    me.greet()
    gather.swap().start()
    total.send(0)
    layer.masks(lengths[0], sizes[0])

    @pl.when(me.stream == 0)
    def _():
        x_clean[...] = x[...]

    gather.swap().wait()
    gather.assemble()
    gather.start(0)
    gather.start(1)
    gather.start(2)
    clean_sends(0)
    total.add(0)
    total.send(1)
    gather.advance(0, 0)
    clean_sends(1)
    total.add(1)
    total.send(2)
    gather.advance(1, 0)
    gather.advance(2, 0)
    gather.advance(0, 1)
    clean_sends(2)
    total.add(2)
    total.send(3)
    total.add(3)
    layer.norm_one(x, gains, 0)
    gather.advance(1, 1)
    gather.advance(2, 1)
    gather.hand_over()
    gather.finish(0)
    layer.unpack(shards[0], perm)
    layer.project(cos, sin, False)
    gather.relay(1)

    @pl.when(me.stream == 1)
    def _():
        wait_came(x_clean, clean_sem.at[1], me.partner())

    layer.norm_one(x_clean, gains, SEQ)
    layer.project(cos, sin, True)
    gather.relay(2)

    def forward(n, carry):
        layer.attend((2 * n, 2 * n + 1))
        for at, s in ((0, 1), (1, 2)):

            @pl.when(n == at)
            def _():
                gather.close(s)

        return carry

    lax.fori_loop(0, PAIRS // 2, forward, 0)
    layer.mix(x, gains)
    for s in range(3):
        if s > 0:
            gather.finish(s)
        gather.drain(s)
    total.drain()
    up, down = shards[1].reshape(6, FF, 128), shards[2].reshape(6, FF, 128)

    def feed(turn, carry):
        layer.feed(up, down, dy, reduce.slab(turn), outputs, grads_in)
        reduce.begin(1, turn)
        reduce.begin(2, turn)

        @pl.when(turn > 0)
        def _():
            reduce.enter(1, turn - 1)
            reduce.enter(2, turn - 1)

        return carry

    lax.fori_loop(0, 4, feed, 0)
    d_gains[...] = jnp.zeros((8, D), f32)
    layer.back_two(dy, gains, outputs, d_gains)
    reduce.enter(1, 3)
    reduce.enter(2, 3)
    layer.back_mix()

    d_values = shards[0].reshape(6, FF, 128)
    grads_qkv = [side.reshape(3, FF, 128) for side in reduce.side[1:]]

    def values(pair, carry):
        layer.back_values(pair, d_values)
        return carry

    lax.fori_loop(0, PAIRS, values, 0)
    odd = lax.rem(me.chip[0], 2)

    def half(second):
        layer.grad_project(grads_qkv, d_values, second)
        for n in (0, 2):
            turn = (odd if second else 1 - odd) + n
            layer.pack(grads_qkv, shards[0], perm, reduce.slab(turn))
            reduce.begin(0, turn)

    def enter(second):
        for n in (0, 2):
            reduce.enter(0, (odd if second else 1 - odd) + n)

    def backward(n, carry):
        layer.back_attend(lax.rem(n + 3, PAIRS), cos, sin, d_values)

        @pl.when(n == 1)
        def _():
            reduce.advance(1, 0)

        @pl.when(n == 2)
        def _():
            reduce.advance(2, 0)
            half(True)

        @pl.when(n == 3)
        def _():
            enter(True)
            reduce.advance(1, 1)

        @pl.when(n == 4)
        def _():
            reduce.advance(2, 1)

        return carry

    lax.fori_loop(0, PAIRS, backward, 0)
    layer.back_clean(gains, x_clean, given, d_gains)
    noisy_sends(0)
    half(False)
    enter(False)
    noisy_sends(1)
    reduce.advance(1, 2)
    layer.back_own(gains, x, layer.x2, d_gains)
    total_back.held[0] = d_gains[...]
    total_back.send(0)
    reduce.advance(0, 0)
    reduce.advance(2, 2)
    reduce.finish(1, grads)
    noisy_sends(2)
    total_back.add(0)
    total_back.send(1)
    reduce.advance(0, 1)
    reduce.finish(2, grads)
    noisy_sends(3)
    total_back.add(1)
    total_back.send(2)
    reduce.advance(0, 2)
    total_back.add(2)
    total_back.send(3)

    @pl.when(me.stream == 0)
    def _():
        wait_came(back, back_sem.at[1], me.partner())
        both = given[...].astype(f32) + back[...].astype(f32)
        grads_in[...] = (layer.x2[...] + both).astype(bf16)

    @pl.when(me.stream == 1)
    def _():
        grads_in[...] = layer.x2[...].astype(bf16)

    reduce.finish(0, grads)
    total_back.add(3)
    d_gains_all[...] = total_back.held[4]

    @pl.when(me.stream == 0)
    def _():
        wait_sent(x_clean, clean_sem.at[0], me.partner())

    @pl.when(me.stream == 1)
    def _():
        wait_sent(back, back_sem.at[0], me.partner())

    total_back.drain()
    for s in range(3):
        reduce.drain(s)


def adam(weight, grad, first, second, rate):
    first_new = BETA_ONE * first + (1.0 - BETA_ONE) * grad
    second_new = BETA_TWO * second + (1.0 - BETA_TWO) * grad * grad
    fix_one = 1.0 - BETA_ONE**STEP
    fix_two = 1.0 - BETA_TWO**STEP
    update = first_new / fix_one / (jnp.sqrt(second_new / fix_two) + ADAM_EPS)
    return (weight - rate * (update + WEIGHT_DECAY * weight), first_new, second_new)


ROWS = ((0, 18), (18, 24), (24, 48), (48, 72))


def adam_kernel(grads, d_gains, outputs, grads_in, *refs):
    weights, firsts, seconds, outs = refs[:5], refs[5:10], refs[10:15], refs[15:]
    outs[19][...] = outputs[...]
    outs[20][...] = grads_in[...]
    turn = lax.rem(D - 6 * lax.axis_index(AXES), D)
    d_gains_own = pltpu.roll(d_gains[...], turn, 1)[0:2, 0:6]
    for n in range(5):
        grad = d_gains_own if n == 4 else grads[ROWS[n][0] : ROWS[n][1]]
        new = adam(weights[n][...], grad, firsts[n][...], seconds[n][...], RATES[n])
        for part in range(3):
            outs[5 * part + n][...] = new[part]
        if n < 4:
            outs[15 + n][...] = new[0].astype(bf16)


def call(kernel, out_shape, operands, scratch=(), collective=None, smem=0):
    spec, place = pl.BlockSpec(memory_space=VMEM), pl.BlockSpec(memory_space=pltpu.SMEM)
    return pl.pallas_call(
        kernel,
        out_shape=out_shape,
        in_specs=[place] * smem + [spec] * (len(operands) - smem),
        out_specs=[spec] * len(out_shape),
        scratch_shapes=list(scratch),
        compiler_params=pltpu.CompilerParams(
            collective_id=collective,
            has_side_effects=collective is not None,
            vmem_limit_bytes=63 << 20,
        ),
    )(*operands)


def permutation():
    perm = np.zeros((192, 192), np.float32)
    for row in range(192):
        if row < 144:
            perm[row, 24 * (row // 18) + row % 18] = 1
        else:
            perm[row, 24 * ((row - 144) // 6) + 18 + (row - 144) % 6] = 1
    return perm


def rotary_tables():
    frequency = 10000.0 ** (-2.0 * np.arange(HD // 2) / HD)
    angles = (np.arange(SEQ)[:, None] * frequency[None, :]).astype(np.float32)
    cos, sin = np.cos(angles), np.sin(angles)
    return np.tile(cos, (1, 4)), np.concatenate([-sin, sin, -sin, sin], axis=1)


def local(
    inputs, cotangent, lengths, block_sizes, w_qkv, w_out, w_up, w_down, gains,
    first_qkv, first_out, first_up, first_down, first_gains,
    second_qkv, second_out, second_up, second_down, second_gains,
):
    shape = jax.ShapeDtypeStruct
    masters = (w_qkv.T, w_out, w_up.T, w_down, gains)
    firsts = (first_qkv.T, first_out, first_up.T, first_down, first_gains)
    seconds = (second_qkv.T, second_out, second_up.T, second_down, second_gains)
    x, dy = inputs[0, 0], cotangent[0, 0]
    rows16, small = shape((SEQ, D), bf16), shape((8, D), f32)
    cos, sin = rotary_tables()
    groups = (Gather, Total, Layer, Reduce, Total, Rest)
    outputs, input_grads, grads, d_gains = call(
        step_kernel,
        [rows16, rows16, shape((72, D), f32), small],
        (lengths, block_sizes, *masters, x, dy, jnp.asarray(permutation(), bf16),
         jnp.asarray(cos, f32), jnp.asarray(sin, f32)),
        [item for group in groups for item in group.scratch],
        collective=0,
        smem=2,
    )
    like = [shape(w.shape, f32) for w in masters]
    *new, outputs, input_grads = call(
        adam_kernel,
        like * 3 + [shape(w.shape, bf16) for w in masters[:4]] + [rows16] * 2,
        (grads, d_gains, outputs, input_grads, *masters, *firsts, *seconds),
    )
    turned = [v.T if n % 5 in (0, 2) else v for n, v in enumerate(new)]
    return (outputs[None, None], input_grads[None, None], *turned)


def solution(mesh):
    mesh = Mesh(mesh.devices.reshape(2, 4, 2, 4, 2), AXES)
    data, one = P("xl", AXES[1:], None, None), P(AXES[1:])
    cols, rows = P(None, AXES), P(AXES, None)
    state = (cols, rows, cols, rows, cols)
    return jax.shard_map(
        local,
        mesh=mesh,
        in_specs=(data, data, one, one) + state * 3,
        out_specs=(data, data) + state * 3 + state[:4],
        check_vma=False,
    )
```
